256 devices in a mesh: row: 16 (over z, core), col: 16 (over y, x).
Axes of the slice: x: 4, y: 4, z: 8, core: 2. Of those that a mesh axis runs over, the one named last changes fastest.
Arguments:
- density: float32 [4096, 4096], P('row', 'col'), as said below
- pattern: int32 [32, 32], P('row', 'col'), may hold values from 0 to 1, as said below
Outputs:
- purified: float32 [4096, 4096], P('row', 'col')
The draws below stay inside these ranges and needn't reach their ends.
Inputs may be any that keep to these rules, and one draw needn't show every extreme that they name: pattern is symmetric, with ones on the block diagonal. density is exactly symmetric and zero in every block where pattern is 0.
All inputs are finite; a program needn't handle non-finite values.
Results may differ from the reference program's by a relative error of at most 0.00016.
Values sent between devices are 32-bit elements; how exact they have to be, the bound alone decides.
A program may use at most 64 MiB of HBM per device.

```python
import jax
import jax.numpy as jnp
from jax import lax

BLOCK = 128
STEPS = 2
BLOCKS = 32


def shared_pattern(key):
    rates = jax.random.randint(jax.random.fold_in(key, 11), (BLOCKS,), 1, 7)
    scores = jax.random.randint(jax.random.fold_in(key, 12), (BLOCKS, BLOCKS), 0, 24)
    linked = (scores < rates[:, None] + rates[None, :]).astype(jnp.int32)
    upper = jnp.triu(linked, 1)
    return upper + upper.T + jnp.eye(BLOCKS, dtype=jnp.int32)


def draw_pattern(key, part):
    result = shared_pattern(key)
    return result


def draw_density(key, part):
    blocks_kept = shared_pattern(key)
    key = jax.random.fold_in(key, 3)
    basis = BLOCKS * BLOCK
    reach = 0.3 * BLOCKS * BLOCK
    scale_entry = 0.21 / jnp.sqrt(jnp.float32(reach))
    noise = jax.random.normal(jax.random.fold_in(key, 1), (basis, basis), jnp.float32)
    half = noise * scale_entry
    symmetric = half + half.T
    occupation = jax.random.uniform(jax.random.fold_in(key, 4), (basis,), jnp.float32, 0.05, 0.95)
    widened = jnp.repeat(jnp.repeat(blocks_kept.astype(jnp.float32), BLOCK, axis=0), BLOCK, axis=1)
    return widened * (symmetric + jnp.diag(occupation))


def setup_inputs(seed: int = 0) -> dict:
    key_list = jax.random.split(jax.random.key(seed), 3)
    density = draw_density(jax.random.fold_in(key_list[2], 71), 0)
    pattern = draw_pattern(jax.random.fold_in(key_list[2], 71), 0)
    return {"density": density, "pattern": pattern}


def expand(pattern):
    widened = jnp.repeat(pattern.astype(jnp.float32), BLOCK, axis=0)
    return jnp.repeat(widened, BLOCK, axis=1)


def reference(density, pattern):
    mask = expand(pattern)
    current = density
    for step in range(STEPS):
        square = mask * jnp.dot(current, current, precision=lax.Precision.HIGHEST, preferred_element_type=jnp.float32)
        cubed = mask * jnp.dot(square, current, precision=lax.Precision.HIGHEST, preferred_element_type=jnp.float32)
        current = 3.0 * square - 2.0 * cubed
    return current
```

```python
import heapq

import jax
import jax.numpy as jnp
from jax import lax
from jax.experimental import pallas as pl
from jax.experimental.pallas import tpu as pltpu
from jax.sharding import PartitionSpec as P

BLOCK = 128
STEPS = 2
NX, NY, NZ = 4, 4, 8
MESH = pl.DeviceIdType.MESH
f32, bf16 = jnp.float32, jnp.bfloat16
OFFSETS = [(dx, dy) for dx in (0, 1, -1, 2) for dy in (0, 1, -1, 2)]
RING = (0, 1, -1, 2, -2, 3, -3, 4)

ROWS64, HOP, PRODUCT, SMALL = 1.4, 1.0, 0.15, 0.05


def row_tile(p, h, plan, a, b):
    if (a, b) == (0, 0):
        return []
    parts = ("q0", "q1") if b == 2 or (b == 0 and a == 2) else ("h",)
    return [("row", p, h, plan, a, b, part) for part in parts]


def col_tile(s, h, dz, other):
    if other:
        return [("col", s, h, dz, "s")]
    if dz == 0:
        return []
    return [("col", s, h, dz, part) for part in (("q0", "q1") if dz == 4 else ("h",))]


def make_jobs():
    jobs = {}

    def link(plan, axis, sign):
        return ("x" if (axis == 0) == (plan == 0) else "y", sign)

    def own_row(p, h):
        pushes = []
        for axis in (0, 1):
            for plan in (0, 1):
                for sign in (1, -1):
                    a, b = (sign, 0) if axis == 0 else (0, sign)
                    pushes.append((link(plan, axis, sign), 1.0, ("row", p, h, plan, a, b, "h")))
        return pushes

    def own_col(s, h):
        return [(("z", sign), 2.0, ("col", s, h, sign, "h")) for sign in (1, -1)] + [
            (("core", 0), 0.3, ("col", s, h, 0, "s"))]

    def start(p, h):
        return ("start",) if p == 0 else ("final", p - 1, h)

    jobs[("start",)] = (0, SMALL, [], own_row(0, 0) + own_col(0, 0) + own_col(0, 1) + own_row(0, 1))
    for p in range(2 * STEPS):
        s = p // 2
        for h in (0, 1):
            for plan in (0, 1):
                for sign in (1, -1):
                    part = "q0" if sign == 1 else "q1"
                    for a in (0, 1, -1, 2):
                        pushes = [(link(plan, 1, sign), 0.5, ("row", p, h, plan, a, 2, part))]
                        jobs[("pass", p, h, plan, a, sign)] = (0, SMALL, row_tile(p, h, plan, a, sign), pushes)
                    pushes = [(link(plan, 0, sign), 0.5, ("row", p, h, plan, 2, 0, part))]
                    pushes += [(link(plan, 1, turn), 1.0, ("row", p, h, plan, sign, turn, "h")) for turn in (1, -1)]
                    jobs[("turn", p, h, plan, sign)] = (0, 3 * SMALL, row_tile(p, h, plan, sign, 0), pushes)
                pushes = [(link(plan, 1, turn), 1.0, ("row", p, h, plan, 2, turn, "h")) for turn in (1, -1)]
                jobs[("turn", p, h, plan, 2)] = (0, 2 * SMALL, row_tile(p, h, plan, 2, 0), pushes)
            if p % 2 == 0:
                for dz in RING:
                    pushes = []
                    if dz:
                        sign = 1 if dz > 0 else -1
                        if abs(dz) < 3:
                            pushes.append((("z", sign), 2.0, ("col", s, h, dz + sign, "h")))
                        elif dz != 4:
                            pushes.append((("z", sign), 1.0, ("col", s, h, 4, "q0" if sign == 1 else "q1")))
                        pushes.append((("core", 0), 0.3, ("col", s, h, dz, "s")))
                        jobs[("ring", s, h, dz)] = (0, 2 * SMALL, col_tile(s, h, dz, False), pushes)
                    before = [("ring", s, h, dz)] if dz else [start(p, h)]
                    jobs[("split", s, h, dz, False)] = (2, SMALL, before, [])
                    jobs[("split", s, h, dz, True)] = (2, SMALL, col_tile(s, h, dz, True), [])
            by_col = p == 0 and h == 0
            pieces = {o: row_tile(p, h, 0, *o) + row_tile(p, h, 1, *o[::-1]) for o in OFFSETS}
            if by_col:
                need = [piece for o in OFFSETS for piece in pieces[o]]
                keys = [(dz, other) for dz in RING for other in (False, True)]
                for key in keys:
                    jobs[("mac", p, h) + key] = (
                        4, PRODUCT, need + [("split", s, half, *key) for half in (0, 1)], [])
            else:
                keys = OFFSETS
                need = [("split", s, half, dz, other) for half in (0, 1) for dz in RING for other in (False, True)]
                for key in keys:
                    needs = pieces[key] + [start(p, h)] + (need if p % 2 == 0 else [])
                    jobs[("mac", p, h) + key] = (4 + p, PRODUCT, needs, [])
            pushes = []
            if p < 2 * STEPS - 1:
                pushes = own_row(p + 1, h) + (own_col(s + 1, h) if p % 2 else [])
            jobs[("final", p, h)] = (1, 2 * SMALL, [("mac", p, h) + key for key in keys], pushes)
    return jobs


def make_order(jobs):
    ready_at, missing, users = {}, {}, {}
    for name, (_, _, needs, _) in jobs.items():
        missing[name] = len(set(needs))
        ready_at[name] = 0.0
        for need in set(needs):
            users.setdefault(need, []).append(name)
    waiting, ready, free = [], [], {}
    rank = {name: n for n, name in enumerate(jobs)}

    def done(thing, when):
        for user in users.get(thing, ()):
            missing[user] -= 1
            ready_at[user] = max(ready_at[user], when)
            if missing[user] == 0:
                heapq.heappush(waiting, (ready_at[user], rank[user], user))

    for name in jobs:
        if missing[name] == 0:
            heapq.heappush(waiting, (0.0, rank[name], name))
    now, order = 0.0, []
    while waiting or ready:
        if not ready and waiting[0][0] > now:
            now = waiting[0][0]
        while waiting and waiting[0][0] <= now:
            when, number, name = heapq.heappop(waiting)
            heapq.heappush(ready, (jobs[name][0], when, number, name))
        name = heapq.heappop(ready)[-1]
        _, cost, _, pushes = jobs[name]
        now += cost
        order.append(name)
        for where, amount, piece in pushes:
            rate = 1.0 if where[0] == "core" else ROWS64
            free[where] = max(free.get(where, 0.0), now) + amount * rate
            done(piece, free[where] + HOP)
        done(name, now)
    return order, now


JOBS = make_jobs()
ORDER, MODEL_TIME = make_order(JOBS)
PIECES = [piece for name in JOBS for _, _, piece in JOBS[name][3]]
ROW = {name: n for n, name in enumerate(piece for piece in PIECES if piece[0] == "row")}
COL = {name: n for n, name in enumerate(piece for piece in PIECES if piece[0] == "col")}


def split(value):
    high = value.astype(bf16)
    return high, (value - high.astype(f32)).astype(bf16)


def kernel(pattern_in, density, out, rows, cols, col_hi, col_lo, acc, pattern,
           row_send, row_recv, col_send, col_recv, local_sem):
    size = density.shape[0]
    half, quarter, eighth = size // 2, size // 4, size // 8
    r, c = lax.axis_index("row"), lax.axis_index("col")
    z, core = r // 2, r % 2
    y, x = c // NX, c % NX

    def device(dx=0, dy=0, dz=0):
        return (((z + dz + NZ) % NZ) * 2 + core, ((y + dy + NY) % NY) * NX + (x + dx + NX) % NX)

    sibling = (z * 2 + 1 - core, c)

    def k_row(dx, dy):
        return ((y - dy + NY) % NY) * NX + (x - dx + NX) % NX

    def k_col(dz, other):
        return ((z - dz + NZ) % NZ) * 2 + (1 - core if other else core)

    fetch = [
        pltpu.make_async_copy(density, rows.at[0, c], local_sem.at[0]),
        pltpu.make_async_copy(density, cols.at[0, r], local_sem.at[1]),
        pltpu.make_async_copy(pattern_in, pattern, local_sem.at[2]),
    ]
    for copy in fetch:
        copy.start()

    peers = [device(dx=1), device(dx=-1), device(dy=1), device(dy=-1), device(dz=1), device(dz=-1), sibling]
    barrier = pltpu.get_barrier_semaphore()
    for peer in peers:
        pl.semaphore_signal(barrier, inc=1, device_id=peer, device_id_type=MESH)
    pl.semaphore_wait(barrier, len(peers))
    for copy in fetch:
        copy.wait()

    mask = [[pattern[a, b].astype(f32) for b in range(2)] for a in range(2)]

    def masked(value, h):
        return jnp.concatenate([value[:, :BLOCK] * mask[h][0], value[:, BLOCK:] * mask[h][1]], axis=1)

    def copy_of(piece, target):
        if piece[0] == "row":
            _, p, h, plan, a, b, part = piece
            dx, dy = (a, b) if plan == 0 else (b, a)
            low = h * half + plan * quarter + (eighth if part == "q1" else 0)
            return rows, p, low, quarter if part == "h" else eighth, row_send.at[p], row_recv.at[ROW[piece]], (dx, dy)
        _, s, h, dz, part = piece
        low = h * half + (quarter if part == "q1" else 0)
        return (cols, s, low, quarter if part in ("q0", "q1") else half, col_send.at[s], col_recv.at[COL[piece]], dz)

    def push(where, piece):
        buffer, index, low, count, send, recv, offset = copy_of(piece, None)
        axis, sign = where
        if piece[0] == "row":
            dx, dy = offset
            held = k_row(dx - sign, dy) if axis == "x" else k_row(dx, dy - sign)
        else:
            held = k_col(offset if axis == "core" else offset - sign, False)
        target = sibling if axis == "core" else device(**{"d" + axis: sign})
        part = buffer.at[index, held, pl.ds(low, count)]
        pltpu.make_async_remote_copy(
            src_ref=part, dst_ref=part, send_sem=send, recv_sem=recv,
            device_id=target, device_id_type=MESH).start()

    def wait(piece):
        buffer, index, low, count, send, recv, offset = copy_of(piece, None)
        if piece[0] == "row":
            held = k_row(*offset)
        else:
            held = k_col(offset, piece[-1] == "s")
        part = buffer.at[index, held, pl.ds(low, count)]
        pltpu.make_async_remote_copy(
            src_ref=part, dst_ref=part, send_sem=send, recv_sem=recv,
            device_id=sibling, device_id_type=MESH).wait_recv()

    waited, begun = set(), set()

    def run(name):
        _, _, needs, pushes = JOBS[name]
        for need in needs:
            if need[0] in ("row", "col") and need not in waited:
                waited.add(need)
                wait(need)
        kind = name[0]
        if kind == "split":
            _, s, h, dz, other = name
            k = k_col(dz, other)
            high, low = split(cols[s, k, pl.ds(h * half, half), :])
            col_hi[s, k, pl.ds(h * half, half), :] = high
            col_lo[s, k, pl.ds(h * half, half), :] = low
        elif kind == "mac":
            _, p, h = name[:3]
            by_col = isinstance(name[4], bool)
            k = k_col(*name[3:]) if by_col else k_row(*name[3:])
            high_a, low_a = split(rows[p, k, pl.ds(h * half, half), :])
            high_b, low_b = col_hi[p // 2, k], col_lo[p // 2, k]
            term = (jnp.dot(high_a, high_b, preferred_element_type=f32)
                    + jnp.dot(high_a, low_b, preferred_element_type=f32)
                    + jnp.dot(low_a, high_b, preferred_element_type=f32))
            if (p, h) in begun:
                acc[p, pl.ds(h * half, half), :] += term
            else:
                begun.add((p, h))
                acc[p, pl.ds(h * half, half), :] = term
        elif kind == "final":
            _, p, h = name
            here = pl.ds(h * half, half)
            value = masked(acc[p, here, :], h)
            if p % 2:
                value = 3.0 * rows[p, c, here, :] - 2.0 * value
            if p == 2 * STEPS - 1:
                out[here, :] = value
            else:
                rows[p + 1, c, here, :] = value
                if p % 2:
                    cols[p // 2 + 1, r, here, :] = value
        for where, _, piece in pushes:
            push(where, piece)

    for name in ORDER:
        run(name)

    for p in range(2 * STEPS):
        whole = rows.at[p, pl.ds(0, 15)]
        pltpu.make_async_copy(whole, whole, row_send.at[p]).wait()
    for s in range(STEPS):
        whole = cols.at[s, pl.ds(0, 15)]
        pltpu.make_async_copy(whole, whole, col_send.at[s]).wait()


def local(density, pattern):
    size = density.shape[0]
    tiles = NX * NY
    return pl.pallas_call(
        kernel,
        out_shape=jax.ShapeDtypeStruct(density.shape, f32),
        in_specs=[pl.BlockSpec(memory_space=pl.ANY), pl.BlockSpec(memory_space=pl.ANY)],
        out_specs=pl.BlockSpec(memory_space=pltpu.VMEM),
        scratch_shapes=[
            pltpu.VMEM((2 * STEPS, tiles, size, size), f32),
            pltpu.VMEM((STEPS, tiles, size, size), f32),
            pltpu.VMEM((STEPS, tiles, size, size), bf16),
            pltpu.VMEM((STEPS, tiles, size, size), bf16),
            pltpu.VMEM((2 * STEPS, size, size), f32),
            pltpu.SMEM(pattern.shape, jnp.int32),
            pltpu.SemaphoreType.DMA((2 * STEPS,)),
            pltpu.SemaphoreType.DMA((len(ROW),)),
            pltpu.SemaphoreType.DMA((STEPS,)),
            pltpu.SemaphoreType.DMA((len(COL),)),
            pltpu.SemaphoreType.DMA((3,)),
        ],
        compiler_params=pltpu.CompilerParams(
            collective_id=0, has_side_effects=True, vmem_limit_bytes=56 * 1024 * 1024),
    )(pattern, density)


def solution(mesh):
    placed = P("row", "col")
    return jax.shard_map(local, mesh=mesh, in_specs=(placed, placed), out_specs=placed, check_vma=False)
```

```python
import heapq

import jax
import jax.numpy as jnp
from jax import lax
from jax.experimental import pallas as pl
from jax.experimental.pallas import tpu as pltpu
from jax.sharding import PartitionSpec as P

BLOCK = 128
STEPS = 2
NX, NY, NZ = 4, 4, 8
MESH = pl.DeviceIdType.MESH
f32, bf16 = jnp.float32, jnp.bfloat16
OFFSETS = [(dx, dy) for dx in (0, 1, -1, 2) for dy in (0, 1, -1, 2)]
RING = (0, 1, -1, 2, -2, 3, -3, 4)

GROUPS = {}
BEGIN = [(plan, sign) for plan in (0, 1) for sign in (1, -1)]

ROWS64, HOP, SMALL, DOT, DOT_TILE = 1.31, 2.1, 0.03, 0.15, 0.12
NEAR_FIRST = [
    [(0, 0), (1, 0), (-1, 0), (0, 1), (0, -1)],
    [(2, 0), (0, 2), (1, 1), (1, -1), (-1, 1), (-1, -1)],
    [(1, 2), (-1, 2), (2, 1), (2, -1)],
    [(2, 2)],
]
COL_GROUPS = [[0], [1, -1], [2, -2], [3, -3], [4]]


def far_sign(h, plan, a=0):
    return 1 if (h + plan + (0, 1, 2, 1)[a]) % 2 == 0 else -1


def row_tile(p, h, plan, a, b):
    return [] if (a, b) == (0, 0) else [("row", p, h, plan, a, b, "h")]


def col_tile(s, h, dz, other):
    if other:
        return [("col", s, h, dz, "s")]
    if dz == 0:
        return []
    return [("col", s, h, dz, part) for part in (("q0", "q1") if dz == 4 else ("h",))]


def make_jobs():
    jobs = {}

    def link(plan, axis, sign):
        return ("x" if (axis == 0) == (plan == 0) else "y", sign)

    def own_row(p, h):
        pushes = []
        for axis in (0, 1):
            for plan in (0, 1):
                for sign in (1, -1):
                    a, b = (sign, 0) if axis == 0 else (0, sign)
                    pushes.append((link(plan, axis, sign), 1.0, ("row", p, h, plan, a, b, "h")))
        return pushes

    def own_col(s, h):
        pushes = []
        for t in (2 * h, 2 * h + 1):
            pushes += [(("z", sign), 1.0, ("col", s, t, sign, "h")) for sign in (1, -1)]
        return pushes + [(("core", 0), 0.15, ("col", s, t, 0, "s")) for t in (2 * h, 2 * h + 1)]

    def start(p, h):
        return ("start",) if p == 0 else ("final", p - 1, h)

    def add(name, priority, cost, needs, pushes=()):
        jobs[name] = (priority, cost + SMALL * (len(pushes) + len(needs)), needs, list(pushes))

    add(("start",), 0, SMALL, [], own_row(0, 0) + own_col(0, 0) + own_col(0, 1) + own_row(0, 1))
    for p in range(2 * STEPS):
        s = p // 2
        for h in (0, 1):
            for plan in (0, 1):
                for sign in (1, -1):
                    for a in (0, 1, -1, 2):
                        if sign == far_sign(h, plan, a):
                            add(("pass", p, h, plan, a, sign), 0, 0, row_tile(p, h, plan, a, sign),
                                [(link(plan, 1, sign), 1.0, ("row", p, h, plan, a, 2, "h"))])
                    pushes = []
                    if sign == far_sign(h, plan):
                        pushes = [(link(plan, 0, sign), 1.0, ("row", p, h, plan, 2, 0, "h"))]
                    pushes += [(link(plan, 1, turn), 1.0, ("row", p, h, plan, sign, turn, "h")) for turn in (1, -1)]
                    add(("turn", p, h, plan, sign), 0, 0, row_tile(p, h, plan, sign, 0), pushes)
                pushes = [(link(plan, 1, turn), 1.0, ("row", p, h, plan, 2, turn, "h")) for turn in (1, -1)]
                add(("turn", p, h, plan, 2), 0, 0, row_tile(p, h, plan, 2, 0), pushes)
            if p % 2 == 0:
                for t, dz in ((t, dz) for dz in RING for t in (2 * h, 2 * h + 1)):
                    pushes = []
                    if dz:
                        sign = 1 if dz > 0 else -1
                        if abs(dz) < 3:
                            pushes.append((("z", sign), 1.0, ("col", s, t, dz + sign, "h")))
                        elif dz != 4:
                            pushes.append((("z", sign), 0.5, ("col", s, t, 4, "q0" if sign == 1 else "q1")))
                        pushes.append((("core", 0), 0.15, ("col", s, t, dz, "s")))
                        add(("ring", s, t, dz), 0, 0, col_tile(s, t, dz, False), pushes)
                    before = [("ring", s, t, dz)] if dz else [start(p, h)]
                    add(("split", s, t, dz, False), 2, SMALL, before)
                    add(("split", s, t, dz, True), 2, SMALL, col_tile(s, t, dz, True))
            pieces = {o: row_tile(p, h, 0, *o) + row_tile(p, h, 1, *o[::-1]) for o in OFFSETS}
            if p % 2 == 0 and h == 0:
                need = [piece for o in OFFSETS for piece in pieces[o]]
                groups = [[(dz, other) for dz in group for other in (False, True)] for group in COL_GROUPS]
                needs = [need + [("split", s, t, *key) for t in range(4) for key in group] for group in groups]
            else:
                groups = NEAR_FIRST
                need = [("split", s, t, dz, other) for t in range(4) for dz in RING for other in (False, True)]
                needs = [[piece for key in group for piece in pieces[key]] + [start(p, h)] + (need if p % 2 == 0 else [])
                         for group in groups]
            for n, group in enumerate(groups):
                jobs[("mac", p, h, n)] = (4 + p, DOT + DOT_TILE * len(group), needs[n], [])
                GROUPS[p, h, n] = group
            pushes = []
            if p < 2 * STEPS - 1:
                pushes = own_row(p + 1, h) + (own_col(s + 1, h) if p % 2 else [])
            if p % 2 == 0 and h:
                add(("final", p, h), 1, 2 * SMALL, [("mac", p, h, n) for n in range(len(groups))])
                add(("begin", p, h), 1, 0, [("final", p, h)] + [("turn", p + 1, 0, *key) for key in BEGIN], pushes)
            else:
                add(("final", p, h), 1, 2 * SMALL, [("mac", p, h, n) for n in range(len(groups))], pushes)
    return jobs


def make_order(jobs):
    ready_at, missing, users = {}, {}, {}
    for name, (_, _, needs, _) in jobs.items():
        missing[name] = len(set(needs))
        ready_at[name] = 0.0
        for need in set(needs):
            users.setdefault(need, []).append(name)
    waiting, ready, free = [], [], {}
    rank = {name: n for n, name in enumerate(jobs)}

    def done(thing, when):
        for user in users.get(thing, ()):
            missing[user] -= 1
            ready_at[user] = max(ready_at[user], when)
            if missing[user] == 0:
                heapq.heappush(waiting, (ready_at[user], rank[user], user))

    for name in jobs:
        if missing[name] == 0:
            heapq.heappush(waiting, (0.0, rank[name], name))
    now, order, times = 0.0, [], {}
    while waiting or ready:
        if not ready and waiting[0][0] > now:
            now = waiting[0][0]
        while waiting and waiting[0][0] <= now:
            when, number, name = heapq.heappop(waiting)
            heapq.heappush(ready, (jobs[name][0], when, number, name))
        name = heapq.heappop(ready)[-1]
        _, cost, _, pushes = jobs[name]
        now += cost
        order.append(name)
        times[name] = now
        for where, amount, piece in pushes:
            rate = 1.0 if where[0] == "core" else ROWS64
            free[where] = max(free.get(where, 0.0), now) + amount * rate
            done(piece, free[where] + HOP)
        done(name, now)
    return order, times


JOBS = make_jobs()
ORDER, TIMES = make_order(JOBS)
PIECES = [piece for name in JOBS for _, _, piece in JOBS[name][3]]
ROW = {name: n for n, name in enumerate(piece for piece in PIECES if piece[0] == "row")}
COL = {name: n for n, name in enumerate(piece for piece in PIECES if piece[0] == "col")}


def split(value):
    high = value.astype(bf16)
    return high, (value - high.astype(f32)).astype(bf16)


def kernel(pattern_in, density, out, rows, cols, col_hi, col_lo, acc, pattern,
           row_send, row_recv, col_send, col_recv, local_sem):
    size = density.shape[0]
    half, quarter, eighth = size // 2, size // 4, size // 8
    r, c = lax.axis_index("row"), lax.axis_index("col")
    z, core = r // 2, r % 2
    y, x = c // NX, c % NX

    def device(dx=0, dy=0, dz=0):
        return (((z + dz + NZ) % NZ) * 2 + core, ((y + dy + NY) % NY) * NX + (x + dx + NX) % NX)

    sibling = (z * 2 + 1 - core, c)

    def k_row(dx, dy):
        return ((y - dy + NY) % NY) * NX + (x - dx + NX) % NX

    def k_col(dz, other):
        return ((z - dz + NZ) % NZ) * 2 + (1 - core if other else core)

    fetch = [
        pltpu.make_async_copy(density, rows.at[0, c], local_sem.at[0]),
        pltpu.make_async_copy(density, cols.at[0, r], local_sem.at[1]),
        pltpu.make_async_copy(pattern_in, pattern, local_sem.at[2]),
    ]
    for copy in fetch:
        copy.start()

    peers = [device(dx=1), device(dx=-1), device(dy=1), device(dy=-1), device(dz=1), device(dz=-1), sibling]
    barrier = pltpu.get_barrier_semaphore()
    for peer in peers:
        pl.semaphore_signal(barrier, inc=1, device_id=peer, device_id_type=MESH)
    pl.semaphore_wait(barrier, len(peers))
    for copy in fetch:
        copy.wait()

    mask = [[pattern[a, b].astype(f32) for b in range(2)] for a in range(2)]

    def masked(value, h):
        return jnp.concatenate([value[:, :BLOCK] * mask[h][0], value[:, BLOCK:] * mask[h][1]], axis=1)

    def copy_of(piece, target):
        if piece[0] == "row":
            _, p, h, plan, a, b, part = piece
            dx, dy = (a, b) if plan == 0 else (b, a)
            low = h * half + plan * quarter
            return rows, p, low, quarter, row_send.at[p], row_recv.at[ROW[piece]], (dx, dy)
        _, s, h, dz, part = piece
        low = h * quarter + (eighth if part == "q1" else 0)
        return (cols, s, low, eighth if part in ("q0", "q1") else quarter, col_send.at[s], col_recv.at[COL[piece]], dz)

    def push(where, piece):
        buffer, index, low, count, send, recv, offset = copy_of(piece, None)
        axis, sign = where
        if piece[0] == "row":
            dx, dy = offset
            held = k_row(dx - sign, dy) if axis == "x" else k_row(dx, dy - sign)
        else:
            held = k_col(offset if axis == "core" else offset - sign, False)
        target = sibling if axis == "core" else device(**{"d" + axis: sign})
        part = buffer.at[index, held, pl.ds(low, count)]
        pltpu.make_async_remote_copy(
            src_ref=part, dst_ref=part, send_sem=send, recv_sem=recv,
            device_id=target, device_id_type=MESH).start()

    def wait(piece):
        buffer, index, low, count, send, recv, offset = copy_of(piece, None)
        if piece[0] == "row":
            held = k_row(*offset)
        else:
            held = k_col(offset, piece[-1] == "s")
        part = buffer.at[index, held, pl.ds(low, count)]
        pltpu.make_async_remote_copy(
            src_ref=part, dst_ref=part, send_sem=send, recv_sem=recv,
            device_id=sibling, device_id_type=MESH).wait_recv()

    waited, begun = set(), set()

    def run(name):
        _, _, needs, pushes = JOBS[name]
        for need in needs:
            if need[0] in ("row", "col") and need not in waited:
                waited.add(need)
                wait(need)
        kind = name[0]
        if kind == "split":
            _, s, h, dz, other = name
            k = k_col(dz, other)
            here = pl.ds(h * quarter, quarter)
            high, low = split(cols[s, k, here, :])
            col_hi[s, k, here, :] = high
            col_lo[s, k, here, :] = low
        elif kind == "mac":
            _, p, h = name[:3]
            here = pl.ds(h * half, half)
            term = None
            for key in GROUPS[name[1:]]:
                k = k_col(*key) if isinstance(key[1], bool) else k_row(*key)
                high_a, low_a = split(rows[p, k, here, :])
                high_b, low_b = col_hi[p // 2, k], col_lo[p // 2, k]
                for one, other in ((high_a, high_b), (high_a, low_b), (low_a, high_b)):
                    dot = jnp.dot(one, other, preferred_element_type=f32)
                    term = dot if term is None else term + dot
            if (p, h) in begun:
                acc[p, here, :] += term
            else:
                begun.add((p, h))
                acc[p, here, :] = term
        elif kind == "final":
            _, p, h = name
            here = pl.ds(h * half, half)
            value = masked(acc[p, here, :], h)
            if p % 2:
                value = 3.0 * rows[p, c, here, :] - 2.0 * value
            if p == 2 * STEPS - 1:
                out[here, :] = value
            else:
                rows[p + 1, c, here, :] = value
                if p % 2:
                    cols[p // 2 + 1, r, here, :] = value
        for where, _, piece in pushes:
            push(where, piece)

    for name in ORDER:
        run(name)

    for p in range(2 * STEPS):
        whole = rows.at[p, pl.ds(0, 15)]
        pltpu.make_async_copy(whole, whole, row_send.at[p]).wait()
    for s in range(STEPS):
        whole = cols.at[s, pl.ds(0, 15)]
        pltpu.make_async_copy(whole, whole, col_send.at[s]).wait()


def local(density, pattern):
    size = density.shape[0]
    tiles = NX * NY
    return pl.pallas_call(
        kernel,
        out_shape=jax.ShapeDtypeStruct(density.shape, f32),
        in_specs=[pl.BlockSpec(memory_space=pltpu.HBM), pl.BlockSpec(memory_space=pltpu.HBM)],
        out_specs=pl.BlockSpec(memory_space=pltpu.VMEM),
        scratch_shapes=[
            pltpu.VMEM((2 * STEPS, tiles, size, size), f32),
            pltpu.VMEM((STEPS, tiles, size, size), f32),
            pltpu.VMEM((STEPS, tiles, size, size), bf16),
            pltpu.VMEM((STEPS, tiles, size, size), bf16),
            pltpu.VMEM((2 * STEPS, size, size), f32),
            pltpu.SMEM(pattern.shape, jnp.int32),
            pltpu.SemaphoreType.DMA((2 * STEPS,)),
            pltpu.SemaphoreType.DMA((len(ROW),)),
            pltpu.SemaphoreType.DMA((STEPS,)),
            pltpu.SemaphoreType.DMA((len(COL),)),
            pltpu.SemaphoreType.DMA((3,)),
        ],
        compiler_params=pltpu.CompilerParams(
            collective_id=0, has_side_effects=True, vmem_limit_bytes=56 * 1024 * 1024),
    )(pattern, density)


def solution(mesh):
    placed = P("row", "col")
    return jax.shard_map(local, mesh=mesh, in_specs=(placed, placed), out_specs=placed, check_vma=False)
```

```python
import heapq

import jax
import jax.numpy as jnp
from jax import lax
from jax.experimental import pallas as pl
from jax.experimental.pallas import tpu as pltpu
from jax.sharding import PartitionSpec as P

BLOCK = 128
STEPS = 2
NX, NY, NZ = 4, 4, 8
MESH = pl.DeviceIdType.MESH
f32, bf16 = jnp.float32, jnp.bfloat16
OFFSETS = [(dx, dy) for dx in (0, 1, -1, 2) for dy in (0, 1, -1, 2)]
RING = (0, 1, -1, 2, -2, 3, -3, 4)

GROUPS = {}
BEGIN_ROWS = [(0, 2), (1, 2)]
BEGIN_COLS = (1, -1)
BEGIN = [(plan, sign) for plan in (0, 1) for sign in (1, -1)]

ROWS64, HOP, SMALL, DOT, DOT_TILE = 1.31, 2.1, 0.03, 0.15, 0.12
NEAR_FIRST = [
    [(0, 0), (1, 0), (-1, 0), (0, 1), (0, -1)],
    [(2, 0), (0, 2), (1, 1), (1, -1), (-1, 1), (-1, -1)],
    [(1, 2), (-1, 2), (2, 1), (2, -1)],
    [(2, 2)],
]
COL_GROUPS = [[0], [1, -1], [2, -2], [3, -3], [4]]


HALVES = [(0, 128, 0, 256), (128, 128, 0, 256)]
SQUARE = [(0, 128, 0, 128), (0, 128, 128, 128), (128, 128, 0, 256)]
STREAMS = [HALVES, SQUARE, HALVES, SQUARE, HALVES]
COLUMNS = [(0, 128, 0, 128), (128, 128, 0, 128), (0, 128, 128, 128), (128, 128, 128, 128)]
COL_SIZE = 1.0


def far_sign(h, plan, a=0):
    return 1 if (h + plan + (0, 1, 2, 1)[a]) % 2 == 0 else -1


def row_tile(p, h, plan, a, b):
    return [] if (a, b) == (0, 0) else [("row", p, h, plan, a, b, "h")]


def col_tile(s, t, dz, other):
    if other:
        return [("col", s, t, dz, "s")]
    if dz == 0:
        return []
    return [("col", s, t, dz, part) for part in (("q0", "q1") if dz == 4 else ("h",))]


def make_jobs():
    jobs = {}

    def link(plan, axis, sign):
        return ("x" if (axis == 0) == (plan == 0) else "y", sign)

    def row_size(p, h):
        return STREAMS[p][h][1] * STREAMS[p][h][3] / (128 * 256)

    def own_row(p, h):
        pushes = []
        for axis in (0, 1):
            for plan in (0, 1):
                for sign in (1, -1):
                    a, b = (sign, 0) if axis == 0 else (0, sign)
                    pushes.append((link(plan, axis, sign), row_size(p, h), ("row", p, h, plan, a, b, "h")))
        return pushes

    def own_col(s, ts):
        pushes = []
        for t in ts:
            pushes += [(("z", sign), COL_SIZE, ("col", s, t, sign, "h")) for sign in (1, -1)]
        return pushes + [(("core", 0), 0.15, ("col", s, t, 0, "s")) for t in ts]

    def overlap(one, other):
        return all(one[i] < other[i] + other[i + 1] and other[i] < one[i] + one[i + 1] for i in (0, 2))

    def add(name, priority, cost, needs, pushes=()):
        jobs[name] = (priority, cost + SMALL * (len(pushes) + len(needs)), needs, list(pushes))

    add(("start",), 0, SMALL, [], own_row(0, 0) + own_col(0, (0, 1)))
    add(("begin", 0, 1), 0, 0, [("turn", 0, 0, *key) for key in BEGIN_ROWS], own_row(0, 1))
    add(("begin_col",), 0, 0, [("ring", 0, t, dz) for t in (0, 1) for dz in BEGIN_COLS], own_col(0, (2, 3)))
    for p in range(2 * STEPS):
        s = p // 2
        for h, stream in enumerate(STREAMS[p]):
            size = row_size(p, h)
            for plan in (0, 1):
                for sign in (1, -1):
                    for a in (0, 1, -1, 2):
                        if sign == far_sign(h, plan, a):
                            add(("pass", p, h, plan, a, sign), 0, 0, row_tile(p, h, plan, a, sign),
                                [(link(plan, 1, sign), size, ("row", p, h, plan, a, 2, "h"))])
                    pushes = []
                    if sign == far_sign(h, plan):
                        pushes = [(link(plan, 0, sign), size, ("row", p, h, plan, 2, 0, "h"))]
                    pushes += [(link(plan, 1, turn), size, ("row", p, h, plan, sign, turn, "h")) for turn in (1, -1)]
                    add(("turn", p, h, plan, sign), 0, 0, row_tile(p, h, plan, sign, 0), pushes)
                pushes = [(link(plan, 1, turn), size, ("row", p, h, plan, 2, turn, "h")) for turn in (1, -1)]
                add(("turn", p, h, plan, 2), 0, 0, row_tile(p, h, plan, 2, 0), pushes)
        if p % 2 == 0:
            for t, dz in ((t, dz) for dz in RING for t in range(4)):
                pushes = []
                if dz:
                    sign = 1 if dz > 0 else -1
                    if abs(dz) < 3:
                        pushes.append((("z", sign), COL_SIZE, ("col", s, t, dz + sign, "h")))
                    elif dz != 4:
                        pushes.append((("z", sign), COL_SIZE / 2, ("col", s, t, 4, "q0" if sign == 1 else "q1")))
                    pushes.append((("core", 0), 0.15, ("col", s, t, dz, "s")))
                    add(("ring", s, t, dz), 0, 0, col_tile(s, t, dz, False), pushes)
                before = [("ring", s, t, dz)] if dz else [("start",) if p == 0 else ("final", p - 1, t % 2)]
                add(("split", s, t, dz, False), 2, SMALL, before)
                add(("split", s, t, dz, True), 2, SMALL, col_tile(s, t, dz, True))
        for o, target in enumerate(STREAMS[p + 1]):
            rows_used = [h for h, stream in enumerate(STREAMS[p]) if overlap(stream, (target[0], target[1], 0, 256))]
            cols_used = [t for t, col in enumerate(COLUMNS) if overlap(col, (0, 256, target[2], target[3]))]
            pieces = {key: [piece for h in rows_used
                            for piece in row_tile(p, h, 0, *key) + row_tile(p, h, 1, *key[::-1])] for key in OFFSETS}
            starts = [("start",) if p == 0 else ("final", p - 1, h) for h in rows_used]
            if p % 2 == 0 and target[0] == 0:
                need = [piece for key in OFFSETS for piece in pieces[key]] + starts
                groups = [[(dz, other) for dz in group for other in (False, True)] for group in COL_GROUPS]
                needs = [need + [("split", s, t, *key) for t in cols_used for key in group] for group in groups]
            else:
                groups = NEAR_FIRST
                need = [("split", s, t, dz, other) for t in cols_used for dz in RING for other in (False, True)]
                needs = [[piece for key in group for piece in pieces[key]] + starts + (need if p % 2 == 0 else [])
                         for group in groups]
            for n, group in enumerate(groups):
                cost = DOT + DOT_TILE * len(group) * (0.6 if target[3] == 128 else 1)
                jobs[("mac", p, o, n)] = (4 + p, cost, needs[n], [])
                GROUPS[p, o, n] = group
            pushes = []
            if p < 2 * STEPS - 1:
                pushes = own_row(p + 1, o) + (own_col(s + 1, (o, 2 + o)) if p % 2 else [])
            macs = [("mac", p, o, n) for n in range(len(groups))]
            if p % 2 == 0 and o == 2:
                add(("final", p, o), 1, 2 * SMALL, macs)
                add(("begin", p, o), 1, 0, [("final", p, o)] + [("turn", p + 1, 1, *key) for key in BEGIN], pushes)
            else:
                add(("final", p, o), 1, 2 * SMALL, macs, pushes)
    return jobs


def make_order(jobs):
    ready_at, missing, users = {}, {}, {}
    for name, (_, _, needs, _) in jobs.items():
        missing[name] = len(set(needs))
        ready_at[name] = 0.0
        for need in set(needs):
            users.setdefault(need, []).append(name)
    waiting, ready, free = [], [], {}
    rank = {name: n for n, name in enumerate(jobs)}

    def done(thing, when):
        for user in users.get(thing, ()):
            missing[user] -= 1
            ready_at[user] = max(ready_at[user], when)
            if missing[user] == 0:
                heapq.heappush(waiting, (ready_at[user], rank[user], user))

    for name in jobs:
        if missing[name] == 0:
            heapq.heappush(waiting, (0.0, rank[name], name))
    now, order, times = 0.0, [], {}
    while waiting or ready:
        if not ready and waiting[0][0] > now:
            now = waiting[0][0]
        while waiting and waiting[0][0] <= now:
            when, number, name = heapq.heappop(waiting)
            heapq.heappush(ready, (jobs[name][0], when, number, name))
        name = heapq.heappop(ready)[-1]
        _, cost, _, pushes = jobs[name]
        now += cost
        order.append(name)
        times[name] = now
        for where, amount, piece in pushes:
            rate = 1.0 if where[0] == "core" else ROWS64
            free[where] = max(free.get(where, 0.0), now) + amount * rate
            done(piece, free[where] + HOP)
        done(name, now)
    return order, times


JOBS = make_jobs()
ORDER, TIMES = make_order(JOBS)
PIECES = [piece for name in JOBS for _, _, piece in JOBS[name][3]]
ROW = {name: n for n, name in enumerate(piece for piece in PIECES if piece[0] == "row")}
COL = {name: n for n, name in enumerate(piece for piece in PIECES if piece[0] == "col")}


def split(value):
    high = value.astype(bf16)
    return high, (value - high.astype(f32)).astype(bf16)


def kernel(pattern_in, density, out, rows, cols, col_hi, col_lo, acc, pattern,
           row_send, row_recv, col_send, col_recv, local_sem):
    size = density.shape[0]
    r, c = lax.axis_index("row"), lax.axis_index("col")
    z, core = r // 2, r % 2
    y, x = c // NX, c % NX

    def device(dx=0, dy=0, dz=0):
        return (((z + dz + NZ) % NZ) * 2 + core, ((y + dy + NY) % NY) * NX + (x + dx + NX) % NX)

    sibling = (z * 2 + 1 - core, c)

    def k_row(dx, dy):
        return ((y - dy + NY) % NY) * NX + (x - dx + NX) % NX

    def k_col(dz, other):
        return ((z - dz + NZ) % NZ) * 2 + (1 - core if other else core)

    fetch = [
        pltpu.make_async_copy(density, rows.at[0, c], local_sem.at[0]),
        pltpu.make_async_copy(density, cols.at[0, r], local_sem.at[1]),
        pltpu.make_async_copy(pattern_in, pattern, local_sem.at[2]),
    ]
    for copy in fetch:
        copy.start()

    peers = [device(dx=1), device(dx=-1), device(dy=1), device(dy=-1), device(dz=1), device(dz=-1), sibling]
    barrier = pltpu.get_barrier_semaphore()
    for peer in peers:
        pl.semaphore_signal(barrier, inc=1, device_id=peer, device_id_type=MESH)
    pl.semaphore_wait(barrier, len(peers))
    for copy in fetch:
        copy.wait()

    mask = [[pattern[a, b].astype(f32) for b in range(2)] for a in range(2)]

    def masked(value, low, lane):
        parts = [value[:, n:n + BLOCK] * mask[low // BLOCK][(lane + n) // BLOCK] for n in range(0, value.shape[1], BLOCK)]
        return jnp.concatenate(parts, axis=1)

    def copy_of(piece):
        if piece[0] == "row":
            _, p, h, plan, a, b, _ = piece
            low, count, lane, lanes = STREAMS[p][h]
            here = pl.ds(low + plan * (count // 2), count // 2), pl.ds(lane, lanes)
            return rows, p, here, row_send.at[p], row_recv.at[ROW[piece]], (a, b) if plan == 0 else (b, a)
        _, s, t, dz, part = piece
        low, count, lane, lanes = COLUMNS[t]
        if part in ("q0", "q1"):
            count //= 2
            low += count if part == "q1" else 0
        here = pl.ds(low, count), pl.ds(lane, lanes)
        return cols, s, here, col_send.at[s], col_recv.at[COL[piece]], dz

    def push(where, piece):
        buffer, index, here, send, recv, offset = copy_of(piece)
        axis, sign = where
        if piece[0] == "row":
            dx, dy = offset
            held = k_row(dx - sign, dy) if axis == "x" else k_row(dx, dy - sign)
        else:
            held = k_col(offset if axis == "core" else offset - sign, False)
        target = sibling if axis == "core" else device(**{"d" + axis: sign})
        part = buffer.at[index, held, *here]
        pltpu.make_async_remote_copy(
            src_ref=part, dst_ref=part, send_sem=send, recv_sem=recv,
            device_id=target, device_id_type=MESH).start()

    def wait(piece):
        buffer, index, here, send, recv, offset = copy_of(piece)
        if piece[0] == "row":
            held = k_row(*offset)
        else:
            held = k_col(offset, piece[-1] == "s")
        part = buffer.at[index, held, *here]
        pltpu.make_async_remote_copy(
            src_ref=part, dst_ref=part, send_sem=send, recv_sem=recv,
            device_id=sibling, device_id_type=MESH).wait_recv()

    waited, begun = set(), set()

    def run(name):
        _, _, needs, pushes = JOBS[name]
        for need in needs:
            if need[0] in ("row", "col") and need not in waited:
                waited.add(need)
                wait(need)
        kind = name[0]
        if kind == "split":
            _, s, t, dz, other = name
            k = k_col(dz, other)
            here = pl.ds(*COLUMNS[t][:2]), pl.ds(*COLUMNS[t][2:])
            high, low = split(cols[s, k, *here])
            col_hi[s, k, *here] = high
            col_lo[s, k, *here] = low
        elif kind == "mac":
            _, p, o = name[:3]
            low, count, lane, lanes = STREAMS[p + 1][o]
            here, wide = pl.ds(low, count), pl.ds(lane, lanes)
            term = None
            for key in GROUPS[name[1:]]:
                k = k_col(*key) if isinstance(key[1], bool) else k_row(*key)
                high_a, low_a = split(rows[p, k, here, :])
                high_b, low_b = col_hi[p // 2, k, :, wide], col_lo[p // 2, k, :, wide]
                for one, other in ((high_a, high_b), (high_a, low_b), (low_a, high_b)):
                    dot = jnp.dot(one, other, preferred_element_type=f32)
                    term = dot if term is None else term + dot
            if (p, o) in begun:
                acc[p, here, wide] += term
            else:
                begun.add((p, o))
                acc[p, here, wide] = term
        elif kind == "final":
            _, p, o = name
            low, count, lane, lanes = STREAMS[p + 1][o]
            here, wide = pl.ds(low, count), pl.ds(lane, lanes)
            value = masked(acc[p, here, wide], low, lane)
            if p % 2:
                value = 3.0 * rows[p, c, here, wide] - 2.0 * value
            if p == 2 * STEPS - 1:
                out[here, wide] = value
            else:
                rows[p + 1, c, here, wide] = value
                if p % 2:
                    cols[p // 2 + 1, r, here, wide] = value
        for where, _, piece in pushes:
            push(where, piece)

    for name in ORDER:
        run(name)

    for p in range(2 * STEPS):
        whole = rows.at[p, pl.ds(0, 15)]
        pltpu.make_async_copy(whole, whole, row_send.at[p]).wait()
    for s in range(STEPS):
        whole = cols.at[s, pl.ds(0, 15)]
        pltpu.make_async_copy(whole, whole, col_send.at[s]).wait()


def local(density, pattern):
    size = density.shape[0]
    tiles = NX * NY
    return pl.pallas_call(
        kernel,
        out_shape=jax.ShapeDtypeStruct(density.shape, f32),
        in_specs=[pl.BlockSpec(memory_space=pltpu.HBM), pl.BlockSpec(memory_space=pltpu.HBM)],
        out_specs=pl.BlockSpec(memory_space=pltpu.VMEM),
        scratch_shapes=[
            pltpu.VMEM((2 * STEPS, tiles, size, size), f32),
            pltpu.VMEM((STEPS, tiles, size, size), f32),
            pltpu.VMEM((STEPS, tiles, size, size), bf16),
            pltpu.VMEM((STEPS, tiles, size, size), bf16),
            pltpu.VMEM((2 * STEPS, size, size), f32),
            pltpu.SMEM(pattern.shape, jnp.int32),
            pltpu.SemaphoreType.DMA((2 * STEPS,)),
            pltpu.SemaphoreType.DMA((len(ROW),)),
            pltpu.SemaphoreType.DMA((STEPS,)),
            pltpu.SemaphoreType.DMA((len(COL),)),
            pltpu.SemaphoreType.DMA((3,)),
        ],
        compiler_params=pltpu.CompilerParams(
            collective_id=0, has_side_effects=True, vmem_limit_bytes=56 * 1024 * 1024),
    )(pattern, density)


def solution(mesh):
    placed = P("row", "col")
    return jax.shard_map(local, mesh=mesh, in_specs=(placed, placed), out_specs=placed, check_vma=False)
```

```python
import heapq

import jax
import jax.numpy as jnp
from jax import lax
from jax.experimental import pallas as pl
from jax.experimental.pallas import tpu as pltpu
from jax.sharding import PartitionSpec as P

BLOCK = 128
STEPS = 2
NX, NY, NZ = 4, 4, 8
MESH = pl.DeviceIdType.MESH
f32, bf16 = jnp.float32, jnp.bfloat16
OFFSETS = [(dx, dy) for dx in (0, 1, -1, 2) for dy in (0, 1, -1, 2)]
RING = (0, 1, -1, 2, -2, 3, -3, 4)

GROUPS = {}
BEGIN_ROWS = [(0, 2), (1, 2)]
Z_STEPS = [(1, -1), (1, -1)]
BEGIN_COLS = (1, -1)
BEGIN = [(plan, sign) for plan in (0, 1) for sign in (1, -1)]

ROWS64, HOP, SMALL, DOT, DOT_TILE = 1.45, 2.2, 0.03, 0.15, 0.12
NEAR_FIRST = [
    [(0, 0), (1, 0), (-1, 0), (0, 1), (0, -1)],
    [(2, 0), (0, 2), (1, 1), (1, -1), (-1, 1), (-1, -1)],
    [(1, 2), (-1, 2), (2, 1), (2, -1)],
    [(2, 2)],
]
COL_GROUPS = [[0], [1, -1], [2, -2], [3, -3], [4]]


HALVES = [(0, 128, 0, 256), (128, 128, 0, 256)]
SQUARE = [(0, 128, 0, 128), (0, 128, 128, 128), (128, 128, 0, 256)]
STREAMS = [HALVES, SQUARE, HALVES, SQUARE, HALVES]
COLUMNS = [(0, 128, 0, 128), (128, 128, 0, 128), (0, 128, 128, 128), (128, 128, 128, 128)]
COL_SIZE = 1.0


def far_sign(h, plan, a=0):
    return 1 if (h + plan + (0, 1, 2, 1)[a]) % 2 == 0 else -1


def row_tile(p, h, plan, a, b):
    return [] if (a, b) == (0, 0) else [("row", p, h, plan, a, b, "h")]


def col_tile(s, t, dz, other):
    if other:
        return [("col", s, t, dz, "s")]
    if dz == 0:
        return []
    return [("col", s, t, dz, part) for part in (("q0", "q1") if dz == 4 else ("h",))]


def make_jobs():
    jobs = {}

    def link(plan, axis, sign):
        return ("x" if (axis == 0) == (plan == 0) else "y", sign)

    def row_size(p, h):
        return STREAMS[p][h][1] * STREAMS[p][h][3] / (128 * 256)

    def own_row(p, h):
        pushes = []
        for axis in (0, 1):
            for plan in (0, 1):
                for sign in (1, -1):
                    a, b = (sign, 0) if axis == 0 else (0, sign)
                    pushes.append((link(plan, axis, sign), row_size(p, h), ("row", p, h, plan, a, b, "h")))
        return pushes

    def own_col(s, ts):
        pushes = []
        for t in ts:
            pushes += [(("z", step), COL_SIZE, ("col", s, t, step, "h")) for step in Z_STEPS[s]]
        return pushes + [(("core", 0), 0.15, ("col", s, t, 0, "s")) for t in ts]

    def overlap(one, other):
        return all(one[i] < other[i] + other[i + 1] and other[i] < one[i] + one[i + 1] for i in (0, 2))

    def add(name, priority, cost, needs, pushes=()):
        jobs[name] = (priority, cost + SMALL * (len(pushes) + len(needs)), needs, list(pushes))

    add(("start",), 0, SMALL, [], own_row(0, 0) + own_col(0, (0, 1)))
    add(("begin", 0, 1), 0, 0, [("turn", 0, 0, *key) for key in BEGIN_ROWS], own_row(0, 1))
    add(("begin_col",), 0, 0, [("ring", 0, t, dz) for t in (0, 1) for dz in BEGIN_COLS], own_col(0, (2, 3)))
    for p in range(2 * STEPS):
        s = p // 2
        for h, stream in enumerate(STREAMS[p]):
            size = row_size(p, h)
            for plan in (0, 1):
                for sign in (1, -1):
                    for a in (0, 1, -1, 2):
                        if sign == far_sign(h, plan, a):
                            add(("pass", p, h, plan, a, sign), 0, 0, row_tile(p, h, plan, a, sign),
                                [(link(plan, 1, sign), size, ("row", p, h, plan, a, 2, "h"))])
                    pushes = []
                    if sign == far_sign(h, plan):
                        pushes = [(link(plan, 0, sign), size, ("row", p, h, plan, 2, 0, "h"))]
                    pushes += [(link(plan, 1, turn), size, ("row", p, h, plan, sign, turn, "h")) for turn in (1, -1)]
                    add(("turn", p, h, plan, sign), 0, 0, row_tile(p, h, plan, sign, 0), pushes)
                pushes = [(link(plan, 1, turn), size, ("row", p, h, plan, 2, turn, "h")) for turn in (1, -1)]
                add(("turn", p, h, plan, 2), 0, 0, row_tile(p, h, plan, 2, 0), pushes)
        if p % 2 == 0:
            for t, dz in ((t, dz) for dz in RING for t in range(4)):
                pushes = []
                if dz:
                    sign = 1 if dz > 0 else -1
                    reach = max(Z_STEPS[s])
                    last = ("col", s, t, 4, "q0" if sign == 1 else "q1")
                    if dz != 4 and reach == 1:
                        pushes.append((("z", sign), COL_SIZE, ("col", s, t, dz + sign, "h")) if abs(dz) < 3
                                      else (("z", sign), COL_SIZE / 2, last))
                    elif abs(dz) == 2:
                        pushes.append((("z", sign), COL_SIZE, ("col", s, t, dz + sign, "h")))
                        pushes.append((("z", 2 * sign), COL_SIZE / 2, last))
                    pushes.append((("core", 0), 0.15, ("col", s, t, dz, "s")))
                    add(("ring", s, t, dz), 0, 0, col_tile(s, t, dz, False), pushes)
                before = [("ring", s, t, dz)] if dz else [("start",) if p == 0 else ("final", p - 1, t % 2)]
                add(("split", s, t, dz, False), 2, SMALL, before)
                add(("split", s, t, dz, True), 2, SMALL, col_tile(s, t, dz, True))
        for o, target in enumerate(STREAMS[p + 1]):
            rows_used = [h for h, stream in enumerate(STREAMS[p]) if overlap(stream, (target[0], target[1], 0, 256))]
            cols_used = [t for t, col in enumerate(COLUMNS) if overlap(col, (0, 256, target[2], target[3]))]
            pieces = {key: [piece for h in rows_used
                            for piece in row_tile(p, h, 0, *key) + row_tile(p, h, 1, *key[::-1])] for key in OFFSETS}
            starts = [("start",) if p == 0 else ("final", p - 1, h) for h in rows_used]
            if p % 2 == 0 and target[0] == 0:
                need = [piece for key in OFFSETS for piece in pieces[key]] + starts
                groups = [[(dz, other) for dz in group for other in (False, True)] for group in COL_GROUPS]
                needs = [need + [("split", s, t, *key) for t in cols_used for key in group] for group in groups]
            else:
                groups = NEAR_FIRST
                need = [("split", s, t, dz, other) for t in cols_used for dz in RING for other in (False, True)]
                needs = [[piece for key in group for piece in pieces[key]] + starts + (need if p % 2 == 0 else [])
                         for group in groups]
            for n, group in enumerate(groups):
                cost = DOT + DOT_TILE * len(group) * (0.6 if target[3] == 128 else 1)
                jobs[("mac", p, o, n)] = (4 + p, cost, needs[n], [])
                GROUPS[p, o, n] = group
            pushes = []
            if p < 2 * STEPS - 1:
                pushes = own_row(p + 1, o) + (own_col(s + 1, (o, 2 + o)) if p % 2 else [])
            macs = [("mac", p, o, n) for n in range(len(groups))]
            if p % 2 == 0 and o == 2:
                add(("final", p, o), 1, 2 * SMALL, macs)
                add(("begin", p, o), 1, 0, [("final", p, o)] + [("turn", p + 1, 1, *key) for key in BEGIN], pushes)
            else:
                add(("final", p, o), 1, 2 * SMALL, macs, pushes)
    return jobs


def make_order(jobs):
    ready_at, missing, users = {}, {}, {}
    for name, (_, _, needs, _) in jobs.items():
        missing[name] = len(set(needs))
        ready_at[name] = 0.0
        for need in set(needs):
            users.setdefault(need, []).append(name)
    waiting, ready, free = [], [], {}
    rank = {name: n for n, name in enumerate(jobs)}

    def done(thing, when):
        for user in users.get(thing, ()):
            missing[user] -= 1
            ready_at[user] = max(ready_at[user], when)
            if missing[user] == 0:
                heapq.heappush(waiting, (ready_at[user], rank[user], user))

    for name in jobs:
        if missing[name] == 0:
            heapq.heappush(waiting, (0.0, rank[name], name))
    now, order, times = 0.0, [], {}
    while waiting or ready:
        if not ready and waiting[0][0] > now:
            now = waiting[0][0]
        while waiting and waiting[0][0] <= now:
            when, number, name = heapq.heappop(waiting)
            heapq.heappush(ready, (jobs[name][0], when, number, name))
        name = heapq.heappop(ready)[-1]
        _, cost, _, pushes = jobs[name]
        now += cost
        order.append(name)
        times[name] = now
        for (axis, steps), amount, piece in pushes:
            way = axis, steps > 0
            free[way] = max(free.get(way, 0.0), now) + amount * max(1, abs(steps)) * ROWS64
            done(piece, free[way] + HOP)
        done(name, now)
    return order, times


JOBS = make_jobs()
ORDER, TIMES = make_order(JOBS)
PIECES = [piece for name in JOBS for _, _, piece in JOBS[name][3]]
ROW = {name: n for n, name in enumerate(piece for piece in PIECES if piece[0] == "row")}
COL = {name: n for n, name in enumerate(piece for piece in PIECES if piece[0] == "col")}


def split(value):
    high = value.astype(bf16)
    return high, (value - high.astype(f32)).astype(bf16)


def kernel(pattern_in, density, out, rows, cols, col_hi, col_lo, acc, pattern,
           row_send, row_recv, col_send, col_recv, local_sem):
    size = density.shape[0]
    r, c = lax.axis_index("row"), lax.axis_index("col")
    z, core = r // 2, r % 2
    y, x = c // NX, c % NX

    def device(dx=0, dy=0, dz=0):
        return (((z + dz + NZ) % NZ) * 2 + core, ((y + dy + NY) % NY) * NX + (x + dx + NX) % NX)

    sibling = (z * 2 + 1 - core, c)

    def k_row(dx, dy):
        return ((y - dy + NY) % NY) * NX + (x - dx + NX) % NX

    def k_col(dz, other):
        return ((z - dz + NZ) % NZ) * 2 + (1 - core if other else core)

    fetch = [
        pltpu.make_async_copy(density, rows.at[0, c], local_sem.at[0]),
        pltpu.make_async_copy(density, cols.at[0, r], local_sem.at[1]),
        pltpu.make_async_copy(pattern_in, pattern, local_sem.at[2]),
    ]
    for copy in fetch:
        copy.start()

    peers = [device(dx=1), device(dx=-1), device(dy=1), device(dy=-1), sibling]
    peers += [device(dz=step) for step in (1, -1)]
    barrier = pltpu.get_barrier_semaphore()
    for peer in peers:
        pl.semaphore_signal(barrier, inc=1, device_id=peer, device_id_type=MESH)
    pl.semaphore_wait(barrier, len(peers))
    for copy in fetch:
        copy.wait()

    mask = [[pattern[a, b].astype(f32) for b in range(2)] for a in range(2)]

    def masked(value, low, lane):
        parts = [value[:, n:n + BLOCK] * mask[low // BLOCK][(lane + n) // BLOCK] for n in range(0, value.shape[1], BLOCK)]
        return jnp.concatenate(parts, axis=1)

    def copy_of(piece):
        if piece[0] == "row":
            _, p, h, plan, a, b, _ = piece
            low, count, lane, lanes = STREAMS[p][h]
            here = pl.ds(low + plan * (count // 2), count // 2), pl.ds(lane, lanes)
            return rows, p, here, row_send.at[p], row_recv.at[ROW[piece]], (a, b) if plan == 0 else (b, a)
        _, s, t, dz, part = piece
        low, count, lane, lanes = COLUMNS[t]
        if part in ("q0", "q1"):
            count //= 2
            low += count if part == "q1" else 0
        here = pl.ds(low, count), pl.ds(lane, lanes)
        return cols, s, here, col_send.at[s], col_recv.at[COL[piece]], dz

    def push(where, piece):
        buffer, index, here, send, recv, offset = copy_of(piece)
        axis, sign = where
        if piece[0] == "row":
            dx, dy = offset
            held = k_row(dx - sign, dy) if axis == "x" else k_row(dx, dy - sign)
        else:
            held = k_col(offset if axis == "core" else offset - sign, False)
        target = sibling if axis == "core" else device(**{"d" + axis: sign})
        part = buffer.at[index, held, *here]
        pltpu.make_async_remote_copy(
            src_ref=part, dst_ref=part, send_sem=send, recv_sem=recv,
            device_id=target, device_id_type=MESH).start()

    def wait(piece):
        buffer, index, here, send, recv, offset = copy_of(piece)
        if piece[0] == "row":
            held = k_row(*offset)
        else:
            held = k_col(offset, piece[-1] == "s")
        part = buffer.at[index, held, *here]
        pltpu.make_async_remote_copy(
            src_ref=part, dst_ref=part, send_sem=send, recv_sem=recv,
            device_id=sibling, device_id_type=MESH).wait_recv()

    waited, begun = set(), set()

    def run(name):
        _, _, needs, pushes = JOBS[name]
        for need in needs:
            if need[0] in ("row", "col") and need not in waited:
                waited.add(need)
                wait(need)
        kind = name[0]
        if kind == "split":
            _, s, t, dz, other = name
            k = k_col(dz, other)
            here = pl.ds(*COLUMNS[t][:2]), pl.ds(*COLUMNS[t][2:])
            high, low = split(cols[s, k, *here])
            col_hi[s, k, *here] = high
            col_lo[s, k, *here] = low
        elif kind == "mac":
            _, p, o = name[:3]
            low, count, lane, lanes = STREAMS[p + 1][o]
            here, wide = pl.ds(low, count), pl.ds(lane, lanes)
            places = [k_col(*key) if isinstance(key[1], bool) else k_row(*key) for key in GROUPS[name[1:]]]
            if (p, o) not in begun:
                begun.add((p, o))
                acc[p, here, wide] = jnp.zeros((count, lanes), f32)

            def one_tile(n, carry):
                k = places[0]
                for other in range(1, len(places)):
                    k = jnp.where(n == other, places[other], k)
                high_a, low_a = split(rows[p, k, here, :])
                high_b, low_b = col_hi[p // 2, k, :, wide], col_lo[p // 2, k, :, wide]
                left = jnp.concatenate([high_a, low_a, high_a], axis=1)
                right = jnp.concatenate([high_b, high_b, low_b], axis=0)
                acc[p, here, wide] += jnp.dot(left, right, preferred_element_type=f32)
                return carry

            lax.fori_loop(0, len(places), one_tile, 0)
        elif kind == "final":
            _, p, o = name
            low, count, lane, lanes = STREAMS[p + 1][o]
            here, wide = pl.ds(low, count), pl.ds(lane, lanes)
            value = masked(acc[p, here, wide], low, lane)
            if p % 2:
                value = 3.0 * rows[p, c, here, wide] - 2.0 * value
            if p == 2 * STEPS - 1:
                out[here, wide] = value
            else:
                rows[p + 1, c, here, wide] = value
                if p % 2:
                    cols[p // 2 + 1, r, here, wide] = value
        for where, _, piece in pushes:
            push(where, piece)

    for name in ORDER:
        run(name)

    for p in range(2 * STEPS):
        whole = rows.at[p, pl.ds(0, 15)]
        pltpu.make_async_copy(whole, whole, row_send.at[p]).wait()
    for s in range(STEPS):
        whole = cols.at[s, pl.ds(0, 15)]
        pltpu.make_async_copy(whole, whole, col_send.at[s]).wait()


def local(density, pattern):
    size = density.shape[0]
    tiles = NX * NY
    return pl.pallas_call(
        kernel,
        out_shape=jax.ShapeDtypeStruct(density.shape, f32),
        in_specs=[pl.BlockSpec(memory_space=pltpu.HBM), pl.BlockSpec(memory_space=pltpu.HBM)],
        out_specs=pl.BlockSpec(memory_space=pltpu.VMEM),
        scratch_shapes=[
            pltpu.VMEM((2 * STEPS, tiles, size, size), f32),
            pltpu.VMEM((STEPS, tiles, size, size), f32),
            pltpu.VMEM((STEPS, tiles, size, size), bf16),
            pltpu.VMEM((STEPS, tiles, size, size), bf16),
            pltpu.VMEM((2 * STEPS, size, size), f32),
            pltpu.SMEM(pattern.shape, jnp.int32),
            pltpu.SemaphoreType.DMA((2 * STEPS,)),
            pltpu.SemaphoreType.DMA((len(ROW),)),
            pltpu.SemaphoreType.DMA((STEPS,)),
            pltpu.SemaphoreType.DMA((len(COL),)),
            pltpu.SemaphoreType.DMA((3,)),
        ],
        compiler_params=pltpu.CompilerParams(
            collective_id=0, has_side_effects=True, vmem_limit_bytes=56 * 1024 * 1024),
    )(pattern, density)


def solution(mesh):
    placed = P("row", "col")
    return jax.shard_map(local, mesh=mesh, in_specs=(placed, placed), out_specs=placed, check_vma=False)
```

```python
import heapq

import jax
import jax.numpy as jnp
from jax import lax
from jax.experimental import pallas as pl
from jax.experimental.pallas import tpu as pltpu
from jax.sharding import PartitionSpec as P

BLOCK = 128
STEPS = 2
NX, NY, NZ = 4, 4, 8
MESH = pl.DeviceIdType.MESH
f32, bf16 = jnp.float32, jnp.bfloat16
OFFSETS = [(dx, dy) for dx in (0, 1, -1, 2) for dy in (0, 1, -1, 2)]
RING = (0, 1, -1, 2, -2, 3, -3, 4)

GROUPS = {}
BEGIN_ROWS = [(0, 2), (1, 2)]
Z_STEPS = [(1, -1), (1, -1)]
BEGIN_COLS = (1, -1)
BEGIN = [(plan, sign) for plan in (0, 1) for sign in (1, -1)]

ROWS64, HOP, SMALL, DOT, DOT_TILE = 1.45, 2.2, 0.03, 0.15, 0.12
NEAR_FIRST = [
    [(0, 0), (1, 0), (-1, 0), (0, 1), (0, -1)],
    [(2, 0), (0, 2), (1, 1), (1, -1), (-1, 1), (-1, -1)],
    [(1, 2), (-1, 2), (2, 1), (2, -1)],
    [(2, 2)],
]
COL_GROUPS = [[0], [1, -1], [2, -2], [3, -3], [4]]


HALVES = [(0, 128, 0, 256), (128, 128, 0, 256)]
SQUARE = [(0, 128, 0, 128), (0, 128, 128, 128), (128, 128, 0, 256)]
STREAMS = [HALVES, SQUARE, HALVES, SQUARE, HALVES]
COLUMNS = [(0, 128, 0, 128), (128, 128, 0, 128), (0, 128, 128, 128), (128, 128, 128, 128)]
COL_SIZE = 1.0


def far_sign(h, plan, a=0):
    return 1 if (h + plan + (0, 1, 2, 1)[a]) % 2 == 0 else -1


def row_tile(p, h, plan, a, b):
    return [] if (a, b) == (0, 0) else [("row", p, h, plan, a, b, "h")]


def col_tile(s, t, dz, other):
    if other:
        return [("col", s, t, dz, "s")]
    if dz == 0:
        return []
    return [("col", s, t, dz, part) for part in (("q0", "q1") if dz == 4 else ("h",))]


def make_jobs():
    jobs = {}

    def link(plan, axis, sign):
        return ("x" if (axis == 0) == (plan == 0) else "y", sign)

    def row_size(p, h):
        return STREAMS[p][h][1] * STREAMS[p][h][3] / (128 * 256)

    def own_row(p, h):
        pushes = []
        for axis in (0, 1):
            for plan in (0, 1):
                for sign in (1, -1):
                    a, b = (sign, 0) if axis == 0 else (0, sign)
                    pushes.append((link(plan, axis, sign), row_size(p, h), ("row", p, h, plan, a, b, "h")))
        return pushes

    def own_col(s, ts):
        pushes = []
        for t in ts:
            pushes += [(("z", step), COL_SIZE, ("col", s, t, step, "h")) for step in Z_STEPS[s]]
        return pushes + [(("core", 0), 0.15, ("col", s, t, 0, "s")) for t in ts]

    def overlap(one, other):
        return all(one[i] < other[i] + other[i + 1] and other[i] < one[i] + one[i + 1] for i in (0, 2))

    def add(name, priority, cost, needs, pushes=()):
        jobs[name] = (priority, cost + SMALL * (len(pushes) + len(needs)), needs, list(pushes))

    add(("start",), 0, SMALL, [], own_row(0, 0) + own_col(0, (0, 1)))
    add(("begin", 0, 1), 0, 0, [("turn", 0, 0, *key) for key in BEGIN_ROWS], own_row(0, 1))
    add(("begin_col",), 0, 0, [("ring", 0, t, dz) for t in (0, 1) for dz in BEGIN_COLS], own_col(0, (2, 3)))
    for p in range(2 * STEPS):
        s = p // 2
        for h, stream in enumerate(STREAMS[p]):
            size = row_size(p, h)
            for plan in (0, 1):
                for sign in (1, -1):
                    for a in (0, 1, -1, 2):
                        if sign == far_sign(h, plan, a):
                            add(("pass", p, h, plan, a, sign), 0, 0, row_tile(p, h, plan, a, sign),
                                [(link(plan, 1, sign), size, ("row", p, h, plan, a, 2, "h"))])
                    pushes = []
                    if sign == far_sign(h, plan):
                        pushes = [(link(plan, 0, sign), size, ("row", p, h, plan, 2, 0, "h"))]
                    pushes += [(link(plan, 1, turn), size, ("row", p, h, plan, sign, turn, "h")) for turn in (1, -1)]
                    add(("turn", p, h, plan, sign), 0, 0, row_tile(p, h, plan, sign, 0), pushes)
                pushes = [(link(plan, 1, turn), size, ("row", p, h, plan, 2, turn, "h")) for turn in (1, -1)]
                add(("turn", p, h, plan, 2), 0, 0, row_tile(p, h, plan, 2, 0), pushes)
        if p % 2 == 0:
            for t, dz in ((t, dz) for dz in RING for t in range(4)):
                pushes = []
                if dz:
                    sign = 1 if dz > 0 else -1
                    reach = max(Z_STEPS[s])
                    last = ("col", s, t, 4, "q0" if sign == 1 else "q1")
                    if dz != 4 and reach == 1:
                        pushes.append((("z", sign), COL_SIZE, ("col", s, t, dz + sign, "h")) if abs(dz) < 3
                                      else (("z", sign), COL_SIZE / 2, last))
                    elif abs(dz) == 2:
                        pushes.append((("z", sign), COL_SIZE, ("col", s, t, dz + sign, "h")))
                        pushes.append((("z", 2 * sign), COL_SIZE / 2, last))
                    pushes.append((("core", 0), 0.15, ("col", s, t, dz, "s")))
                    add(("ring", s, t, dz), 0, 0, col_tile(s, t, dz, False), pushes)
                before = [("ring", s, t, dz)] if dz else [("start",) if p == 0 else ("final", p - 1, t % 2)]
                add(("split", s, t, dz, False), 2, SMALL, before)
                add(("split", s, t, dz, True), 2, SMALL, col_tile(s, t, dz, True))
        for o, target in enumerate(STREAMS[p + 1]):
            rows_used = [h for h, stream in enumerate(STREAMS[p]) if overlap(stream, (target[0], target[1], 0, 256))]
            cols_used = [t for t, col in enumerate(COLUMNS) if overlap(col, (0, 256, target[2], target[3]))]
            pieces = {key: [piece for h in rows_used
                            for piece in row_tile(p, h, 0, *key) + row_tile(p, h, 1, *key[::-1])] for key in OFFSETS}
            starts = [("start",) if p == 0 else ("final", p - 1, h) for h in rows_used]
            if p % 2 == 0 and target[0] == 0:
                need = [piece for key in OFFSETS for piece in pieces[key]] + starts
                groups = [[(dz, other) for dz in group for other in (False, True)] for group in COL_GROUPS]
                needs = [need + [("split", s, t, *key) for t in cols_used for key in group] for group in groups]
            else:
                groups = NEAR_FIRST
                need = [("split", s, t, dz, other) for t in cols_used for dz in RING for other in (False, True)]
                needs = [[piece for key in group for piece in pieces[key]] + starts + (need if p % 2 == 0 else [])
                         for group in groups]
            for n, group in enumerate(groups):
                cost = DOT + DOT_TILE * len(group) * (0.6 if target[3] == 128 else 1)
                jobs[("mac", p, o, n)] = (4 + p, cost, needs[n], [])
                GROUPS[p, o, n] = group
            pushes = []
            if p < 2 * STEPS - 1:
                pushes = own_row(p + 1, o) + (own_col(s + 1, (o, 2 + o)) if p % 2 else [])
            macs = [("mac", p, o, n) for n in range(len(groups))]
            if p % 2 == 0 and o == 2:
                add(("final", p, o), 1, 2 * SMALL, macs)
                add(("begin", p, o), 1, 0, [("final", p, o)] + [("turn", p + 1, 1, *key) for key in BEGIN], pushes)
            else:
                add(("final", p, o), 1, 2 * SMALL, macs, pushes)
    return jobs


def make_order(jobs):
    ready_at, missing, users = {}, {}, {}
    for name, (_, _, needs, _) in jobs.items():
        missing[name] = len(set(needs))
        ready_at[name] = 0.0
        for need in set(needs):
            users.setdefault(need, []).append(name)
    waiting, ready, free = [], [], {}
    rank = {name: n for n, name in enumerate(jobs)}

    def done(thing, when):
        for user in users.get(thing, ()):
            missing[user] -= 1
            ready_at[user] = max(ready_at[user], when)
            if missing[user] == 0:
                heapq.heappush(waiting, (ready_at[user], rank[user], user))

    for name in jobs:
        if missing[name] == 0:
            heapq.heappush(waiting, (0.0, rank[name], name))
    now, order, times = 0.0, [], {}
    while waiting or ready:
        if not ready and waiting[0][0] > now:
            now = waiting[0][0]
        while waiting and waiting[0][0] <= now:
            when, number, name = heapq.heappop(waiting)
            heapq.heappush(ready, (jobs[name][0], when, number, name))
        name = heapq.heappop(ready)[-1]
        _, cost, _, pushes = jobs[name]
        now += cost
        order.append(name)
        times[name] = now
        for (axis, steps), amount, piece in pushes:
            way = axis, steps > 0
            free[way] = max(free.get(way, 0.0), now) + amount * max(1, abs(steps)) * ROWS64
            done(piece, free[way] + HOP)
        done(name, now)
    return order, times


JOBS = make_jobs()
ORDER, TIMES = make_order(JOBS)
PIECES = [piece for name in JOBS for _, _, piece in JOBS[name][3]]
ROW = {name: n for n, name in enumerate(piece for piece in PIECES if piece[0] == "row")}
COL = {name: n for n, name in enumerate(piece for piece in PIECES if piece[0] == "col")}


def split(value):
    high = value.astype(bf16)
    return high, (value - high.astype(f32)).astype(bf16)


def kernel(pattern_in, density, out, rows, cols, col_hi, col_lo, acc, pattern,
           row_send, row_recv, col_send, col_recv, local_sem):
    size = density.shape[0]
    r, c = lax.axis_index("row"), lax.axis_index("col")
    z, core = r // 2, r % 2
    y, x = c // NX, c % NX

    def device(dx=0, dy=0, dz=0):
        return (((z + dz + NZ) % NZ) * 2 + core, ((y + dy + NY) % NY) * NX + (x + dx + NX) % NX)

    sibling = (z * 2 + 1 - core, c)

    def k_row(dx, dy):
        return ((y - dy + NY) % NY) * NX + (x - dx + NX) % NX

    def k_col(dz, other):
        return ((z - dz + NZ) % NZ) * 2 + (1 - core if other else core)

    fetch = [
        pltpu.make_async_copy(density, rows.at[0, c], local_sem.at[0]),
        pltpu.make_async_copy(density, cols.at[0, r], local_sem.at[1]),
        pltpu.make_async_copy(pattern_in, pattern, local_sem.at[2]),
    ]
    for copy in fetch:
        copy.start()

    peers = [device(dx=1), device(dx=-1), device(dy=1), device(dy=-1), sibling]
    peers += [device(dz=step) for step in (1, -1)]
    barrier = pltpu.get_barrier_semaphore()
    for peer in peers:
        pl.semaphore_signal(barrier, inc=1, device_id=peer, device_id_type=MESH)
    pl.semaphore_wait(barrier, len(peers))
    for copy in fetch:
        copy.wait()

    mask = [[pattern[a, b].astype(f32) for b in range(2)] for a in range(2)]

    def masked(value, low, lane):
        parts = [value[:, n:n + BLOCK] * mask[low // BLOCK][(lane + n) // BLOCK] for n in range(0, value.shape[1], BLOCK)]
        return jnp.concatenate(parts, axis=1)

    def copy_of(piece):
        if piece[0] == "row":
            _, p, h, plan, a, b, _ = piece
            low, count, lane, lanes = STREAMS[p][h]
            here = pl.ds(low + plan * (count // 2), count // 2), pl.ds(lane, lanes)
            return rows, p, here, row_send.at[p], row_recv.at[ROW[piece]], (a, b) if plan == 0 else (b, a)
        _, s, t, dz, part = piece
        low, count, lane, lanes = COLUMNS[t]
        if part in ("q0", "q1"):
            count //= 2
            low += count if part == "q1" else 0
        here = pl.ds(low, count), pl.ds(lane, lanes)
        return cols, s, here, col_send.at[s], col_recv.at[COL[piece]], dz

    def push(where, piece):
        buffer, index, here, send, recv, offset = copy_of(piece)
        axis, sign = where
        if piece[0] == "row":
            dx, dy = offset
            held = k_row(dx - sign, dy) if axis == "x" else k_row(dx, dy - sign)
        else:
            held = k_col(offset if axis == "core" else offset - sign, False)
        target = sibling if axis == "core" else device(**{"d" + axis: sign})
        part = buffer.at[index, held, *here]
        pltpu.make_async_remote_copy(
            src_ref=part, dst_ref=part, send_sem=send, recv_sem=recv,
            device_id=target, device_id_type=MESH).start()

    def wait(piece):
        buffer, index, here, send, recv, offset = copy_of(piece)
        if piece[0] == "row":
            held = k_row(*offset)
        else:
            held = k_col(offset, piece[-1] == "s")
        part = buffer.at[index, held, *here]
        pltpu.make_async_remote_copy(
            src_ref=part, dst_ref=part, send_sem=send, recv_sem=recv,
            device_id=sibling, device_id_type=MESH).wait_recv()

    waited, begun = set(), set()

    def run(name):
        _, _, needs, pushes = JOBS[name]
        for need in needs:
            if need[0] in ("row", "col") and need not in waited:
                waited.add(need)
                wait(need)
        kind = name[0]
        if kind == "split":
            _, s, t, dz, other = name
            k = k_col(dz, other)
            here = pl.ds(*COLUMNS[t][:2]), pl.ds(*COLUMNS[t][2:])
            high, low = split(cols[s, k, *here])
            col_hi[s, k, *here] = high
            col_lo[s, k, *here] = low
        elif kind == "mac":
            _, p, o = name[:3]
            low, count, lane, lanes = STREAMS[p + 1][o]
            here, wide = pl.ds(low, count), pl.ds(lane, lanes)
            keys = GROUPS[name[1:]]
            places = [k_col(*key) if isinstance(key[1], bool) else k_row(*key) for key in keys]
            high_a, low_a = split(jnp.concatenate([rows[p, k, here, :] for k in places], axis=1))
            high_b = jnp.concatenate([col_hi[p // 2, k, :, wide] for k in places], axis=0)
            low_b = jnp.concatenate([col_lo[p // 2, k, :, wide] for k in places], axis=0)
            both = jnp.dot(jnp.concatenate([high_a, low_a], axis=0), high_b, preferred_element_type=f32)
            term = both[:count] + both[count:] + jnp.dot(high_a, low_b, preferred_element_type=f32)
            if (p, o) in begun:
                acc[p, here, wide] += term
            else:
                begun.add((p, o))
                acc[p, here, wide] = term
        elif kind == "final":
            _, p, o = name
            low, count, lane, lanes = STREAMS[p + 1][o]
            here, wide = pl.ds(low, count), pl.ds(lane, lanes)
            value = masked(acc[p, here, wide], low, lane)
            if p % 2:
                value = 3.0 * rows[p, c, here, wide] - 2.0 * value
            if p == 2 * STEPS - 1:
                out[here, wide] = value
            else:
                rows[p + 1, c, here, wide] = value
                if p % 2:
                    cols[p // 2 + 1, r, here, wide] = value
        for where, _, piece in pushes:
            push(where, piece)

    for name in ORDER:
        run(name)

    for p in range(2 * STEPS):
        whole = rows.at[p, pl.ds(0, 15)]
        pltpu.make_async_copy(whole, whole, row_send.at[p]).wait()
    for s in range(STEPS):
        whole = cols.at[s, pl.ds(0, 15)]
        pltpu.make_async_copy(whole, whole, col_send.at[s]).wait()


def local(density, pattern):
    size = density.shape[0]
    tiles = NX * NY
    return pl.pallas_call(
        kernel,
        out_shape=jax.ShapeDtypeStruct(density.shape, f32),
        in_specs=[pl.BlockSpec(memory_space=pltpu.HBM), pl.BlockSpec(memory_space=pltpu.HBM)],
        out_specs=pl.BlockSpec(memory_space=pltpu.VMEM),
        scratch_shapes=[
            pltpu.VMEM((2 * STEPS, tiles, size, size), f32),
            pltpu.VMEM((STEPS, tiles, size, size), f32),
            pltpu.VMEM((STEPS, tiles, size, size), bf16),
            pltpu.VMEM((STEPS, tiles, size, size), bf16),
            pltpu.VMEM((2 * STEPS, size, size), f32),
            pltpu.SMEM(pattern.shape, jnp.int32),
            pltpu.SemaphoreType.DMA((2 * STEPS,)),
            pltpu.SemaphoreType.DMA((len(ROW),)),
            pltpu.SemaphoreType.DMA((STEPS,)),
            pltpu.SemaphoreType.DMA((len(COL),)),
            pltpu.SemaphoreType.DMA((3,)),
        ],
        compiler_params=pltpu.CompilerParams(
            collective_id=0, has_side_effects=True, vmem_limit_bytes=56 * 1024 * 1024),
    )(pattern, density)


def solution(mesh):
    placed = P("row", "col")
    return jax.shard_map(local, mesh=mesh, in_specs=(placed, placed), out_specs=placed, check_vma=False)
```

```python
import heapq

import jax
import jax.numpy as jnp
from jax import lax
from jax.experimental import pallas as pl
from jax.experimental.pallas import tpu as pltpu
from jax.sharding import PartitionSpec as P

BLOCK = 128
STEPS = 2
NX, NY, NZ = 4, 4, 8
MESH = pl.DeviceIdType.MESH
f32, bf16 = jnp.float32, jnp.bfloat16
OFFSETS = [(dx, dy) for dx in (0, 1, -1, 2) for dy in (0, 1, -1, 2)]
RING = (0, 1, -1, 2, -2, 3, -3, 4)

GROUPS = {}
BEGIN_ROWS = [(0, "g1"), (1, "g1")]
COL_SIZE = 1.0
BEGIN_COLS = ()
BEGIN = [(0, "g1"), (1, "g1")]

ROWS64, HOP, SMALL, DOT, DOT_TILE = 1.5, 1.8, 0.03, 0.15, 0.12
NEAR_FIRST = [
    [(0, 0), (1, 0), (-1, 0), (0, 1), (0, -1)],
    [(2, 0), (0, 2), (1, 1), (1, -1), (-1, 1), (-1, -1)],
    [(1, 2), (-1, 2), (2, 1), (2, -1)],
    [(2, 2)],
]
COL_GROUPS = [[0], [1, -1], [2, -2], [3, -3], [4]]


HALVES = [(0, 128, 0, 256), (128, 128, 0, 256)]
SQUARE = [(0, 128, 0, 128), (0, 128, 128, 128), (128, 128, 0, 256)]
STREAMS = [HALVES, SQUARE, HALVES, SQUARE, HALVES]
COLUMNS = [(0, 128, 0, 128), (128, 128, 0, 128), (0, 128, 128, 128), (128, 128, 128, 128)]
SLOTS = (0, 1, -1, 2)
SETS = [((0, 1), (1, 2), (3, 1)), ((0, 1), (1, 3))]
SET_CHOICE = [[0, 0], [0, 0, 0], [0, 0], [0, 0, 0]]
FAR = [(0, 1, 0), (0, 1)]


def sets_of(p, h):
    return SETS[SET_CHOICE[p][h]]


def far_sign(p, h, plan, group=None):
    turn = 0 if group is None else FAR[SET_CHOICE[p][h]][group]
    return 1 if (h + plan + turn) % 2 == 0 else -1


def group_of(p, h, a):
    slot = SLOTS.index(a)
    return next(n for n, (first, count) in enumerate(sets_of(p, h)) if first <= slot < first + count)


def row_tile(p, h, plan, a, b):
    if (a, b) == (0, 0):
        return []
    return [("row", p, h, plan, a if b == 0 else "g%d" % group_of(p, h, a), b)]


def col_tile(s, t, dz, other):
    if other:
        return [("col", s, t, dz, "s")]
    if dz == 0:
        return []
    return [("col", s, t, dz, part) for part in (("q0", "q1") if dz == 4 else ("h",))]


def make_jobs():
    jobs = {}

    def link(plan, axis, sign):
        return ("x" if (axis == 0) == (plan == 0) else "y", sign)

    def row_size(p, h):
        return STREAMS[p][h][1] * STREAMS[p][h][3] / (128 * 256)

    def own_row(p, h):
        pushes = []
        for axis in (0, 1):
            for plan in (0, 1):
                for sign in (1, -1):
                    a, b = (sign, 0) if axis == 0 else ("g0", sign)
                    pushes.append((link(plan, axis, sign), row_size(p, h), ("row", p, h, plan, a, b)))
        return pushes

    def own_col(s, ts):
        pushes = []
        for t in ts:
            pushes += [(("z", step), COL_SIZE, ("col", s, t, step, "h")) for step in (1, -1)]
        return pushes + [(("core", 0), 0.15, ("col", s, t, 0, "s")) for t in ts]

    def overlap(one, other):
        return all(one[i] < other[i] + other[i + 1] and other[i] < one[i] + one[i + 1] for i in (0, 2))

    def add(name, priority, cost, needs, pushes=()):
        jobs[name] = (priority, cost + SMALL * (len(pushes) + len(needs)), needs, list(pushes))

    add(("start",), 0, SMALL, [], own_row(0, 0) + own_col(0, (0, 1)))
    add(("begin", 0, 1), 0, 0, [("turn", 0, 0, *key) for key in BEGIN_ROWS], own_row(0, 1))
    add(("begin_col",), 0, 0, [("ring", 0, t, dz) for t in (0, 1) for dz in BEGIN_COLS], own_col(0, (2, 3)))
    for p in range(2 * STEPS):
        s = p // 2
        for h, stream in enumerate(STREAMS[p]):
            size = row_size(p, h)
            for plan in (0, 1):
                for sign in (1, -1):
                    pushes = []
                    if sign == far_sign(p, h, plan):
                        pushes = [(link(plan, 0, sign), size, ("row", p, h, plan, 2, 0))]
                        add(("turn", p, h, plan, sign), 0, 0, row_tile(p, h, plan, sign, 0), pushes)
                for g, (first, count) in enumerate(sets_of(p, h)):
                    if g:
                        needs = [piece for a in SLOTS[first:first + count] for piece in row_tile(p, h, plan, a, 0)]
                        add(("turn", p, h, plan, "g%d" % g), 0, 0, needs, [
                            (link(plan, 1, turn), size * count, ("row", p, h, plan, "g%d" % g, turn)) for turn in (1, -1)])
                    sign = far_sign(p, h, plan, g)
                    add(("pass", p, h, plan, "g%d" % g), 0, 0, [("row", p, h, plan, "g%d" % g, sign)],
                        [(link(plan, 1, sign), size * count, ("row", p, h, plan, "g%d" % g, 2))])
        if p % 2 == 0:
            for t, dz in ((t, dz) for dz in RING for t in range(4)):
                pushes = []
                if dz:
                    sign = 1 if dz > 0 else -1
                    if abs(dz) < 3:
                        pushes.append((("z", sign), COL_SIZE, ("col", s, t, dz + sign, "h")))
                    elif dz != 4:
                        pushes.append((("z", sign), COL_SIZE / 2, ("col", s, t, 4, "q0" if sign == 1 else "q1")))
                    pushes.append((("core", 0), 0.15, ("col", s, t, dz, "s")))
                    add(("ring", s, t, dz), 0, 0, col_tile(s, t, dz, False), pushes)
                before = [("ring", s, t, dz)] if dz else [("start",) if p == 0 else ("final", p - 1, t % 2)]
                add(("split", s, t, dz, False), 2, SMALL, before)
                add(("split", s, t, dz, True), 2, SMALL, col_tile(s, t, dz, True))
        for o, target in enumerate(STREAMS[p + 1]):
            rows_used = [h for h, stream in enumerate(STREAMS[p]) if overlap(stream, (target[0], target[1], 0, 256))]
            cols_used = [t for t, col in enumerate(COLUMNS) if overlap(col, (0, 256, target[2], target[3]))]
            pieces = {key: [piece for h in rows_used
                            for piece in row_tile(p, h, 0, *key) + row_tile(p, h, 1, *key[::-1])] for key in OFFSETS}
            starts = [("start",) if p == 0 else ("final", p - 1, h) for h in rows_used]
            if p % 2 == 0 and target[0] == 0:
                need = [piece for key in OFFSETS for piece in pieces[key]] + starts
                groups = [[(dz, other) for dz in group for other in (False, True)] for group in COL_GROUPS]
                needs = [need + [("split", s, t, *key) for t in cols_used for key in group] for group in groups]
            else:
                groups = NEAR_FIRST
                need = [("split", s, t, dz, other) for t in cols_used for dz in RING for other in (False, True)]
                needs = [[piece for key in group for piece in pieces[key]] + starts + (need if p % 2 == 0 else [])
                         for group in groups]
            for n, group in enumerate(groups):
                cost = DOT + DOT_TILE * len(group) * (0.6 if target[3] == 128 else 1)
                jobs[("mac", p, o, n)] = (4 + p, cost, needs[n], [])
                GROUPS[p, o, n] = group
            pushes = []
            if p < 2 * STEPS - 1:
                pushes = own_row(p + 1, o) + (own_col(s + 1, (o, 2 + o)) if p % 2 else [])
            macs = [("mac", p, o, n) for n in range(len(groups))]
            if p % 2 == 0 and o == 2:
                add(("final", p, o), 1, 2 * SMALL, macs)
                add(("begin", p, o), 1, 0, [("final", p, o)] + [("turn", p + 1, 1, *key) for key in BEGIN], pushes)
            else:
                add(("final", p, o), 1, 2 * SMALL, macs, pushes)
    return jobs


def make_order(jobs):
    ready_at, missing, users = {}, {}, {}
    for name, (_, _, needs, _) in jobs.items():
        missing[name] = len(set(needs))
        ready_at[name] = 0.0
        for need in set(needs):
            users.setdefault(need, []).append(name)
    waiting, ready, free = [], [], {}
    rank = {name: n for n, name in enumerate(jobs)}

    def done(thing, when):
        for user in users.get(thing, ()):
            missing[user] -= 1
            ready_at[user] = max(ready_at[user], when)
            if missing[user] == 0:
                heapq.heappush(waiting, (ready_at[user], rank[user], user))

    for name in jobs:
        if missing[name] == 0:
            heapq.heappush(waiting, (0.0, rank[name], name))
    now, order, times = 0.0, [], {}
    while waiting or ready:
        if not ready and waiting[0][0] > now:
            now = waiting[0][0]
        while waiting and waiting[0][0] <= now:
            when, number, name = heapq.heappop(waiting)
            heapq.heappush(ready, (jobs[name][0], when, number, name))
        name = heapq.heappop(ready)[-1]
        _, cost, _, pushes = jobs[name]
        now += cost
        order.append(name)
        times[name] = now
        for (axis, steps), amount, piece in pushes:
            way = axis, steps > 0
            free[way] = max(free.get(way, 0.0), now) + amount * max(1, abs(steps)) * ROWS64
            done(piece, free[way] + HOP)
        done(name, now)
    return order, times


JOBS = make_jobs()
ORDER, TIMES = make_order(JOBS)
PIECES = [piece for name in JOBS for _, _, piece in JOBS[name][3]]
ROW = {name: n for n, name in enumerate(piece for piece in PIECES if piece[0] == "row")}
COL = {name: n for n, name in enumerate(piece for piece in PIECES if piece[0] == "col")}


def split(value):
    high = value.astype(bf16)
    return high, (value - high.astype(f32)).astype(bf16)


def kernel(pattern_in, density, out, wide_rows, half_rows, cols, col_hi, col_lo, acc, pattern,
           row_send, row_recv, col_send, col_recv, local_sem):
    size = density.shape[0]
    r, c = lax.axis_index("row"), lax.axis_index("col")
    z, core = r // 2, r % 2
    y, x = c // NX, c % NX

    def device(dx=0, dy=0, dz=0):
        return (((z + dz + NZ) % NZ) * 2 + core, ((y + dy + NY) % NY) * NX + (x + dx + NX) % NX)

    sibling = (z * 2 + 1 - core, c)

    def k_row(dx, dy):
        return ((y - dy + NY) % NY) * NX + (x - dx + NX) % NX

    def k_col(dz, other):
        return ((z - dz + NZ) % NZ) * 2 + (1 - core if other else core)

    def stream_of(p, h):
        before = [h_ for p_ in range(4) for h_, other in enumerate(STREAMS[p_])
                  if (p_, h_) < (p, h) and other[3] == STREAMS[p][h][3]]
        return (wide_rows if STREAMS[p][h][3] == size else half_rows).at[len(before)]

    step_rows = HALVES[0][1] // 2
    fetch = [
        pltpu.make_async_copy(density.at[pl.ds((2 * h + plan) * step_rows, step_rows)], stream_of(0, h).at[plan, 0, 0],
                              local_sem.at[2 * h + plan])
        for h in (0, 1) for plan in (0, 1)]
    fetch += [
        pltpu.make_async_copy(density, cols.at[0, r], local_sem.at[4]),
        pltpu.make_async_copy(pattern_in, pattern, local_sem.at[5]),
    ]
    for copy in fetch:
        copy.start()

    peers = [device(dx=1), device(dx=-1), device(dy=1), device(dy=-1), sibling]
    peers += [device(dz=step) for step in (1, -1)]
    barrier = pltpu.get_barrier_semaphore()
    for peer in peers:
        pl.semaphore_signal(barrier, inc=1, device_id=peer, device_id_type=MESH)
    pl.semaphore_wait(barrier, len(peers))
    for copy in fetch:
        copy.wait()

    mask = [[pattern[a, b].astype(f32) for b in range(2)] for a in range(2)]

    def masked(value, low, lane):
        parts = [value[:, n:n + BLOCK] * mask[low // BLOCK][(lane + n) // BLOCK] for n in range(0, value.shape[1], BLOCK)]
        return jnp.concatenate(parts, axis=1)

    def slot_of(distance):
        return distance + distance // 2 - 2 * (distance // 3)

    def gathered(p, low, dx, dy):
        parts = []
        for h, stream in enumerate(STREAMS[p]):
            if stream[0] == low:
                ref = stream_of(p, h)
                parts.append(jnp.concatenate([ref[0, slot_of(dy), slot_of(dx)], ref[1, slot_of(dx), slot_of(dy)]], axis=0))
        return parts[0] if len(parts) == 1 else jnp.concatenate(parts, axis=1)

    def remote(src, dst, send, recv, target):
        return pltpu.make_async_remote_copy(
            src_ref=src, dst_ref=dst, send_sem=send, recv_sem=recv, device_id=target, device_id_type=MESH)

    def row_copy(piece, where):
        _, p, h, plan, a, b = piece
        ref = stream_of(p, h).at[plan]
        moved = a if b == 0 else b
        held = SLOTS.index(0 if abs(moved) == 1 else where[1]) if where else SLOTS.index(moved)
        if b == 0:
            src, dst = ref.at[0, held], ref.at[0, SLOTS.index(a)]
        else:
            first, count = sets_of(p, h)[int(a[1])]
            src, dst = ref.at[held, pl.ds(first, count)], ref.at[SLOTS.index(b), pl.ds(first, count)]
        target = device(**{"d" + where[0]: where[1]}) if where else sibling
        return remote(src, dst, row_send.at[p], row_recv.at[ROW[piece]], target)

    def col_copy(piece, where):
        _, s, t, dz, part = piece
        low, count, lane, lanes = COLUMNS[t]
        if part in ("q0", "q1"):
            count //= 2
            low += count if part == "q1" else 0
        if not where:
            held, target = k_col(dz, part == "s"), sibling
        elif where[0] == "core":
            held, target = k_col(dz, False), sibling
        else:
            held, target = k_col(dz - where[1], False), device(dz=where[1])
        ref = cols.at[s, held, pl.ds(low, count), pl.ds(lane, lanes)]
        return remote(ref, ref, col_send.at[s], col_recv.at[COL[piece]], target)

    def copy_of(piece, where=None):
        return (row_copy if piece[0] == "row" else col_copy)(piece, where)

    waited, begun = set(), set()

    def run(name):
        _, _, needs, pushes = JOBS[name]
        for need in needs:
            if need[0] in ("row", "col") and need not in waited:
                waited.add(need)
                copy_of(need).wait_recv()
        kind = name[0]
        if kind == "split":
            _, s, t, dz, other = name
            k = k_col(dz, other)
            here = pl.ds(*COLUMNS[t][:2]), pl.ds(*COLUMNS[t][2:])
            high, low = split(cols[s, k, *here])
            col_hi[s, k, *here] = high
            col_lo[s, k, *here] = low
        elif kind == "mac":
            _, p, o = name[:3]
            low, count, lane, lanes = STREAMS[p + 1][o]
            here, wide = pl.ds(low, count), pl.ds(lane, lanes)
            keys = GROUPS[name[1:]]
            if isinstance(keys[0][1], bool):
                places = [k_col(*key) for key in keys]
                steps = [((x - k % NX + NX) % NX, (y - k // NX + NY) % NY) for k in places]
            else:
                places = [k_row(*key) for key in keys]
                steps = [(dx % NX, dy % NY) for dx, dy in keys]
            high_a, low_a = split(jnp.concatenate([gathered(p, low, *step) for step in steps], axis=1))
            high_b = jnp.concatenate([col_hi[p // 2, k, :, wide] for k in places], axis=0)
            low_b = jnp.concatenate([col_lo[p // 2, k, :, wide] for k in places], axis=0)
            both = jnp.dot(jnp.concatenate([high_a, low_a], axis=0), high_b, preferred_element_type=f32)
            term = both[:count] + both[count:] + jnp.dot(high_a, low_b, preferred_element_type=f32)
            if (p, o) in begun:
                acc[p, here, wide] += term
            else:
                begun.add((p, o))
                acc[p, here, wide] = term
        elif kind == "final":
            _, p, o = name
            low, count, lane, lanes = STREAMS[p + 1][o]
            here, wide = pl.ds(low, count), pl.ds(lane, lanes)
            value = masked(acc[p, here, wide], low, lane)
            if p % 2:
                value = 3.0 * gathered(p, low, 0, 0) - 2.0 * value
            if p == 2 * STEPS - 1:
                out[here, wide] = value
            else:
                ref = stream_of(p + 1, o)
                ref[0, 0, 0] = value[:count // 2]
                ref[1, 0, 0] = value[count // 2:]
                if p % 2:
                    cols[p // 2 + 1, r, here, wide] = value
        for where, _, piece in pushes:
            copy_of(piece, where).start()

    for name in ORDER:
        run(name)

    def sent(ref, sem):
        pltpu.make_async_copy(ref, ref, sem).wait()

    for p in range(2 * STEPS):
        sent(cols.at[0, pl.ds(0, 15)], row_send.at[p])
    for s in range(STEPS):
        sent(cols.at[s, pl.ds(0, 15)], col_send.at[s])


def local(density, pattern):
    size = density.shape[0]
    tiles = NX * NY
    return pl.pallas_call(
        kernel,
        out_shape=jax.ShapeDtypeStruct(density.shape, f32),
        in_specs=[pl.BlockSpec(memory_space=pltpu.HBM), pl.BlockSpec(memory_space=pltpu.HBM)],
        out_specs=pl.BlockSpec(memory_space=pltpu.VMEM),
        scratch_shapes=[
            pltpu.VMEM((3 * STEPS, 2, NY, NX, size // 4, size), f32),
            pltpu.VMEM((2 * STEPS, 2, NY, NX, size // 4, size // 2), f32),
            pltpu.VMEM((STEPS, tiles, size, size), f32),
            pltpu.VMEM((STEPS, tiles, size, size), bf16),
            pltpu.VMEM((STEPS, tiles, size, size), bf16),
            pltpu.VMEM((2 * STEPS, size, size), f32),
            pltpu.SMEM(pattern.shape, jnp.int32),
            pltpu.SemaphoreType.DMA((2 * STEPS,)),
            pltpu.SemaphoreType.DMA((len(ROW),)),
            pltpu.SemaphoreType.DMA((STEPS,)),
            pltpu.SemaphoreType.DMA((len(COL),)),
            pltpu.SemaphoreType.DMA((6,)),
        ],
        compiler_params=pltpu.CompilerParams(
            collective_id=0, has_side_effects=True, vmem_limit_bytes=56 * 1024 * 1024),
    )(pattern, density)


def solution(mesh):
    placed = P("row", "col")
    return jax.shard_map(local, mesh=mesh, in_specs=(placed, placed), out_specs=placed, check_vma=False)
```

```python
import heapq

import jax
import jax.numpy as jnp
from jax import lax
from jax.experimental import pallas as pl
from jax.experimental.pallas import tpu as pltpu
from jax.sharding import PartitionSpec as P

BLOCK = 128
STEPS = 2
NX, NY, NZ = 4, 4, 8
MESH = pl.DeviceIdType.MESH
f32, bf16 = jnp.float32, jnp.bfloat16
OFFSETS = [(dx, dy) for dx in (0, 1, -1, 2) for dy in (0, 1, -1, 2)]
RING = (0, 1, -1, 2, -2, 3, -3, 4)

GROUPS = {}
BEGIN_ROWS = [(0, "g1"), (1, "g1")]
COL_SIZE = 1.0
BEGIN_COLS = ()
BEGIN = [(0, "g1"), (1, "g1")]

ROWS64, HOP, SMALL, DOT, DOT_TILE = 1.6, 1.7, 0.015, 0.08, 0.06
NEAR_FIRST = [
    [(0, 0), (1, 0), (-1, 0), (0, 1), (0, -1)],
    [(2, 0), (0, 2), (1, 1), (1, -1), (-1, 1), (-1, -1)],
    [(1, 2), (-1, 2), (2, 1), (2, -1)],
    [(2, 2)],
]
COL_GROUPS = [[0], [1, -1], [2, -2], [3, -3], [4]]


HALVES = [(0, 128, 0, 256), (128, 128, 0, 256)]
SQUARE = [(0, 128, 0, 128), (0, 128, 128, 128), (128, 128, 0, 256)]
STREAMS = [HALVES, SQUARE, HALVES, SQUARE, HALVES]
COLUMNS = [(0, 128, 0, 128), (128, 128, 0, 128), (0, 128, 128, 128), (128, 128, 128, 128)]
SLOTS = (0, 1, -1, 2)
SETS = [((0, 1), (1, 2), (3, 1)), ((0, 1), (1, 3))]
SET_CHOICE = [[0, 0], [0, 0, 0], [0, 0], [0, 0, 0]]
FAR = [(0, 1, 0), (0, 1)]


PAIRED = 2 * STEPS - 1
CHUNKS = 2
COLUMN_PARTS = [(0, 2), (1, 3)]
PAIR_GROUPS = [[(0, 0), (0, 1), (0, -1), (1, 0)], [(0, 2), (1, 1), (1, -1)], [(1, 2)]]
PAIR_OFFSETS = [key for group in PAIR_GROUPS for key in group]
MOVE_AFTER = [(0, "g2"), (1, "g2")]
OWN_AFTER = []
WAITED = ("row", "col", "pair", "part")


def sets_of(p, h):
    return SETS[SET_CHOICE[p][h]]


def far_sign(p, h, plan, group=None):
    turn = 0 if group is None else FAR[SET_CHOICE[p][h]][group]
    return 1 if (h + plan + turn) % 2 == 0 else -1


def group_of(p, h, a):
    slot = SLOTS.index(a)
    return next(n for n, (first, count) in enumerate(sets_of(p, h)) if first <= slot < first + count)


def row_tile(p, h, plan, a, b):
    if (a, b) == (0, 0):
        return []
    return [("row", p, h, plan, a if b == 0 else "g%d" % group_of(p, h, a), b)]


def pair_tile(h, plan, dx, dy):
    if (dx, dy) == (0, 0):
        return []
    name = "near" if plan == 0 and dx == 1 and abs(dy) == 1 else dy
    return [("pair", h, plan, dx, name)]


def col_tile(s, t, dz, other):
    if other:
        return [("col", s, t, dz, "s")]
    if dz == 0:
        return []
    return [("col", s, t, dz, part) for part in (("q0", "q1") if dz == 4 else ("h",))]


def make_jobs():
    jobs = {}

    def link(plan, axis, sign):
        return ("x" if (axis == 0) == (plan == 0) else "y", sign)

    def row_size(p, h):
        return STREAMS[p][h][1] * STREAMS[p][h][3] / (128 * 256)

    def own_row(p, h):
        pushes = []
        if p == PAIRED:
            size = row_size(p, h)
            pushes = [(("pair", 1), size, ("pair", h, 1, 1, 0))]
            pushes += [(("y", sign), size, ("pair", h, 0, 0, sign)) for sign in (1, -1)]
            pushes += [(("pair", 1), size, ("pair", h, 0, 1, 0))]
            return pushes + [(("y", sign), size, ("pair", h, 1, 0, sign)) for sign in (1, -1)]
        for axis in (0, 1):
            for plan in (0, 1):
                for sign in (1, -1):
                    a, b = (sign, 0) if axis == 0 else ("g0", sign)
                    pushes.append((link(plan, axis, sign), row_size(p, h), ("row", p, h, plan, a, b)))
        return pushes

    def own_col(s, ts):
        pushes = []
        for t in ts:
            pushes += [(("z", step), COL_SIZE, ("col", s, t, step, "h")) for step in (1, -1)]
        return pushes + [(("core", 0), 0.15, ("col", s, t, 0, "s")) for t in ts]

    def overlap(one, other):
        return all(one[i] < other[i] + other[i + 1] and other[i] < one[i] + one[i + 1] for i in (0, 2))

    def add(name, priority, cost, needs, pushes=()):
        jobs[name] = (priority, cost + SMALL * (len(pushes) + len(needs)), needs, list(pushes))

    add(("start",), 0, SMALL, [], own_row(0, 0) + own_col(0, (0, 1)))
    add(("begin", 0, 1), 0, 0, [("turn", 0, 0, *key) for key in BEGIN_ROWS], own_row(0, 1))
    add(("begin_col",), 0, 0, [("ring", 0, t, dz) for t in (0, 1) for dz in BEGIN_COLS], own_col(0, (2, 3)))
    for p in range(2 * STEPS):
        s = p // 2
        for h, stream in enumerate(STREAMS[p]):
            size = row_size(p, h)
            for plan in (0, 1) if p != PAIRED else ():
                for sign in (1, -1):
                    pushes = []
                    if sign == far_sign(p, h, plan):
                        pushes = [(link(plan, 0, sign), size, ("row", p, h, plan, 2, 0))]
                        add(("turn", p, h, plan, sign), 0, 0, row_tile(p, h, plan, sign, 0), pushes)
                for g, (first, count) in enumerate(sets_of(p, h)):
                    if g:
                        needs = [piece for a in SLOTS[first:first + count] for piece in row_tile(p, h, plan, a, 0)]
                        add(("turn", p, h, plan, "g%d" % g), 0, 0, needs, [
                            (link(plan, 1, turn), size * count, ("row", p, h, plan, "g%d" % g, turn)) for turn in (1, -1)])
                    sign = far_sign(p, h, plan, g)
                    add(("pass", p, h, plan, "g%d" % g), 0, 0, [("row", p, h, plan, "g%d" % g, sign)],
                        [(link(plan, 1, sign), size * count, ("row", p, h, plan, "g%d" % g, 2))])
            if p == PAIRED:
                turn = far_sign(p, h, 0)
                add(("pass", p, h, 0, 0), 0, 0, pair_tile(h, 0, 0, turn), [(("y", turn), size, ("pair", h, 0, 0, 2))])
                add(("turn", p, h, 0, "g1"), 0, 0, pair_tile(h, 0, 0, 1) + pair_tile(h, 0, 0, -1),
                    [(("pair", 1), 2 * size, ("pair", h, 0, 1, "near"))])
                add(("turn", p, h, 0, "g2"), 0, 0, pair_tile(h, 0, 0, 2), [(("pair", 1), size, ("pair", h, 0, 1, 2))])
                add(("turn", p, h, 1, "g1"), 0, 0, pair_tile(h, 1, 1, 0),
                    [(("y", sign), size, ("pair", h, 1, 1, sign)) for sign in (1, -1)])
                for dx in (0, 1):
                    turn = far_sign(p, h, 1) * (1 - 2 * dx)
                    add(("pass", p, h, 1, dx), 0, 0, pair_tile(h, 1, dx, turn), [(("y", turn), size, ("pair", h, 1, dx, 2))])
        if p == PAIRED - 1:
            for e in range(CHUNKS):
                size = 4.0 / CHUNKS
                begun = ("final", p - 1, e)
                add(("move", e), 1.5, SMALL, [begun] + [("turn", p, 1, *key) for key in MOVE_AFTER],
                    [(("mate", 1), size / 2, ("moved", e))])
                add(("own", e), 0, SMALL, [begun, ("moved", e)] + [("ring", s, t, dz) for t, dz in OWN_AFTER], [
                    (("z", 1), size, ("e", e, 0)), (("z", -1), size, ("e", e, 1)), (("core", 0), 0.15 * size, ("shared", e, 3))])
                near = [("ring", s, t, dz) for t in COLUMN_PARTS[e] for dz in (3, -3, 4)]
                add(("lend", e), 1.5, SMALL, near, [(("mate", 1), size / (n - 1), ("lent", e, n)) for n in (2, 3)])
                for n in range(4):
                    came = ("e" if n < 2 else "lent", e, n)
                    if n < 2:
                        pushes = [(("z", 1 - 2 * n), size / 2, ("e2", e, n)), (("core", 0), 0.15 * size, ("shared", e, n))]
                    else:
                        pushes = [(("core", 0), 0.15 * size, ("shared", e, n))] if n == 2 else []
                    add(("slot", e, n), 0, SMALL, [came], pushes)
                    after = [("slot", e, n)] + ([("own", e)] if n == 3 else [])
                    add(("esplit", e, n, False), 2, 2 * SMALL, after)
                    add(("esplit", e, n, True), 2, 2 * SMALL, [("shared", e, n)] + after)
        if p % 2 == 0:
            for t, dz in ((t, dz) for dz in RING for t in range(4)):
                pushes = []
                if dz:
                    sign = 1 if dz > 0 else -1
                    if abs(dz) < 3:
                        pushes.append((("z", sign), COL_SIZE, ("col", s, t, dz + sign, "h")))
                    elif dz != 4:
                        pushes.append((("z", sign), COL_SIZE / 2, ("col", s, t, 4, "q0" if sign == 1 else "q1")))
                    pushes.append((("core", 0), 0.15, ("col", s, t, dz, "s")))
                    add(("ring", s, t, dz), 0, 0, col_tile(s, t, dz, False), pushes)
                before = [("ring", s, t, dz)] if dz else [("start",) if p == 0 else ("final", p - 1, t % 2)]
                add(("split", s, t, dz, False), 2, SMALL, before)
                add(("split", s, t, dz, True), 2, SMALL, col_tile(s, t, dz, True))
        for o, target in enumerate(STREAMS[p + 1]):
            rows_used = [h for h, stream in enumerate(STREAMS[p]) if overlap(stream, (target[0], target[1], 0, 256))]
            cols_used = [t for t, col in enumerate(COLUMNS) if overlap(col, (0, 256, target[2], target[3]))]
            if p == PAIRED:
                pieces = {key: [piece for h in rows_used for plan in (0, 1) for piece in pair_tile(h, plan, *key)]
                          for key in PAIR_OFFSETS}
            else:
                pieces = {key: [piece for h in rows_used
                                for piece in row_tile(p, h, 0, *key) + row_tile(p, h, 1, *key[::-1])] for key in OFFSETS}
            starts = [("start",) if p == 0 else ("final", p - 1, h) for h in rows_used]
            if p % 2 == 0 and target[0] == 0:
                need = [piece for key in OFFSETS for piece in pieces[key]] + starts
                groups = [[(dz, other) for dz in group for other in (False, True)] for group in COL_GROUPS]
                needs = [need + [("split", s, t, *key) for t in cols_used for key in group] for group in groups]
            else:
                groups = PAIR_GROUPS if p == PAIRED else NEAR_FIRST
                need = [("split", s, t, dz, other) for t in cols_used for dz in RING for other in (False, True)]
                needs = [[piece for key in group for piece in pieces[key]] + starts + (need if p % 2 == 0 else [])
                         for group in groups]
            for n, group in enumerate(groups):
                cost = DOT + DOT_TILE * len(group) * (0.6 if target[3] == 128 else 1)
                jobs[("mac", p, o, n)] = (4 + p, cost, needs[n], [])
                GROUPS[p, o, n] = group
            pushes = []
            if p < 2 * STEPS - 1:
                pushes = own_row(p + 1, o) + (own_col(s + 1, (o, 2 + o)) if p % 2 else [])
            macs = [("mac", p, o, n) for n in range(len(groups))]
            if p == PAIRED:
                extra = [("esplit", e, n, other) for e in range(CHUNKS) for n in range(4) for other in (False, True)]
                for n, group in enumerate(groups):
                    jobs[("macx", p, o, n)] = (3.5 + p, DOT + DOT_TILE * len(group), needs[n] + extra, [])
                add(("give", o), 1, SMALL, [("macx", p, o, n) for n in range(len(groups))], [(("mate", 1), 2.0, ("part", o))])
                macs.append(("part", o))
            if p % 2 == 0 and o == 2:
                add(("final", p, o), 1, 2 * SMALL, macs)
                add(("begin", p, o), 1, 0, [("final", p, o)] + [("turn", p + 1, 1, *key) for key in BEGIN], pushes)
            else:
                add(("final", p, o), 1, 2 * SMALL, macs, pushes)
    return jobs


def make_order(jobs):
    ready_at, missing, users = {}, {}, {}
    for name, (_, _, needs, _) in jobs.items():
        missing[name] = len(set(needs))
        ready_at[name] = 0.0
        for need in set(needs):
            users.setdefault(need, []).append(name)
    waiting, ready, free = [], [], {}
    rank = {name: n for n, name in enumerate(jobs)}

    def done(thing, when):
        for user in users.get(thing, ()):
            missing[user] -= 1
            ready_at[user] = max(ready_at[user], when)
            if missing[user] == 0:
                heapq.heappush(waiting, (ready_at[user], rank[user], user))

    for name in jobs:
        if missing[name] == 0:
            heapq.heappush(waiting, (0.0, rank[name], name))
    now, order, times = 0.0, [], {}
    while waiting or ready:
        if not ready and waiting[0][0] > now:
            now = waiting[0][0]
        while waiting and waiting[0][0] <= now:
            when, number, name = heapq.heappop(waiting)
            heapq.heappush(ready, (jobs[name][0], when, number, name))
        name = heapq.heappop(ready)[-1]
        _, cost, _, pushes = jobs[name]
        now += cost
        order.append(name)
        times[name] = now
        for (axis, steps), amount, piece in pushes:
            way = {"pair": ("x", True), "mate": ("x", False)}.get(axis, (axis, steps > 0))
            free[way] = max(free.get(way, 0.0), now) + amount * max(1, abs(steps)) * ROWS64
            done(piece, free[way] + HOP * (3.5 if piece[0] == "e" else 1))
        done(name, now)
    return order, times


JOBS = make_jobs()
ORDER, TIMES = make_order(JOBS)
PIECES = [piece for name in JOBS for _, _, piece in JOBS[name][3]]
ROW = {name: n for n, name in enumerate(piece for piece in PIECES if piece[0] == "row")}
PAIR = {name: n for n, name in enumerate(piece for piece in PIECES if piece[0] == "pair")}
COL = {name: n for n, name in enumerate(piece for piece in PIECES if piece[0] == "col")}


def split(value):
    high = value.astype(bf16)
    return high, (value - high.astype(f32)).astype(bf16)


def kernel(pattern_in, density, out, wide_rows, half_rows, cols, col_hi, col_lo, acc, extra, extra_hi, extra_lo,
           partial, landed, pattern, row_send, row_recv, pair_recv, col_send, col_recv, part_send, part_recv, move_send, move_recv,
           ring_send, ring_recv, lend_send, lend_recv, share_send, share_recv, local_sem):
    size = density.shape[0]
    r, c = lax.axis_index("row"), lax.axis_index("col")
    z, core = r // 2, r % 2
    y, x = c // NX, c % NX

    def device(dx=0, dy=0, dz=0):
        return (((z + dz + NZ) % NZ) * 2 + core, ((y + dy + NY) % NY) * NX + (x + dx + NX) % NX)

    sibling = (z * 2 + 1 - core, c)

    def k_row(dx, dy):
        return ((y - dy + NY) % NY) * NX + (x - dx + NX) % NX

    def k_col(dz, other):
        return ((z - dz + NZ) % NZ) * 2 + (1 - core if other else core)

    def stream_of(p, h):
        before = [h_ for p_ in range(4) for h_, other in enumerate(STREAMS[p_])
                  if (p_, h_) < (p, h) and other[3] == STREAMS[p][h][3]]
        return (wide_rows if STREAMS[p][h][3] == size else half_rows).at[len(before)]

    step_rows = HALVES[0][1] // 2
    fetch = [
        pltpu.make_async_copy(density.at[pl.ds((2 * h + plan) * step_rows, step_rows)], stream_of(0, h).at[plan, 0, 0],
                              local_sem.at[2 * h + plan])
        for h in (0, 1) for plan in (0, 1)]
    fetch += [
        pltpu.make_async_copy(density, cols.at[0, r], local_sem.at[4]),
        pltpu.make_async_copy(pattern_in, pattern, local_sem.at[5]),
    ]
    for copy in fetch:
        copy.start()

    peers = [device(dx=1), device(dx=-1), device(dy=1), device(dy=-1), sibling]
    peers += [device(dz=step) for step in (1, -1)]
    barrier = pltpu.get_barrier_semaphore()
    for peer in peers:
        pl.semaphore_signal(barrier, inc=1, device_id=peer, device_id_type=MESH)
    pl.semaphore_wait(barrier, len(peers))
    for copy in fetch:
        copy.wait()

    mask = [[pattern[a, b].astype(f32) for b in range(2)] for a in range(2)]

    def masked(value, low, lane):
        parts = [value[:, n:n + BLOCK] * mask[low // BLOCK][(lane + n) // BLOCK] for n in range(0, value.shape[1], BLOCK)]
        return jnp.concatenate(parts, axis=1)

    def slot_of(distance):
        return distance + distance // 2 - 2 * (distance // 3)

    def gathered(p, low, dx, dy):
        parts = []
        for h, stream in enumerate(STREAMS[p]):
            if stream[0] == low:
                ref = stream_of(p, h)
                parts.append(jnp.concatenate([ref[0, slot_of(dy), slot_of(dx)], ref[1, slot_of(dx), slot_of(dy)]], axis=0))
        return parts[0] if len(parts) == 1 else jnp.concatenate(parts, axis=1)

    def gathered_pair(low, dx, dy):
        parts = []
        for h, stream in enumerate(STREAMS[PAIRED]):
            if stream[0] == low:
                ref = stream_of(PAIRED, h)
                parts.append(jnp.concatenate([ref[plan, dx, slot_of(dy)] for plan in (0, 1)], axis=0))
        return parts[0] if len(parts) == 1 else jnp.concatenate(parts, axis=1)

    def remote(src, dst, send, recv, target):
        return pltpu.make_async_remote_copy(
            src_ref=src, dst_ref=dst, send_sem=send, recv_sem=recv, device_id=target, device_id_type=MESH)

    def row_copy(piece, where):
        _, p, h, plan, a, b = piece
        ref = stream_of(p, h).at[plan]
        moved = a if b == 0 else b
        held = SLOTS.index(0 if abs(moved) == 1 else where[1]) if where else SLOTS.index(moved)
        if b == 0:
            src, dst = ref.at[0, held], ref.at[0, SLOTS.index(a)]
        else:
            first, count = sets_of(p, h)[int(a[1])]
            src, dst = ref.at[held, pl.ds(first, count)], ref.at[SLOTS.index(b), pl.ds(first, count)]
        target = device(**{"d" + where[0]: where[1]}) if where else sibling
        return remote(src, dst, row_send.at[p], row_recv.at[ROW[piece]], target)

    def col_copy(piece, where):
        _, s, t, dz, part = piece
        low, count, lane, lanes = COLUMNS[t]
        if part in ("q0", "q1"):
            count //= 2
            low += count if part == "q1" else 0
        if not where:
            held, target = k_col(dz, part == "s"), sibling
        elif where[0] == "core":
            held, target = k_col(dz, False), sibling
        else:
            held, target = k_col(dz - where[1], False), device(dz=where[1])
        ref = cols.at[s, held, pl.ds(low, count), pl.ds(lane, lanes)]
        return remote(ref, ref, col_send.at[s], col_recv.at[COL[piece]], target)

    inward = 1 - 2 * (x % 2)
    mate = device(dx=-inward)
    odd = (z + x // 2) % 2
    count_e = size // CHUNKS

    def k_pair(dx, dy):
        return ((y - dy + NY) % NY) * NX + (x + inward if dx else x)

    def pair_copy(piece, where):
        _, h, plan, dx, dy = piece
        ref = stream_of(PAIRED, h).at[plan]
        if dy == "near":
            src, dst = ref.at[0, pl.ds(1, 2)], ref.at[1, pl.ds(1, 2)]
        elif where and where[0] == "pair":
            src, dst = ref.at[0, SLOTS.index(dy)], ref.at[1, SLOTS.index(dy)]
        else:
            held = 0 if abs(dy) < 2 else where[1] if where else 2
            src, dst = ref.at[dx, SLOTS.index(held)], ref.at[dx, SLOTS.index(dy)]
        target = sibling
        if where:
            target = device(dx=inward) if where[0] == "pair" else device(dy=where[1])
        return remote(src, dst, row_send.at[PAIRED], pair_recv.at[PAIR[piece]], target)

    def part_copy(piece, where):
        here = pl.ds(piece[1] * (size // 2), size // 2)
        return remote(partial.at[here], landed.at[here], part_send.at[0], part_recv.at[piece[1]], mate)

    def slot_rows(n):
        offset = (odd - 2, 2 - odd, 4 + odd, 3 * odd)[n]
        return ((z + offset + NZ) % NZ) // 2

    def extra_part(e, n, other):
        index = slot_rows(n) * 2 + (1 - core if other else core)
        return extra.at[index, pl.ds(e * count_e, count_e)]

    def ring_copy(e, n, ref):
        return remote(ref, ref, ring_send.at[0], ring_recv.at[e * 2 + n], device(dz=1 - 2 * n))

    def share_copy(e, n, other=False):
        ref = extra_part(e, n, other)
        return remote(ref, ref, share_send.at[0], share_recv.at[e * 4 + n], sibling)

    def move_copy(e):
        here = pl.ds(e * count_e, count_e)
        return remote(cols.at[1, r, here], extra.at[(z // 2) * 2 + core, here], move_send.at[0], move_recv.at[e], mate)

    def lend_copy(e, n):
        z_from = (z + (5 - odd if n == 2 else 3)) % NZ
        here = pl.ds(e * count_e, count_e)
        return remote(cols.at[1, z_from * 2 + core, here], extra.at[(z_from // 2) * 2 + core, here], lend_send.at[0],
                      lend_recv.at[e * 2 + n - 2], mate)

    def copy_of(piece, where=None):
        return {"row": row_copy, "col": col_copy, "pair": pair_copy, "part": part_copy}[piece[0]](piece, where)

    waited, begun = set(), set()

    def run(name):
        _, _, needs, pushes = JOBS[name]
        for need in needs:
            if need[0] in WAITED and need not in waited:
                waited.add(need)
                copy_of(need).wait_recv()
        kind = name[0]
        if kind == "split":
            _, s, t, dz, other = name
            k = k_col(dz, other)
            here = pl.ds(*COLUMNS[t][:2]), pl.ds(*COLUMNS[t][2:])
            high, low = split(cols[s, k, *here])
            col_hi[s, k, *here] = high
            col_lo[s, k, *here] = low
        elif kind == "move":
            @pl.when(odd == 1)
            def _():
                move_copy(name[1]).start()
        elif kind == "own":
            e = name[1]

            @pl.when(odd == 0)
            def _():
                move_copy(e).wait_recv()
                ring_copy(e, 0, extra_part(e, 3, False)).start()
                ring_copy(e, 1, extra_part(e, 3, False)).start()
                share_copy(e, 3).start()
        elif kind == "slot":
            _, e, n = name
            if n < 2:
                ring_copy(e, n, extra_part(e, n, False)).wait_recv()

                @pl.when(odd == 1)
                def _():
                    ring_copy(e, n, extra_part(e, n, False)).start()

                share_copy(e, n).start()
            elif n == 2:
                lend_copy(e, 2).wait_recv()
                share_copy(e, 2).start()
            else:
                @pl.when(odd == 1)
                def _():
                    lend_copy(e, 3).wait_recv()
                    share_copy(e, 3).start()
        elif kind == "lend":
            lend_copy(name[1], 2).start()

            @pl.when(odd == 0)
            def _():
                lend_copy(name[1], 3).start()
        elif kind == "esplit":
            _, e, n, other = name
            if other:
                share_copy(e, n, True).wait_recv()
            here = pl.ds(e * count_e, count_e)
            index = slot_rows(n) * 2 + (1 - core if other else core)
            high, low = split(extra[index, here, :])
            extra_hi[index, here, :] = high
            extra_lo[index, here, :] = low
        elif kind in ("mac", "macx"):
            _, p, o = name[:3]
            low, count, lane, lanes = STREAMS[p + 1][o]
            here, wide = pl.ds(low, count), pl.ds(lane, lanes)
            keys = GROUPS[p, o, name[3]]
            if p == PAIRED:
                places = [k_pair(*key) for key in keys]
                tiles = [gathered_pair(low, dx, dy % NY) for dx, dy in keys]
            elif isinstance(keys[0][1], bool):
                places = [k_col(*key) for key in keys]
                tiles = [gathered(p, low, (x - k % NX + NX) % NX, (y - k // NX + NY) % NY) for k in places]
            else:
                places = [k_row(*key) for key in keys]
                tiles = [gathered(p, low, dx % NX, dy % NY) for dx, dy in keys]
            high_a, low_a = split(jnp.concatenate(tiles, axis=1))
            if kind == "mac":
                high_b = jnp.concatenate([col_hi[p // 2, k, :, wide] for k in places], axis=0)
                low_b = jnp.concatenate([col_lo[p // 2, k, :, wide] for k in places], axis=0)
            else:
                places = [(k // NX) * 2 + k % 2 for k in places]
                high_b = jnp.concatenate([extra_hi[k] for k in places], axis=0)
                low_b = jnp.concatenate([extra_lo[k] for k in places], axis=0)
            both = jnp.dot(jnp.concatenate([high_a, low_a], axis=0), high_b, preferred_element_type=f32)
            term = both[:count] + both[count:] + jnp.dot(high_a, low_b, preferred_element_type=f32)
            total, at = (acc, (p, here, wide)) if kind == "mac" else (partial, (here, wide))
            if (kind, p, o) in begun:
                total[at] += term
            else:
                begun.add((kind, p, o))
                total[at] = term
        elif kind == "final":
            _, p, o = name
            low, count, lane, lanes = STREAMS[p + 1][o]
            here, wide = pl.ds(low, count), pl.ds(lane, lanes)
            value = acc[p, here, wide]
            if p == PAIRED:
                value += landed[here, wide]
            value = masked(value, low, lane)
            if p % 2:
                value = 3.0 * gathered(p, low, 0, 0) - 2.0 * value
            if p == 2 * STEPS - 1:
                out[here, wide] = value
            else:
                ref = stream_of(p + 1, o)
                ref[0, 0, 0] = value[:count // 2]
                ref[1, 0, 0] = value[count // 2:]
                if p % 2:
                    cols[p // 2 + 1, r, here, wide] = value
        for where, _, piece in pushes:
            if piece[0] in WAITED:
                copy_of(piece, where).start()

    for name in ORDER:
        run(name)

    def sent(ref, sem):
        pltpu.make_async_copy(ref, ref, sem).wait()

    for p in range(2 * STEPS):
        sent(cols.at[0, pl.ds(0, 7 if p == PAIRED else 15)], row_send.at[p])
    for s in range(STEPS):
        sent(cols.at[s, pl.ds(0, 15)], col_send.at[s])
    sent(partial, part_send.at[0])
    sent(extra.at[pl.ds(0, 4)], share_send.at[0])
    sent(extra.at[pl.ds(0, 2)], ring_send.at[0])

    @pl.when(odd == 0)
    def _():
        sent(extra.at[pl.ds(0, 2)], lend_send.at[0])

    @pl.when(odd == 1)
    def _():
        sent(extra.at[0], lend_send.at[0])
        sent(extra.at[0], move_send.at[0])


def local(density, pattern):
    size = density.shape[0]
    tiles = NX * NY
    dma = pltpu.SemaphoreType.DMA
    return pl.pallas_call(
        kernel,
        out_shape=jax.ShapeDtypeStruct(density.shape, f32),
        in_specs=[pl.BlockSpec(memory_space=pltpu.HBM), pl.BlockSpec(memory_space=pltpu.HBM)],
        out_specs=pl.BlockSpec(memory_space=pltpu.VMEM),
        scratch_shapes=[
            pltpu.VMEM((3 * STEPS, 2, NY, NX, size // 4, size), f32),
            pltpu.VMEM((2 * STEPS, 2, NY, NX, size // 4, size // 2), f32),
            pltpu.VMEM((STEPS, tiles, size, size), f32),
            pltpu.VMEM((STEPS, tiles, size, size), bf16),
            pltpu.VMEM((STEPS, tiles, size, size), bf16),
            pltpu.VMEM((2 * STEPS, size, size), f32),
            pltpu.VMEM((tiles // 2, size, size), f32),
            pltpu.VMEM((tiles // 2, size, size), bf16),
            pltpu.VMEM((tiles // 2, size, size), bf16),
            pltpu.VMEM((size, size), f32),
            pltpu.VMEM((size, size), f32),
            pltpu.SMEM(pattern.shape, jnp.int32),
            dma((2 * STEPS,)), dma((len(ROW),)), dma((len(PAIR),)),
            dma((STEPS,)), dma((len(COL),)),
            dma((1,)), dma((2,)),
            dma((1,)), dma((CHUNKS,)),
            dma((1,)), dma((CHUNKS * 2,)),
            dma((1,)), dma((CHUNKS * 2,)),
            dma((1,)), dma((CHUNKS * 4,)),
            dma((6,)),
        ],
        compiler_params=pltpu.CompilerParams(
            collective_id=0, has_side_effects=True, vmem_limit_bytes=56 * 1024 * 1024),
    )(pattern, density)


def solution(mesh):
    placed = P("row", "col")
    return jax.shard_map(local, mesh=mesh, in_specs=(placed, placed), out_specs=placed, check_vma=False)
```

```python
import heapq

import jax
import jax.numpy as jnp
from jax import lax
from jax.experimental import pallas as pl
from jax.experimental.pallas import tpu as pltpu
from jax.sharding import PartitionSpec as P

BLOCK = 128
STEPS = 2
NX, NY, NZ = 4, 4, 8
MESH = pl.DeviceIdType.MESH
f32, bf16 = jnp.float32, jnp.bfloat16
OFFSETS = [(dx, dy) for dx in (0, 1, -1, 2) for dy in (0, 1, -1, 2)]
RING = (0, 1, -1, 2, -2, 3, -3, 4)

GROUPS = {}
BEGIN_ROWS = ["g2"]
COL_SIZE = 1.0
BEGIN_COLS = (1, -1)
BEGIN = ["g1"]

ROWS64, HOP, SMALL, DOT, DOT_TILE = 1.45, 2.0, 0.03, 0.1, 0.1
NEAR_FIRST = [
    [(0, 0), (1, 0), (-1, 0), (0, 1), (0, -1)],
    [(2, 0), (0, 2), (1, 1), (1, -1), (-1, 1), (-1, -1)],
    [(1, 2), (-1, 2), (2, 1), (2, -1)],
    [(2, 2)],
]
COL_GROUPS = [[0], [1, -1], [2, -2], [3, -3], [4]]


HALVES = [(0, 128, 0, 256), (128, 128, 0, 256)]
SQUARE = [(0, 128, 0, 128), (0, 128, 128, 128), (128, 128, 0, 256)]
STREAMS = [HALVES, SQUARE, HALVES, SQUARE, HALVES]
COLUMNS = [(0, 128, 0, 128), (128, 128, 0, 128), (0, 128, 128, 128), (128, 128, 128, 128)]
AXES = {(axis, sign): (("first", "second")[axis], sign) for axis in (0, 1) for sign in (1, -1)}
SLOTS = (0, 1, -1, 2)
SETS = [((0, 1), (1, 2), (3, 1)), ((0, 1), (1, 3))]
SET_CHOICE = [[0, 0], [0, 0, 0], [0, 0], [0, 0, 0]]
FAR = [(0, 1, 0), (0, 1)]


def sets_of(p, h):
    return SETS[SET_CHOICE[p][h]]


def far_sign(p, h, group=None):
    turn = 0 if group is None else FAR[SET_CHOICE[p][h]][group]
    return 1 if (h + turn) % 2 == 0 else -1


def group_of(p, h, a):
    slot = SLOTS.index(a)
    return next(n for n, (first, count) in enumerate(sets_of(p, h)) if first <= slot < first + count)


def row_tile(p, h, a, b):
    if (a, b) == (0, 0):
        return []
    return [("row", p, h, a if b == 0 else "g%d" % group_of(p, h, a), b)]


def col_tile(s, t, dz, other):
    if other:
        return [("col", s, t, dz, "s")]
    if dz == 0:
        return []
    return [("col", s, t, dz, part) for part in (("q0", "q1") if dz == 4 else ("h",))]


def make_jobs():
    jobs = {}

    def row_size(p, h):
        return STREAMS[p][h][1] * STREAMS[p][h][3] / (128 * 256)

    def own_row(p, h):
        pushes = []
        for axis in (0, 1):
            for sign in (1, -1):
                a, b = (sign, 0) if axis == 0 else ("g0", sign)
                pushes.append((AXES[axis, sign], row_size(p, h), ("row", p, h, a, b)))
        return pushes

    def own_col(s, ts):
        pushes = []
        for t in ts:
            pushes += [(("z", step), COL_SIZE, ("col", s, t, step, "h")) for step in (1, -1)]
        return pushes + [(("core", 0), 0.15, ("col", s, t, 0, "s")) for t in ts]

    def overlap(one, other):
        return all(one[i] < other[i] + other[i + 1] and other[i] < one[i] + one[i + 1] for i in (0, 2))

    def add(name, priority, cost, needs, pushes=()):
        jobs[name] = (priority, cost + SMALL * (len(pushes) + len(needs)), needs, list(pushes))

    add(("start",), 0, SMALL, [], own_row(0, 0) + own_col(0, (0, 1)))
    add(("begin", 0, 1), 0, 0, [("turn", 0, 0, key) for key in BEGIN_ROWS], own_row(0, 1))
    add(("begin_col",), 0, 0, [("ring", 0, t, dz) for t in (0, 1) for dz in BEGIN_COLS], own_col(0, (2, 3)))
    for p in range(2 * STEPS):
        s = p // 2
        for h, stream in enumerate(STREAMS[p]):
            size = row_size(p, h)
            sign = far_sign(p, h)
            add(("turn", p, h, "far"), 0, 0, row_tile(p, h, sign, 0), [(AXES[0, sign], size, ("row", p, h, 2, 0))])
            for g, (first, count) in enumerate(sets_of(p, h)):
                if g:
                    needs = [piece for a in SLOTS[first:first + count] for piece in row_tile(p, h, a, 0)]
                    add(("turn", p, h, "g%d" % g), 0, 0, needs, [
                        (AXES[1, turn], size * count, ("row", p, h, "g%d" % g, turn)) for turn in (1, -1)])
                sign = far_sign(p, h, g)
                add(("pass", p, h, "g%d" % g), 0, 0, [("row", p, h, "g%d" % g, sign)],
                    [(AXES[1, sign], size * count, ("row", p, h, "g%d" % g, 2))])
        if p % 2 == 0:
            for t, dz in ((t, dz) for dz in RING for t in range(4)):
                pushes = []
                if dz:
                    sign = 1 if dz > 0 else -1
                    if abs(dz) < 3:
                        pushes.append((("z", sign), COL_SIZE, ("col", s, t, dz + sign, "h")))
                    elif dz != 4:
                        pushes.append((("z", sign), COL_SIZE / 2, ("col", s, t, 4, "q0" if sign == 1 else "q1")))
                    pushes.append((("core", 0), 0.15, ("col", s, t, dz, "s")))
                    add(("ring", s, t, dz), 0, 0, col_tile(s, t, dz, False), pushes)
                before = [("ring", s, t, dz)] if dz else [("start",) if p == 0 else ("final", p - 1, t % 2)]
                add(("split", s, t, dz, False), 2, SMALL, before)
                add(("split", s, t, dz, True), 2, SMALL, col_tile(s, t, dz, True))
        for o, target in enumerate(STREAMS[p + 1]):
            rows_used = [h for h, stream in enumerate(STREAMS[p]) if overlap(stream, (target[0], target[1], 0, 256))]
            cols_used = [t for t, col in enumerate(COLUMNS) if overlap(col, (0, 256, target[2], target[3]))]
            pieces = {key: [piece for h in rows_used for piece in row_tile(p, h, *key)] for key in OFFSETS}
            starts = [("start",) if p == 0 else ("final", p - 1, h) for h in rows_used]
            if p % 2 == 0 and target[0] == 0:
                need = [piece for key in OFFSETS for piece in pieces[key]] + starts
                groups = [[(dz, other) for dz in group for other in (False, True)] for group in COL_GROUPS]
                needs = [need + [("split", s, t, *key) for t in cols_used for key in group] for group in groups]
            else:
                groups = NEAR_FIRST
                need = [("split", s, t, dz, other) for t in cols_used for dz in RING for other in (False, True)]
                needs = [[piece for key in group for piece in pieces[key]] + starts + (need if p % 2 == 0 else [])
                         for group in groups]
            for n, group in enumerate(groups):
                cost = DOT + DOT_TILE * len(group) * (0.6 if target[3] == 128 else 1)
                jobs[("mac", p, o, n)] = (4 + p, cost, needs[n], [])
                GROUPS[p, o, n] = group
            pushes = []
            if p < 2 * STEPS - 1:
                pushes = own_row(p + 1, o) + (own_col(s + 1, (o, 2 + o)) if p % 2 else [])
            macs = [("mac", p, o, n) for n in range(len(groups))]
            if p % 2 == 0 and o == 2:
                add(("final", p, o), 1, 2 * SMALL, macs)
                add(("begin", p, o), 1, 0, [("final", p, o)] + [("turn", p + 1, 1, key) for key in BEGIN], pushes)
            else:
                add(("final", p, o), 1, 2 * SMALL, macs, pushes)
    return jobs


def make_order(jobs):
    ready_at, missing, users = {}, {}, {}
    for name, (_, _, needs, _) in jobs.items():
        missing[name] = len(set(needs))
        ready_at[name] = 0.0
        for need in set(needs):
            users.setdefault(need, []).append(name)
    waiting, ready, free = [], [], {}
    rank = {name: n for n, name in enumerate(jobs)}

    def done(thing, when):
        for user in users.get(thing, ()):
            missing[user] -= 1
            ready_at[user] = max(ready_at[user], when)
            if missing[user] == 0:
                heapq.heappush(waiting, (ready_at[user], rank[user], user))

    for name in jobs:
        if missing[name] == 0:
            heapq.heappush(waiting, (0.0, rank[name], name))
    now, order, times = 0.0, [], {}
    while waiting or ready:
        if not ready and waiting[0][0] > now:
            now = waiting[0][0]
        while waiting and waiting[0][0] <= now:
            when, number, name = heapq.heappop(waiting)
            heapq.heappush(ready, (jobs[name][0], when, number, name))
        name = heapq.heappop(ready)[-1]
        _, cost, _, pushes = jobs[name]
        now += cost
        order.append(name)
        times[name] = now
        for (axis, steps), amount, piece in pushes:
            way = "z" if axis == "z" else "core" if axis == "core" else "xy", steps > 0
            free[way] = max(free.get(way, 0.0), now) + amount * max(1, abs(steps)) * ROWS64
            done(piece, free[way] + HOP)
        done(name, now)
    return order, times


JOBS = make_jobs()
ORDER, TIMES = make_order(JOBS)
PIECES = [piece for name in JOBS for _, _, piece in JOBS[name][3]]
ROW = {name: n for n, name in enumerate(piece for piece in PIECES if piece[0] == "row")}
COL = {name: n for n, name in enumerate(piece for piece in PIECES if piece[0] == "col")}


def split(value):
    high = value.astype(bf16)
    return high, (value - high.astype(f32)).astype(bf16)


def kernel(pattern_in, density, out, wide_rows, half_rows, cols, col_hi, col_lo, acc, pattern,
           row_send, row_recv, col_send, col_recv, local_sem):
    size = density.shape[0]
    r, c = lax.axis_index("row"), lax.axis_index("col")
    z, core = r // 2, r % 2
    y, x = c // NX, c % NX

    def device(dx=0, dy=0, dz=0):
        return (((z + dz + NZ) % NZ) * 2 + core, ((y + dy + NY) % NY) * NX + (x + dx + NX) % NX)

    sibling = (z * 2 + 1 - core, c)

    def turned(a, b):
        return a * (1 - core) + b * core, b * (1 - core) + a * core

    def k_row(a, b):
        dx, dy = turned(a, b)
        return ((y - dy + NY) % NY) * NX + (x - dx + NX) % NX

    def k_col(dz, other):
        return ((z - dz + NZ) % NZ) * 2 + (1 - core if other else core)

    def stream_of(p, h):
        before = [h_ for p_ in range(4) for h_, other in enumerate(STREAMS[p_])
                  if (p_, h_) < (p, h) and other[3] == STREAMS[p][h][3]]
        return (wide_rows if STREAMS[p][h][3] == size else half_rows).at[len(before)]

    fetch = [pltpu.make_async_copy(density.at[pl.ds(*HALVES[h][:2])], stream_of(0, h).at[0, 0], local_sem.at[h]) for h in (0, 1)]
    fetch += [
        pltpu.make_async_copy(density, cols.at[0, r], local_sem.at[2]),
        pltpu.make_async_copy(pattern_in, pattern, local_sem.at[3]),
    ]
    for copy in fetch:
        copy.start()

    peers = [device(dx=1), device(dx=-1), device(dy=1), device(dy=-1), sibling]
    peers += [device(dz=step) for step in (1, -1)]
    barrier = pltpu.get_barrier_semaphore()
    for peer in peers:
        pl.semaphore_signal(barrier, inc=1, device_id=peer, device_id_type=MESH)
    pl.semaphore_wait(barrier, len(peers))
    for copy in fetch:
        copy.wait()

    mask = [[pattern[a, b].astype(f32) for b in range(2)] for a in range(2)]

    def masked(value, low, lane):
        parts = [value[:, n:n + BLOCK] * mask[low // BLOCK][(lane + n) // BLOCK] for n in range(0, value.shape[1], BLOCK)]
        return jnp.concatenate(parts, axis=1)

    def slot_of(distance):
        return distance + distance // 2 - 2 * (distance // 3)

    def gathered(p, low, a, b):
        parts = []
        for h, stream in enumerate(STREAMS[p]):
            if stream[0] == low:
                parts.append(stream_of(p, h)[slot_of(b), slot_of(a)])
        return parts[0] if len(parts) == 1 else jnp.concatenate(parts, axis=1)

    def remote(src, dst, send, recv, target):
        return pltpu.make_async_remote_copy(
            src_ref=src, dst_ref=dst, send_sem=send, recv_sem=recv, device_id=target, device_id_type=MESH)

    def row_copy(piece, where):
        _, p, h, a, b = piece
        ref = stream_of(p, h)
        moved = a if b == 0 else b
        held = SLOTS.index(0 if abs(moved) == 1 else where[1]) if where else SLOTS.index(moved)
        if b == 0:
            src, dst = ref.at[0, held], ref.at[0, SLOTS.index(a)]
        else:
            first, count = sets_of(p, h)[int(a[1])]
            src, dst = ref.at[held, pl.ds(first, count)], ref.at[SLOTS.index(b), pl.ds(first, count)]
        target = sibling
        if where:
            dx, dy = turned(where[1], 0) if where[0] == "first" else turned(0, where[1])
            target = device(dx=dx, dy=dy)
        return remote(src, dst, row_send.at[p], row_recv.at[ROW[piece]], target)

    def col_copy(piece, where):
        _, s, t, dz, part = piece
        low, count, lane, lanes = COLUMNS[t]
        if part in ("q0", "q1"):
            count //= 2
            low += count if part == "q1" else 0
        if not where:
            held, target = k_col(dz, part == "s"), sibling
        elif where[0] == "core":
            held, target = k_col(dz, False), sibling
        else:
            held, target = k_col(dz - where[1], False), device(dz=where[1])
        ref = cols.at[s, held, pl.ds(low, count), pl.ds(lane, lanes)]
        return remote(ref, ref, col_send.at[s], col_recv.at[COL[piece]], target)

    def copy_of(piece, where=None):
        return (row_copy if piece[0] == "row" else col_copy)(piece, where)

    waited, begun = set(), set()

    def run(name):
        _, _, needs, pushes = JOBS[name]
        for need in needs:
            if need[0] in ("row", "col") and need not in waited:
                waited.add(need)
                copy_of(need).wait_recv()
        kind = name[0]
        if kind == "split":
            _, s, t, dz, other = name
            k = k_col(dz, other)
            here = pl.ds(*COLUMNS[t][:2]), pl.ds(*COLUMNS[t][2:])
            high, low = split(cols[s, k, *here])
            col_hi[s, k, *here] = high
            col_lo[s, k, *here] = low
        elif kind == "mac":
            _, p, o = name[:3]
            low, count, lane, lanes = STREAMS[p + 1][o]
            here, wide = pl.ds(low, count), pl.ds(lane, lanes)
            keys = GROUPS[name[1:]]
            if isinstance(keys[0][1], bool):
                places = [k_col(*key) for key in keys]
                steps = [turned((x - k % NX + NX) % NX, (y - k // NX + NY) % NY) for k in places]
            else:
                places = [k_row(*key) for key in keys]
                steps = [(a % NX, b % NY) for a, b in keys]
            high_a, low_a = split(jnp.concatenate([gathered(p, low, *step) for step in steps], axis=1))
            high_b = jnp.concatenate([col_hi[p // 2, k, :, wide] for k in places], axis=0)
            low_b = jnp.concatenate([col_lo[p // 2, k, :, wide] for k in places], axis=0)
            both = jnp.dot(jnp.concatenate([high_a, low_a], axis=0), high_b, preferred_element_type=f32)
            term = both[:count] + both[count:] + jnp.dot(high_a, low_b, preferred_element_type=f32)
            if (p, o) in begun:
                acc[p, here, wide] += term
            else:
                begun.add((p, o))
                acc[p, here, wide] = term
        elif kind == "final":
            _, p, o = name
            low, count, lane, lanes = STREAMS[p + 1][o]
            here, wide = pl.ds(low, count), pl.ds(lane, lanes)
            value = masked(acc[p, here, wide], low, lane)
            if p % 2:
                value = 3.0 * gathered(p, low, 0, 0) - 2.0 * value
            if p == 2 * STEPS - 1:
                out[here, wide] = value
            else:
                ref = stream_of(p + 1, o)
                ref[0, 0] = value
                if p % 2:
                    cols[p // 2 + 1, r, here, wide] = value
        for where, _, piece in pushes:
            copy_of(piece, where).start()

    for name in ORDER:
        run(name)

    def sent(ref, sem):
        pltpu.make_async_copy(ref, ref, sem).wait()

    for p in range(2 * STEPS):
        sent(cols.at[0, pl.ds(0, 15)], row_send.at[p])
    for s in range(STEPS):
        sent(cols.at[s, pl.ds(0, 15)], col_send.at[s])


def local(density, pattern):
    size = density.shape[0]
    tiles = NX * NY
    return pl.pallas_call(
        kernel,
        out_shape=jax.ShapeDtypeStruct(density.shape, f32),
        in_specs=[pl.BlockSpec(memory_space=pltpu.HBM), pl.BlockSpec(memory_space=pltpu.HBM)],
        out_specs=pl.BlockSpec(memory_space=pltpu.VMEM),
        scratch_shapes=[
            pltpu.VMEM((3 * STEPS, NY, NX, size // 2, size), f32),
            pltpu.VMEM((2 * STEPS, NY, NX, size // 2, size // 2), f32),
            pltpu.VMEM((STEPS, tiles, size, size), f32),
            pltpu.VMEM((STEPS, tiles, size, size), bf16),
            pltpu.VMEM((STEPS, tiles, size, size), bf16),
            pltpu.VMEM((2 * STEPS, size, size), f32),
            pltpu.SMEM(pattern.shape, jnp.int32),
            pltpu.SemaphoreType.DMA((2 * STEPS,)),
            pltpu.SemaphoreType.DMA((len(ROW),)),
            pltpu.SemaphoreType.DMA((STEPS,)),
            pltpu.SemaphoreType.DMA((len(COL),)),
            pltpu.SemaphoreType.DMA((4,)),
        ],
        compiler_params=pltpu.CompilerParams(
            collective_id=0, has_side_effects=True, vmem_limit_bytes=56 * 1024 * 1024),
    )(pattern, density)


def solution(mesh):
    placed = P("row", "col")
    return jax.shard_map(local, mesh=mesh, in_specs=(placed, placed), out_specs=placed, check_vma=False)
```

```python
import heapq

import jax
import jax.numpy as jnp
from jax import lax
from jax.experimental import pallas as pl
from jax.experimental.pallas import tpu as pltpu
from jax.sharding import PartitionSpec as P

BLOCK = 128
STEPS = 2
NX, NY, NZ = 4, 4, 8
MESH = pl.DeviceIdType.MESH
f32, bf16 = jnp.float32, jnp.bfloat16
OFFSETS = [(dx, dy) for dx in (0, 1, -1, 2) for dy in (0, 1, -1, 2)]
RING = (0, 1, -1, 2, -2, 3, -3, 4)
LAST = 2 * STEPS - 1
GROUPS = {}

ROWS64, HOP, SMALL, DOT, DOT_TILE = 1.4, 2.2, 0.03, 0.15, 0.08
ON_CHIP = 0.3
BEGIN_ROWS = ["g1"]
BEGIN = ["g1"]
NEAR_FIRST = [
    [(0, 0), (1, 0), (-1, 0), (0, 1), (0, -1)],
    [(2, 0), (0, 2), (1, 1), (1, -1), (-1, 1), (-1, -1)],
    [(1, 2), (-1, 2), (2, 1), (2, -1)],
    [(2, 2)],
]
COL_GROUPS = [[0, 1, -1], [2, -2], [3, -3], [4]]
SLOTS = (0, 1, -1, 2)
SETS = [(0, 1), (1, 2), (3, 1)]
FAR = (0, 1, 0)


def far_sign(h, plan, group=None):
    turn = 0 if group is None else FAR[group]
    return 1 if (h + plan + turn) % 2 == 0 else -1


def group_of(a):
    slot = SLOTS.index(a)
    return next(n for n, (first, count) in enumerate(SETS) if first <= slot < first + count)


def row_tile(p, h, plan, a, b):
    if (a, b) == (0, 0):
        return []
    return [("row", p, h, plan, a if b == 0 else "g%d" % group_of(a), b)]


def col_tile(s, t, dz, cc):
    if dz == 0:
        return []
    return [("col", s, t, dz, part, cc) for part in (("q0", "q1") if dz == 4 else ("h",))]


def make_jobs():
    jobs = {}

    def link(plan, axis, sign):
        return ("x" if (axis == 0) == (plan == 0) else "y", sign)

    def own_row(p, h, plans=(0, 1)):
        pushes = []
        for axis in (0, 1):
            for plan in plans:
                for sign in (1, -1):
                    a, b = (sign, 0) if axis == 0 else ("g0", sign)
                    pushes.append((link(plan, axis, sign), 1.0, ("row", p, h, plan, a, b)))
        return pushes

    def own_col(s, cc, ts):
        size = 0.5 if s else 1.0
        return [(("z", sign), size, ("col", s, t, sign, "h", cc)) for t in ts for sign in (1, -1)]

    def add(name, priority, cost, needs, pushes=()):
        jobs[name] = (priority, cost + SMALL * (len(pushes) + len(needs)), needs, list(pushes))

    add(("start",), 0, SMALL, [], [(("core", 0), ON_CHIP, ("init", n)) for n in range(4)]
        + own_row(0, 0, (0,)) + own_col(0, None, (0, 1)))
    add(("start_rows",), 0, 0, [("init", 0)], own_row(0, 0, (1,)))
    add(("start_cols",), 0, 0, [("init", 2)], own_col(0, None, (2, 3)))
    add(("begin", 0, 1), 0, 0, [("init", 1)] + [("turn", 0, 0, plan, key) for plan in (0, 1) for key in BEGIN_ROWS], own_row(0, 1))
    for p in range(2 * STEPS):
        s = p // 2
        for h in (0, 1):
            for plan in (0, 1):
                sign = far_sign(h, plan)
                add(("turn", p, h, plan, "far"), 0, 0, row_tile(p, h, plan, sign, 0),
                    [(link(plan, 0, sign), 1.0, ("row", p, h, plan, 2, 0))])
                for g, (first, count) in enumerate(SETS):
                    if g:
                        needs = [piece for a in SLOTS[first:first + count] for piece in row_tile(p, h, plan, a, 0)]
                        add(("turn", p, h, plan, "g%d" % g), 0, 0, needs, [
                            (link(plan, 1, turn), count, ("row", p, h, plan, "g%d" % g, turn)) for turn in (1, -1)])
                    sign = far_sign(h, plan, g)
                    add(("pass", p, h, plan, "g%d" % g), 0, 0, [("row", p, h, plan, "g%d" % g, sign)],
                        [(link(plan, 1, sign), count, ("row", p, h, plan, "g%d" % g, 2))])
        cores = [None] if s == 0 else [0, 1]
        if p % 2 == 0:
            for cc in cores:
                size = 0.5 if s else 1.0
                if s:
                    add(("begin_col", cc), 0, 0, [("final", p - 1, cc)], own_col(s, cc, range(4)))
                for t, dz in ((t, dz) for dz in RING for t in range(4)):
                    pushes = []
                    if dz:
                        sign = 1 if dz > 0 else -1
                        if abs(dz) < 3:
                            pushes.append((("z", sign), size, ("col", s, t, dz + sign, "h", cc)))
                        elif dz != 4:
                            pushes.append((("z", sign), size / 2, ("col", s, t, 4, "q0" if sign == 1 else "q1", cc)))
                        add(("ring", s, t, dz, cc), 0, 0, col_tile(s, t, dz, cc), pushes)
                    first = ("begin_col", cc) if s else ("start",) if t < 2 else ("start_cols",)
                    add(("split", s, t, dz, cc), 2, SMALL, [("ring", s, t, dz, cc)] if dz else [first])
        for o in (0, 1):
            pieces = {key: row_tile(p, o, 0, *key) + row_tile(p, o, 1, *key[::-1]) for key in OFFSETS}
            if p == 0:
                begun = [("start_rows",)] if o == 0 else [("begin", 0, 1)]
            else:
                begun = [("final", p - 1, o)]
            if p % 2 == 0 and o == 0:
                need = [piece for key in OFFSETS for piece in pieces[key]] + begun
                groups = [[(dz, plan == 1) for dz in group for plan in (0, 1)] for group in COL_GROUPS]
                needs = [need + [("split", s, 2 * other + n, dz, cc) for dz, other in group for n in (0, 1) for cc in cores]
                         for group in groups]
            else:
                groups = NEAR_FIRST
                need = [("split", s, t, dz, cc) for t in range(4) for dz in RING for cc in cores] if p % 2 == 0 else []
                needs = [[piece for key in group for piece in pieces[key]] + begun + need for group in groups]
            for n, group in enumerate(groups):
                jobs[("mac", p, o, n)] = (4 + p, DOT + DOT_TILE * len(group), needs[n], [])
                GROUPS[p, o, n] = group
            add(("give", p, o), 1, SMALL, [("mac", p, o, n) for n in range(len(groups))], [(("core", 0), 2 * ON_CHIP, ("given", p, o))])
            extra = [("squared", o)] if p == LAST else []
            add(("final", p, o), 1, 3 * SMALL, [("give", p, o), ("given", p, o)] + extra)
            if p == LAST:
                continue
            if p % 2 == 0 and o:
                gate = [("turn", p + 1, 0, plan, key) for plan in (0, 1) for key in BEGIN]
            else:
                gate = []
            add(("go", p, o), 1, 0, [("final", p, o)] + gate, own_row(p + 1, o))
            if p == LAST - 1:
                add(("square", o), 3, SMALL, [("final", p, o)], [(("core", 0), ON_CHIP, ("squared", o))])
    return jobs


def make_order(jobs):
    ready_at, missing, users = {}, {}, {}
    for name, (_, _, needs, _) in jobs.items():
        missing[name] = len(set(needs))
        ready_at[name] = 0.0
        for need in set(needs):
            users.setdefault(need, []).append(name)
    waiting, ready, free, brought = [], [], {}, set()
    rank = {name: n for n, name in enumerate(jobs)}

    def done(thing, when):
        if thing in brought:
            return
        brought.add(thing)
        for user in users.get(thing, ()):
            missing[user] -= 1
            ready_at[user] = max(ready_at[user], when)
            if missing[user] == 0:
                heapq.heappush(waiting, (ready_at[user], rank[user], user))

    for name in jobs:
        if missing[name] == 0:
            heapq.heappush(waiting, (0.0, rank[name], name))
    now, order, times = 0.0, [], {}
    while waiting or ready:
        if not ready and waiting[0][0] > now:
            now = waiting[0][0]
        while waiting and waiting[0][0] <= now:
            when, number, name = heapq.heappop(waiting)
            heapq.heappush(ready, (jobs[name][0], when, number, name))
        name = heapq.heappop(ready)[-1]
        _, cost, _, pushes = jobs[name]
        now += cost
        order.append(name)
        times[name] = now
        for (axis, steps), amount, piece in pushes:
            way = axis, steps > 0
            free[way] = max(free.get(way, 0.0), now) + amount * ROWS64
            done(piece, free[way] + HOP)
        done(name, now)
    return order, times


JOBS = make_jobs()
ORDER, TIMES = make_order(JOBS)
PIECES = [piece for name in JOBS for _, _, piece in JOBS[name][3]]
ROW = {name: n for n, name in enumerate(piece for piece in PIECES if piece[0] == "row")}
COL = {name: n for n, name in enumerate(dict.fromkeys(piece[:5] for piece in PIECES if piece[0] == "col"))}


def split(value):
    high = value.astype(bf16)
    return high, (value - high.astype(f32)).astype(bf16)


def kernel(pattern_in, density, out, rows, cols, col_hi, col_lo, acc, landed, square, mask, pattern,
           row_send, row_recv, col_send, col_recv, init_send, init_recv, give_send, give_recv, square_send, square_recv, local_sem):
    half = density.shape[0] // 2
    r, c = lax.axis_index("row"), lax.axis_index("col")
    z, core = r // 2, r % 2
    y, x = c // NX, c % NX
    other = 1 - core

    def device(dx=0, dy=0, dz=0):
        return (((z + dz + NZ) % NZ) * 2 + core, ((y + dy + NY) % NY) * NX + (x + dx + NX) % NX)

    sibling = (z * 2 + other, c)

    def remote(src, dst, send, recv, target):
        return pltpu.make_async_remote_copy(
            src_ref=src, dst_ref=dst, send_sem=send, recv_sem=recv, device_id=target, device_id_type=MESH)

    def k_row(dx, dy):
        return ((y - dy + NY) % NY) * NX + (x - dx + NX) % NX

    def k_col(dz, plan):
        return ((z - dz + NZ) % NZ) * 2 + (other if plan else core)

    def place(p, h, plan, b, a):
        return ((p * 2 + h) * 2 + plan) * 16 + b * 4 + a

    lanes = pl.ds(pl.multiple_of(core * half, half), half)
    lanes_other = pl.ds(pl.multiple_of(other * half, half), half)
    mine = pl.ds(pl.multiple_of(core * half, half), half)
    theirs = pl.ds(pl.multiple_of(other * half, half), half)
    fetch = [pltpu.make_async_copy(density.at[pl.ds(h * half, half), lanes], rows.at[place(0, h, 0, 0, 0)], local_sem.at[h])
             for h in (0, 1)]
    fetch += [
        pltpu.make_async_copy(density.at[mine], cols.at[0, r], local_sem.at[2]),
        pltpu.make_async_copy(pattern_in, pattern, local_sem.at[3]),
    ]
    for copy in fetch:
        copy.start()

    peers = [device(dx=1), device(dx=-1), device(dy=1), device(dy=-1), device(dz=1), device(dz=-1), sibling]
    barrier = pltpu.get_barrier_semaphore()
    for peer in peers:
        pl.semaphore_signal(barrier, inc=1, device_id=peer, device_id_type=MESH)
    pl.semaphore_wait(barrier, len(peers))
    for copy in fetch:
        copy.wait()
    for h in (0, 1):
        for g in (0, 1):
            mask[0, h, g] = jnp.full((8, half), pattern[h, g].astype(f32), f32)

    def init_copy(n):
        if n < 2:
            src, dst = density.at[pl.ds(n * half, half), lanes_other], rows.at[place(0, n, 1, 0, 0)]
        elif n == 2:
            src, dst = density.at[theirs], cols.at[0, r]
        else:
            src, dst = mask.at[0], mask.at[1]
        return remote(src, dst, init_send.at[n], init_recv.at[n], sibling)

    def init_wait(n):
        dst = (rows.at[place(0, n, 1, 0, 0)] if n < 2 else cols.at[0, z * 2 + other] if n == 2 else mask.at[1])
        remote(dst, dst, init_send.at[n], init_recv.at[n], sibling).wait_recv()

    def slot_of(distance):
        return distance + distance // 2 - 2 * (distance // 3)

    def gathered(p, h, dx, dy):
        a, b = slot_of(dx), slot_of(dy)
        return jnp.concatenate([rows[place(p, h, 0, b, a)], rows[place(p, h, 1, a, b)]], axis=0)

    def row_copy(piece, where):
        _, p, h, plan, a, b = piece
        moved = a if b == 0 else b
        held = SLOTS.index(0 if abs(moved) == 1 else where[1]) if where else SLOTS.index(moved)
        if b == 0:
            src, dst = rows.at[place(p, h, plan, 0, held)], rows.at[place(p, h, plan, 0, SLOTS.index(a))]
        else:
            first, count = SETS[int(a[1])]
            src = rows.at[pl.ds(place(p, h, plan, held, first), count)]
            dst = rows.at[pl.ds(place(p, h, plan, SLOTS.index(b), first), count)]
        target = device(**{"d" + where[0]: where[1]}) if where else sibling
        return remote(src, dst, row_send.at[p], row_recv.at[ROW[piece]], target)

    def col_copy(piece, where):
        _, s, t, dz, part, _ = piece
        count = half // 2
        low = (t % 2) * count
        if part != "h":
            count //= 2
            low += count if part == "q1" else 0
        held = k_col(dz - where[1] if where else dz, t // 2)
        ref = cols.at[s, held, pl.ds(low, count)]
        return remote(ref, ref, col_send.at[s], col_recv.at[COL[piece[:5]]], device(dz=where[1]) if where else sibling)

    def give_copy(p, o, plan, whole):
        src, dst = acc.at[p, o, plan], landed.at[p, o, 1 - plan]
        if not whole:
            src, dst = src.at[other], dst.at[other]
        return remote(src, dst, give_send.at[p], give_recv.at[(p * 2 + o) * 2 + 1 - plan], sibling)

    def given_wait(p, o, plan, whole):
        dst = landed.at[p, o, plan]
        if not whole:
            dst = dst.at[core]
        remote(dst, dst, give_send.at[p], give_recv.at[(p * 2 + o) * 2 + plan], sibling).wait_recv()

    def square_copy(h):
        return remote(square.at[1, h, 1, h], square.at[1, h, 0, h], square_send.at[0], square_recv.at[h], sibling)

    def summed(p, o, plan, g):
        return (acc[p, o, plan, g] + landed[p, o, plan, g]) * mask[plan, o, g, 0:1, :]

    waited, begun = set(), set()

    def run_job(name):
        kind = name[0]
        needs, pushes = JOBS[name][2:]
        for need in needs:
            if need[0] in ("row", "col") and need not in waited:
                waited.add(need)
                (row_copy if need[0] == "row" else col_copy)(need, None).wait_recv()
            if need[0] == "init" and need not in waited:
                waited.add(need)
                init_wait(need[1])
        if kind == "split":
            _, s, t, dz, _ = name
            k = k_col(dz, t // 2)
            here = pl.ds((t % 2) * (half // 2), half // 2)
            high, low = split(cols[s, k, here, :])
            col_hi[s, k, here, :] = high
            col_lo[s, k, here, :] = low
        elif kind == "mac":
            _, p, o, _ = name
            keys = GROUPS[name[1:]]
            if isinstance(keys[0][1], bool):
                places = [k_col(*key) for key in keys]
                tiles = [gathered(p, o, (x - k % NX + NX) % NX, (y - k // NX + NY) % NY) for k in places]
            else:
                places = [k_row(*key) for key in keys]
                tiles = [gathered(p, o, dx % NX, dy % NY) for dx, dy in keys]
            high_a, low_a = split(jnp.concatenate(tiles, axis=1))
            high_b = jnp.concatenate([col_hi[p // 2, k] for k in places], axis=0)
            low_b = jnp.concatenate([col_lo[p // 2, k] for k in places], axis=0)
            term = (jnp.dot(high_a, high_b, preferred_element_type=f32) + jnp.dot(low_a, high_b, preferred_element_type=f32)
                    + jnp.dot(high_a, low_b, preferred_element_type=f32))
            for plan in (0, 1):
                for g in (0, 1):
                    part = term[plan * half:(plan + 1) * half, g * half:(g + 1) * half]
                    acc[p, o, plan, g] = acc[p, o, plan, g] + part if (p, o) in begun else part
            begun.add((p, o))
        elif kind == "give":
            _, p, o = name
            if p == LAST:
                give_copy(p, o, 1, True).start()
            else:
                @pl.when(core == o)
                def _():
                    for plan in (0, 1):
                        give_copy(p, o, plan, False).start()

                @pl.when(core != o)
                def _():
                    for plan in (0, 1):
                        give_copy(p, o, plan, True).start()
        elif kind == "final":
            _, p, o = name
            s = p // 2
            here = pl.ds(o * half, half)
            if ("mask",) not in waited:
                waited.add(("mask",))
                init_wait(3)
            if p == LAST:
                given_wait(p, o, 0, True)

                @pl.when(core != o)
                def _():
                    remote(square.at[1, o, 0, o], square.at[1, o, 0, o], square_send.at[0], square_recv.at[o], sibling).wait_recv()

                for g in (0, 1):
                    out[here, pl.ds(g * half, half)] = 3.0 * square[s, o, 0, g] - 2.0 * summed(p, o, 0, g)
                return

            def value_of(plan, g):
                value = summed(p, o, plan, g)
                if p % 2:
                    return 3.0 * square[s, o, plan, g] - 2.0 * value
                square[s, o, plan, g] = value
                return value

            @pl.when(core == o)
            def _():
                for plan in (0, 1):
                    given_wait(p, o, plan, True)
                    for g in (0, 1):
                        value = value_of(plan, g)
                        if g == o:
                            rows[place(p + 1, o, plan, 0, 0)] = value
                        if p % 2:
                            cols[s + 1, k_col(0, plan), :, pl.ds(g * half, half)] = value

            @pl.when(core != o)
            def _():
                for plan in (0, 1):
                    given_wait(p, o, plan, False)
                    rows[place(p + 1, o, plan, 0, 0)] = value_of(plan, 1 - o)
        elif kind == "square":
            h = name[1]

            @pl.when(core == h)
            def _():
                square_copy(h).start()
        for where, _, piece in pushes:
            if piece[0] == "row":
                row_copy(piece, where).start()
            elif piece[0] == "col":
                col_copy(piece, where).start()
            elif piece[0] == "init":
                init_copy(piece[1]).start()

    def run(name):
        cc = name[-1] if name[0] in ("ring", "split", "begin_col") else None
        if cc is None:
            run_job(name)
        else:
            @pl.when(core == cc)
            def _():
                run_job(name)

    for name in ORDER:
        run(name)

    def sent(ref, sem):
        pltpu.make_async_copy(ref, ref, sem).wait()

    for n in (0, 1):
        sent(rows.at[0], init_send.at[n])
    sent(cols.at[0, 0], init_send.at[2])
    sent(mask.at[0], init_send.at[3])
    for p in range(2 * STEPS):
        sent(rows.at[pl.ds(0, 60)], row_send.at[p])
        sent(rows.at[pl.ds(0, 4 if p == LAST else 6)], give_send.at[p])
    for s in range(STEPS):
        sent(rows.at[pl.ds(0, 28)], col_send.at[s])
    sent(rows.at[0], square_send.at[0])


def local(density, pattern):
    size = density.shape[0]
    half = size // 2
    tiles = NX * NY
    phases = 2 * STEPS
    dma = pltpu.SemaphoreType.DMA
    return pl.pallas_call(
        kernel,
        out_shape=jax.ShapeDtypeStruct(density.shape, f32),
        in_specs=[pl.BlockSpec(memory_space=pl.ANY), pl.BlockSpec(memory_space=pl.ANY)],
        out_specs=pl.BlockSpec(memory_space=pltpu.VMEM),
        scratch_shapes=[
            pltpu.VMEM((phases * 4 * tiles, half, half), f32),
            pltpu.VMEM((STEPS, tiles, half, size), f32),
            pltpu.VMEM((STEPS, tiles, half, size), bf16),
            pltpu.VMEM((STEPS, tiles, half, size), bf16),
            pltpu.VMEM((phases, 2, 2, 2, half, half), f32),
            pltpu.VMEM((phases, 2, 2, 2, half, half), f32),
            pltpu.VMEM((STEPS, 2, 2, 2, half, half), f32),
            pltpu.VMEM((2, 2, 2, 8, half), f32),
            pltpu.SMEM(pattern.shape, jnp.int32),
            dma((phases,)), dma((len(ROW),)),
            dma((STEPS,)), dma((len(COL),)),
            dma((4,)), dma((4,)),
            dma((phases,)), dma((phases * 4,)),
            dma((1,)), dma((2,)),
            dma((4,)),
        ],
        compiler_params=pltpu.CompilerParams(
            collective_id=0, has_side_effects=True, vmem_limit_bytes=56 * 1024 * 1024),
    )(pattern, density)


def solution(mesh):
    placed = P("row", "col")
    return jax.shard_map(local, mesh=mesh, in_specs=(placed, placed), out_specs=placed, check_vma=False)
```

```python
import heapq

import jax
import jax.numpy as jnp
from jax import lax
from jax.experimental import pallas as pl
from jax.experimental.pallas import tpu as pltpu
from jax.sharding import PartitionSpec as P

BLOCK = 128
STEPS = 2
NX, NY, NZ = 4, 4, 8
MESH = pl.DeviceIdType.MESH
f32, bf16 = jnp.float32, jnp.bfloat16
OFFSETS = [(dx, dy) for dx in (0, 1, -1, 2) for dy in (0, 1, -1, 2)]
RING = (0, 1, -1, 2, -2, 3, -3, 4)

GROUPS = {}
BEGIN_ROWS = [(0, "g1"), (1, "g1")]
COL_SIZE = 1.0
BEGIN_COLS = {}
LATER_COLS = {}
DIRECT = set()
BEGIN = [(0, "g1"), (1, "g1")]

ROWS64, HOP, SMALL, DOT, DOT_TILE = 1.4, 2.2, 0.02, 0.1, 0.1
NEAR_FIRST = [
    [(0, 0), (1, 0), (-1, 0), (0, 1), (0, -1)],
    [(2, 0), (0, 2), (1, 1), (1, -1), (-1, 1), (-1, -1)],
    [(1, 2), (-1, 2), (2, 1), (2, -1)],
    [(2, 2)],
]
COL_GROUPS = [[0], [1, -1], [2, -2], [3, -3], [4]]


HALVES = [(0, 128, 0, 256), (128, 128, 0, 256)]
SQUARE = [(0, 128, 0, 128), (0, 128, 128, 128), (128, 128, 0, 256)]
STREAMS = [HALVES, SQUARE, HALVES, SQUARE, HALVES]
COLUMNS = [(0, 128, 0, 128), (128, 128, 0, 128), (0, 128, 128, 128), (128, 128, 128, 128)]
SLOTS = (0, 1, -1, 2)
SETS = [((0, 1), (1, 2), (3, 1)), ((0, 1), (1, 3))]
SET_CHOICE = [[0, 0], [0, 0, 0], [0, 0], [0, 0, 0]]
FAR = [(0, 1, 0), (0, 1)]


def sets_of(p, h):
    return SETS[SET_CHOICE[p][h]]


def far_sign(p, h, plan, group=None):
    turn = 0 if group is None else FAR[SET_CHOICE[p][h]][group]
    return 1 if (h + plan + turn) % 2 == 0 else -1


def group_of(p, h, a):
    slot = SLOTS.index(a)
    return next(n for n, (first, count) in enumerate(sets_of(p, h)) if first <= slot < first + count)


def row_tile(p, h, plan, a, b):
    if (a, b) == (0, 0):
        return []
    return [("row", p, h, plan, a if b == 0 else "g%d" % group_of(p, h, a), b)]


def col_tile(s, t, dz, other):
    if other:
        return [("col", s, t, dz, "s")]
    if dz == 0:
        return []
    return [("col", s, t, dz, part) for part in (("q0", "q1") if dz == 4 else ("h",))]


def make_jobs():
    jobs = {}

    def link(plan, axis, sign):
        return ("x" if (axis == 0) == (plan == 0) else "y", sign)

    def row_size(p, h):
        return STREAMS[p][h][1] * STREAMS[p][h][3] / (128 * 256)

    def own_row(p, h):
        pushes = []
        for axis in (0, 1):
            for plan in (0, 1):
                for sign in (1, -1):
                    a, b = (sign, 0) if axis == 0 else ("g0", sign)
                    pushes.append((link(plan, axis, sign), row_size(p, h), ("row", p, h, plan, a, b)))
        return pushes

    def own_col(s, ts):
        pushes = []
        for t in ts:
            pushes += [(("z", step), COL_SIZE, ("col", s, t, step, "h")) for step in ((1, -1, 2, -2) if (s, t) in DIRECT else (1, -1))]
        return pushes + [(("core", 0), 0.15, ("col", s, t, 0, "s")) for t in ts]

    def overlap(one, other):
        return all(one[i] < other[i] + other[i + 1] and other[i] < one[i] + one[i + 1] for i in (0, 2))

    def add(name, priority, cost, needs, pushes=()):
        jobs[name] = (priority, cost + SMALL * (len(pushes) + len(needs)), needs, list(pushes))

    add(("start",), 0, SMALL, [], own_row(0, 0) + own_col(0, [t for t in range(4) if t not in BEGIN_COLS]))
    add(("begin", 0, 1), 0, 0, [("turn", 0, 0, *key) for key in BEGIN_ROWS], own_row(0, 1))
    for t, (behind, dz) in BEGIN_COLS.items():
        add(("begin_col", t), 0, 0, [("ring", 0, behind, sign * dz) for sign in (1, -1)], own_col(0, (t,)))
    for t, (behind, dz) in LATER_COLS.items():
        begun = ("final", 1, COLUMNS[t][0] // 128)
        add(("later_col", t), 0, 0, [begun] + [("ring", 1, behind, sign * dz) for sign in (1, -1)], own_col(1, (t,)))
    for p in range(2 * STEPS):
        s = p // 2
        for h, stream in enumerate(STREAMS[p]):
            size = row_size(p, h)
            for plan in (0, 1):
                for sign in (1, -1):
                    pushes = []
                    if sign == far_sign(p, h, plan):
                        pushes = [(link(plan, 0, sign), size, ("row", p, h, plan, 2, 0))]
                        add(("turn", p, h, plan, sign), 0, 0, row_tile(p, h, plan, sign, 0), pushes)
                for g, (first, count) in enumerate(sets_of(p, h)):
                    if g:
                        needs = [piece for a in SLOTS[first:first + count] for piece in row_tile(p, h, plan, a, 0)]
                        add(("turn", p, h, plan, "g%d" % g), 0, 0, needs, [
                            (link(plan, 1, turn), size * count, ("row", p, h, plan, "g%d" % g, turn)) for turn in (1, -1)])
                    sign = far_sign(p, h, plan, g)
                    add(("pass", p, h, plan, "g%d" % g), 0, 0, [("row", p, h, plan, "g%d" % g, sign)],
                        [(link(plan, 1, sign), size * count, ("row", p, h, plan, "g%d" % g, 2))])
        if p % 2 == 0:
            for t, dz in ((t, dz) for dz in RING for t in range(4)):
                pushes = []
                if dz:
                    sign = 1 if dz > 0 else -1
                    if (s, t) in DIRECT:
                        if abs(dz) == 2:
                            pushes.append((("z", sign), COL_SIZE, ("col", s, t, dz + sign, "h")))
                            pushes.append((("z", 2 * sign), COL_SIZE / 2, ("col", s, t, 4, "q0" if sign == 1 else "q1")))
                    elif abs(dz) < 3:
                        pushes.append((("z", sign), COL_SIZE, ("col", s, t, dz + sign, "h")))
                    elif dz != 4:
                        pushes.append((("z", sign), COL_SIZE / 2, ("col", s, t, 4, "q0" if sign == 1 else "q1")))
                    pushes.append((("core", 0), 0.15, ("col", s, t, dz, "s")))
                    add(("ring", s, t, dz), 0, 0, col_tile(s, t, dz, False), pushes)
                before = [("ring", s, t, dz)] if dz else [("start",) if p == 0 else ("final", p - 1, t % 2)]
                add(("split", s, t, dz, False), 2, SMALL, before)
                add(("split", s, t, dz, True), 2, SMALL, col_tile(s, t, dz, True))
        for o, target in enumerate(STREAMS[p + 1]):
            rows_used = [h for h, stream in enumerate(STREAMS[p]) if overlap(stream, (target[0], target[1], 0, 256))]
            cols_used = [t for t, col in enumerate(COLUMNS) if overlap(col, (0, 256, target[2], target[3]))]
            pieces = {key: [piece for h in rows_used
                            for piece in row_tile(p, h, 0, *key) + row_tile(p, h, 1, *key[::-1])] for key in OFFSETS}
            starts = [("start",) if p == 0 else ("final", p - 1, h) for h in rows_used]
            if p % 2 == 0 and target[0] == 0:
                need = [piece for key in OFFSETS for piece in pieces[key]] + starts
                groups = [[(dz, other) for dz in group for other in (False, True)] for group in COL_GROUPS]
                needs = [need + [("split", s, t, *key) for t in cols_used for key in group] for group in groups]
            else:
                groups = NEAR_FIRST
                need = [("split", s, t, dz, other) for t in cols_used for dz in RING for other in (False, True)]
                needs = [[piece for key in group for piece in pieces[key]] + starts + (need if p % 2 == 0 else [])
                         for group in groups]
            for n, group in enumerate(groups):
                cost = DOT + DOT_TILE * len(group) * (0.6 if target[3] == 128 else 1)
                jobs[("mac", p, o, n)] = (4 + p, cost, needs[n], [])
                GROUPS[p, o, n] = group
            pushes = []
            if p < 2 * STEPS - 1:
                pushes = own_row(p + 1, o) + (own_col(s + 1, [t for t in (o, 2 + o) if t not in LATER_COLS]) if p % 2 else [])
            macs = [("mac", p, o, n) for n in range(len(groups))]
            if p % 2 == 0 and o == 2:
                add(("final", p, o), 1, 2 * SMALL, macs)
                add(("begin", p, o), 1, 0, [("final", p, o)] + [("turn", p + 1, 1, *key) for key in BEGIN], pushes)
            else:
                add(("final", p, o), 1, 2 * SMALL, macs, pushes)
    return jobs


def make_order(jobs):
    ready_at, missing, users = {}, {}, {}
    for name, (_, _, needs, _) in jobs.items():
        missing[name] = len(set(needs))
        ready_at[name] = 0.0
        for need in set(needs):
            users.setdefault(need, []).append(name)
    waiting, ready, free = [], [], {}
    rank = {name: n for n, name in enumerate(jobs)}

    def done(thing, when):
        for user in users.get(thing, ()):
            missing[user] -= 1
            ready_at[user] = max(ready_at[user], when)
            if missing[user] == 0:
                heapq.heappush(waiting, (ready_at[user], rank[user], user))

    for name in jobs:
        if missing[name] == 0:
            heapq.heappush(waiting, (0.0, rank[name], name))
    now, order, times = 0.0, [], {}
    while waiting or ready:
        if not ready and waiting[0][0] > now:
            now = waiting[0][0]
        while waiting and waiting[0][0] <= now:
            when, number, name = heapq.heappop(waiting)
            heapq.heappush(ready, (jobs[name][0], when, number, name))
        name = heapq.heappop(ready)[-1]
        _, cost, _, pushes = jobs[name]
        now += cost
        order.append(name)
        times[name] = now
        for (axis, steps), amount, piece in pushes:
            way = axis, steps > 0
            free[way] = max(free.get(way, 0.0), now) + amount * max(1, abs(steps)) * ROWS64
            done(piece, free[way] + HOP)
        done(name, now)
    return order, times


JOBS = make_jobs()
ORDER, TIMES = make_order(JOBS)
PIECES = [piece for name in JOBS for _, _, piece in JOBS[name][3]]
ROW = {name: n for n, name in enumerate(piece for piece in PIECES if piece[0] == "row")}
COL = {name: n for n, name in enumerate(piece for piece in PIECES if piece[0] == "col")}


def split(value):
    high = value.astype(bf16)
    return high, (value - high.astype(f32)).astype(bf16)


def kernel(pattern_in, density, out, wide_rows, half_rows, cols, col_hi, col_lo, acc, pattern,
           row_send, row_recv, col_send, col_recv, local_sem):
    size = density.shape[0]
    r, c = lax.axis_index("row"), lax.axis_index("col")
    z, core = r // 2, r % 2
    y, x = c // NX, c % NX

    def device(dx=0, dy=0, dz=0):
        return (((z + dz + NZ) % NZ) * 2 + core, ((y + dy + NY) % NY) * NX + (x + dx + NX) % NX)

    sibling = (z * 2 + 1 - core, c)

    def k_row(dx, dy):
        return ((y - dy + NY) % NY) * NX + (x - dx + NX) % NX

    def k_col(dz, other):
        return ((z - dz + NZ) % NZ) * 2 + (1 - core if other else core)

    def stream_of(p, h):
        before = [h_ for p_ in range(4) for h_, other in enumerate(STREAMS[p_])
                  if (p_, h_) < (p, h) and other[3] == STREAMS[p][h][3]]
        return (wide_rows if STREAMS[p][h][3] == size else half_rows).at[len(before)]

    step_rows = HALVES[0][1] // 2
    fetch = [
        pltpu.make_async_copy(density.at[pl.ds((2 * h + plan) * step_rows, step_rows)], stream_of(0, h).at[plan, 0, 0],
                              local_sem.at[2 * h + plan])
        for h in (0, 1) for plan in (0, 1)]
    fetch += [
        pltpu.make_async_copy(density, cols.at[0, r], local_sem.at[4]),
        pltpu.make_async_copy(pattern_in, pattern, local_sem.at[5]),
    ]
    for copy in fetch:
        copy.start()

    peers = [device(dx=1), device(dx=-1), device(dy=1), device(dy=-1), sibling]
    peers += [device(dz=step) for step in ((1, -1, 2, -2) if DIRECT else (1, -1))]
    barrier = pltpu.get_barrier_semaphore()
    for peer in peers:
        pl.semaphore_signal(barrier, inc=1, device_id=peer, device_id_type=MESH)
    pl.semaphore_wait(barrier, len(peers))
    for copy in fetch:
        copy.wait()

    mask = [[pattern[a, b].astype(f32) for b in range(2)] for a in range(2)]

    def masked(value, low, lane):
        parts = [value[:, n:n + BLOCK] * mask[low // BLOCK][(lane + n) // BLOCK] for n in range(0, value.shape[1], BLOCK)]
        return jnp.concatenate(parts, axis=1)

    def slot_of(distance):
        return distance + distance // 2 - 2 * (distance // 3)

    def gathered(p, low, dx, dy):
        parts = []
        for h, stream in enumerate(STREAMS[p]):
            if stream[0] == low:
                ref = stream_of(p, h)
                parts.append(jnp.concatenate([ref[0, slot_of(dy), slot_of(dx)], ref[1, slot_of(dx), slot_of(dy)]], axis=0))
        return parts[0] if len(parts) == 1 else jnp.concatenate(parts, axis=1)

    def remote(src, dst, send, recv, target):
        return pltpu.make_async_remote_copy(
            src_ref=src, dst_ref=dst, send_sem=send, recv_sem=recv, device_id=target, device_id_type=MESH)

    def row_copy(piece, where):
        _, p, h, plan, a, b = piece
        ref = stream_of(p, h).at[plan]
        moved = a if b == 0 else b
        held = SLOTS.index(0 if abs(moved) == 1 else where[1]) if where else SLOTS.index(moved)
        if b == 0:
            src, dst = ref.at[0, held], ref.at[0, SLOTS.index(a)]
        else:
            first, count = sets_of(p, h)[int(a[1])]
            src, dst = ref.at[held, pl.ds(first, count)], ref.at[SLOTS.index(b), pl.ds(first, count)]
        target = device(**{"d" + where[0]: where[1]}) if where else sibling
        return remote(src, dst, row_send.at[p], row_recv.at[ROW[piece]], target)

    def col_copy(piece, where):
        _, s, t, dz, part = piece
        low, count, lane, lanes = COLUMNS[t]
        if part in ("q0", "q1"):
            count //= 2
            low += count if part == "q1" else 0
        if not where:
            held, target = k_col(dz, part == "s"), sibling
        elif where[0] == "core":
            held, target = k_col(dz, False), sibling
        else:
            held, target = k_col(dz - where[1], False), device(dz=where[1])
        ref = cols.at[s, held, pl.ds(low, count), pl.ds(lane, lanes)]
        return remote(ref, ref, col_send.at[s], col_recv.at[COL[piece]], target)

    def copy_of(piece, where=None):
        return (row_copy if piece[0] == "row" else col_copy)(piece, where)

    waited, begun = set(), set()

    def run(name):
        _, _, needs, pushes = JOBS[name]
        for need in needs:
            if need[0] in ("row", "col") and need not in waited:
                waited.add(need)
                copy_of(need).wait_recv()
        kind = name[0]
        if kind == "split":
            _, s, t, dz, other = name
            k = k_col(dz, other)
            here = pl.ds(*COLUMNS[t][:2]), pl.ds(*COLUMNS[t][2:])
            high, low = split(cols[s, k, *here])
            col_hi[s, k, *here] = high
            col_lo[s, k, *here] = low
        elif kind == "mac":
            _, p, o = name[:3]
            low, count, lane, lanes = STREAMS[p + 1][o]
            here, wide = pl.ds(low, count), pl.ds(lane, lanes)
            keys = GROUPS[name[1:]]
            if isinstance(keys[0][1], bool):
                places = [k_col(*key) for key in keys]
                steps = [((x - k % NX + NX) % NX, (y - k // NX + NY) % NY) for k in places]
            else:
                places = [k_row(*key) for key in keys]
                steps = [(dx % NX, dy % NY) for dx, dy in keys]
            high_a, low_a = split(jnp.concatenate([gathered(p, low, *step) for step in steps], axis=1))
            high_b = jnp.concatenate([col_hi[p // 2, k, :, wide] for k in places], axis=0)
            low_b = jnp.concatenate([col_lo[p // 2, k, :, wide] for k in places], axis=0)
            both = jnp.dot(jnp.concatenate([high_a, low_a], axis=0), high_b, preferred_element_type=f32)
            term = both[:count] + both[count:] + jnp.dot(high_a, low_b, preferred_element_type=f32)
            if (p, o) in begun:
                acc[p, here, wide] += term
            else:
                begun.add((p, o))
                acc[p, here, wide] = term
        elif kind == "final":
            _, p, o = name
            low, count, lane, lanes = STREAMS[p + 1][o]
            here, wide = pl.ds(low, count), pl.ds(lane, lanes)
            value = masked(acc[p, here, wide], low, lane)
            if p % 2:
                value = 3.0 * gathered(p, low, 0, 0) - 2.0 * value
            if p == 2 * STEPS - 1:
                out[here, wide] = value
            else:
                ref = stream_of(p + 1, o)
                ref[0, 0, 0] = value[:count // 2]
                ref[1, 0, 0] = value[count // 2:]
                if p % 2:
                    cols[p // 2 + 1, r, here, wide] = value
        for where, _, piece in pushes:
            copy_of(piece, where).start()

    for name in ORDER:
        run(name)

    def sent(ref, sem):
        pltpu.make_async_copy(ref, ref, sem).wait()

    for p in range(2 * STEPS):
        sent(cols.at[0, pl.ds(0, 15)], row_send.at[p])
    for s in range(STEPS):
        sent(cols.at[s, pl.ds(0, 15)], col_send.at[s])


def local(density, pattern):
    size = density.shape[0]
    tiles = NX * NY
    return pl.pallas_call(
        kernel,
        out_shape=jax.ShapeDtypeStruct(density.shape, f32),
        in_specs=[pl.BlockSpec(memory_space=pltpu.HBM), pl.BlockSpec(memory_space=pltpu.HBM)],
        out_specs=pl.BlockSpec(memory_space=pltpu.VMEM),
        scratch_shapes=[
            pltpu.VMEM((3 * STEPS, 2, NY, NX, size // 4, size), f32),
            pltpu.VMEM((2 * STEPS, 2, NY, NX, size // 4, size // 2), f32),
            pltpu.VMEM((STEPS, tiles, size, size), f32),
            pltpu.VMEM((STEPS, tiles, size, size), bf16),
            pltpu.VMEM((STEPS, tiles, size, size), bf16),
            pltpu.VMEM((2 * STEPS, size, size), f32),
            pltpu.SMEM(pattern.shape, jnp.int32),
            pltpu.SemaphoreType.DMA((2 * STEPS,)),
            pltpu.SemaphoreType.DMA((len(ROW),)),
            pltpu.SemaphoreType.DMA((STEPS,)),
            pltpu.SemaphoreType.DMA((len(COL),)),
            pltpu.SemaphoreType.DMA((6,)),
        ],
        compiler_params=pltpu.CompilerParams(
            collective_id=0, has_side_effects=True, vmem_limit_bytes=56 * 1024 * 1024),
    )(pattern, density)


def solution(mesh):
    placed = P("row", "col")
    return jax.shard_map(local, mesh=mesh, in_specs=(placed, placed), out_specs=placed, check_vma=False)
```

```python
import heapq

import jax
import jax.numpy as jnp
from jax import lax
from jax.experimental import pallas as pl
from jax.experimental.pallas import tpu as pltpu
from jax.sharding import PartitionSpec as P

BLOCK = 128
STEPS = 2
NX, NY, NZ = 4, 4, 8
MESH = pl.DeviceIdType.MESH
f32, bf16 = jnp.float32, jnp.bfloat16
OFFSETS = [(dx, dy) for dx in (0, 1, -1, 2) for dy in (0, 1, -1, 2)]
RING = (0, 1, -1, 2, -2, 3, -3, 4)

GROUPS = {}
BEGIN_ROWS = [(0, "g1"), (1, "g1")]
COL_SIZE = 1.0
BEGIN_COLS = {}
LATER_COLS = {}
DIRECT = set()
BEGIN = [(0, "g1"), (1, "g1")]

ROWS64, HOP, SMALL, DOT, DOT_TILE = 1.4, 2.2, 0.02, 0.1, 0.1
NEAR_FIRST = [
    [(0, 0), (1, 0), (-1, 0), (0, 1), (0, -1)],
    [(2, 0), (0, 2), (1, 1), (1, -1), (-1, 1), (-1, -1)],
    [(1, 2), (-1, 2), (2, 1), (2, -1)],
    [(2, 2)],
]
COL_GROUPS = [[0], [1, -1], [2, -2], [3, -3], [4]]


HALVES = [(0, 128, 0, 256), (128, 128, 0, 256)]
SQUARE = [(0, 128, 0, 128), (0, 128, 128, 128), (128, 128, 0, 256)]
STREAMS = [HALVES, SQUARE, HALVES, SQUARE, HALVES]
COLUMNS = [(0, 128, 0, 128), (128, 128, 0, 128), (0, 128, 128, 128), (128, 128, 128, 128)]
SLOTS = (0, 1, -1, 2)
SETS = [((0, 1), (1, 2), (3, 1)), ((0, 1), (1, 3))]
SET_CHOICE = [[0, 0], [0, 0, 0], [0, 0], [0, 0, 0]]
FAR = [(0, 1, 0), (0, 1)]


def sets_of(p, h):
    return SETS[SET_CHOICE[p][h]]


def far_sign(p, h, plan, group=None):
    turn = 0 if group is None else FAR[SET_CHOICE[p][h]][group]
    return 1 if (h + plan + turn) % 2 == 0 else -1


def group_of(p, h, a):
    slot = SLOTS.index(a)
    return next(n for n, (first, count) in enumerate(sets_of(p, h)) if first <= slot < first + count)


def row_tile(p, h, plan, a, b):
    if (a, b) == (0, 0):
        return []
    return [("row", p, h, plan, a if b == 0 else "g%d" % group_of(p, h, a), b)]


def col_tile(s, t, dz, other):
    if other:
        return [("col", s, t, dz, "s")]
    if dz == 0:
        return []
    return [("col", s, t, dz, part) for part in (("q0", "q1") if dz == 4 else ("h",))]


def make_jobs():
    jobs = {}

    def link(plan, axis, sign):
        return ("x" if (axis == 0) == (plan == 0) else "y", sign)

    def row_size(p, h):
        return STREAMS[p][h][1] * STREAMS[p][h][3] / (128 * 256)

    def own_row(p, h):
        pushes = []
        for axis in (0, 1):
            for plan in (0, 1):
                for sign in (1, -1):
                    a, b = (sign, 0) if axis == 0 else ("g0", sign)
                    pushes.append((link(plan, axis, sign), row_size(p, h), ("row", p, h, plan, a, b)))
        return pushes

    def own_col(s, ts):
        pushes = []
        for t in ts:
            pushes += [(("z", step), COL_SIZE, ("col", s, t, step, "h")) for step in ((1, -1, 2, -2) if (s, t) in DIRECT else (1, -1))]
        return pushes + [(("core", 0), 0.15, ("col", s, t, 0, "s")) for t in ts]

    def overlap(one, other):
        return all(one[i] < other[i] + other[i + 1] and other[i] < one[i] + one[i + 1] for i in (0, 2))

    def add(name, priority, cost, needs, pushes=()):
        jobs[name] = (priority, cost + SMALL * (len(pushes) + len(needs)), needs, list(pushes))

    add(("start",), 0, SMALL, [], own_row(0, 0) + own_col(0, [t for t in range(4) if t not in BEGIN_COLS]))
    add(("begin", 0, 1), 0, 0, [("turn", 0, 0, *key) for key in BEGIN_ROWS], own_row(0, 1))
    for t, (behind, dz) in BEGIN_COLS.items():
        add(("begin_col", t), 0, 0, [("ring", 0, behind, sign * dz) for sign in (1, -1)], own_col(0, (t,)))
    for t, (behind, dz) in LATER_COLS.items():
        begun = ("final", 1, COLUMNS[t][0] // 128)
        add(("later_col", t), 0, 0, [begun] + [("ring", 1, behind, sign * dz) for sign in (1, -1)], own_col(1, (t,)))
    for p in range(2 * STEPS):
        s = p // 2
        for h, stream in enumerate(STREAMS[p]):
            size = row_size(p, h)
            for plan in (0, 1):
                for sign in (1, -1):
                    pushes = []
                    if sign == far_sign(p, h, plan):
                        pushes = [(link(plan, 0, sign), size, ("row", p, h, plan, 2, 0))]
                        add(("turn", p, h, plan, sign), 0, 0, row_tile(p, h, plan, sign, 0), pushes)
                for g, (first, count) in enumerate(sets_of(p, h)):
                    if g:
                        needs = [piece for a in SLOTS[first:first + count] for piece in row_tile(p, h, plan, a, 0)]
                        add(("turn", p, h, plan, "g%d" % g), 0, 0, needs, [
                            (link(plan, 1, turn), size * count, ("row", p, h, plan, "g%d" % g, turn)) for turn in (1, -1)])
                    sign = far_sign(p, h, plan, g)
                    add(("pass", p, h, plan, "g%d" % g), 0, 0, [("row", p, h, plan, "g%d" % g, sign)],
                        [(link(plan, 1, sign), size * count, ("row", p, h, plan, "g%d" % g, 2))])
        if p % 2 == 0:
            for t, dz in ((t, dz) for dz in RING for t in range(4)):
                pushes = []
                if dz:
                    sign = 1 if dz > 0 else -1
                    if (s, t) in DIRECT:
                        if abs(dz) == 2:
                            pushes.append((("z", sign), COL_SIZE, ("col", s, t, dz + sign, "h")))
                            pushes.append((("z", 2 * sign), COL_SIZE / 2, ("col", s, t, 4, "q0" if sign == 1 else "q1")))
                    elif abs(dz) < 3:
                        pushes.append((("z", sign), COL_SIZE, ("col", s, t, dz + sign, "h")))
                    elif dz != 4:
                        pushes.append((("z", sign), COL_SIZE / 2, ("col", s, t, 4, "q0" if sign == 1 else "q1")))
                    pushes.append((("core", 0), 0.15, ("col", s, t, dz, "s")))
                    add(("ring", s, t, dz), 0, 0, col_tile(s, t, dz, False), pushes)
                before = [("ring", s, t, dz)] if dz else [("start",) if p == 0 else ("final", p - 1, t % 2)]
                add(("split", s, t, dz, False), 2, SMALL, before)
                add(("split", s, t, dz, True), 2, SMALL, col_tile(s, t, dz, True))
        for o, target in enumerate(STREAMS[p + 1]):
            rows_used = [h for h, stream in enumerate(STREAMS[p]) if overlap(stream, (target[0], target[1], 0, 256))]
            cols_used = [t for t, col in enumerate(COLUMNS) if overlap(col, (0, 256, target[2], target[3]))]
            pieces = {key: [piece for h in rows_used
                            for piece in row_tile(p, h, 0, *key) + row_tile(p, h, 1, *key[::-1])] for key in OFFSETS}
            starts = [("start",) if p == 0 else ("final", p - 1, h) for h in rows_used]
            if p % 2 == 0 and target[0] == 0:
                need = [piece for key in OFFSETS for piece in pieces[key]] + starts
                groups = [[(dz, other) for dz in group for other in (False, True)] for group in COL_GROUPS]
                needs = [need + [("split", s, t, *key) for t in cols_used for key in group] for group in groups]
            else:
                groups = NEAR_FIRST
                need = [("split", s, t, dz, other) for t in cols_used for dz in RING for other in (False, True)]
                needs = [[piece for key in group for piece in pieces[key]] + starts + (need if p % 2 == 0 else [])
                         for group in groups]
            for n, group in enumerate(groups):
                cost = DOT + DOT_TILE * len(group) * (0.6 if target[3] == 128 else 1)
                jobs[("mac", p, o, n)] = (4 + p, cost, needs[n], [])
                GROUPS[p, o, n] = group
            pushes = []
            if p < 2 * STEPS - 1:
                pushes = own_row(p + 1, o) + (own_col(s + 1, [t for t in (o, 2 + o) if t not in LATER_COLS]) if p % 2 else [])
            macs = [("mac", p, o, n) for n in range(len(groups))]
            if p % 2 == 0 and o == 2:
                add(("final", p, o), 1, 2 * SMALL, macs)
                add(("begin", p, o), 1, 0, [("final", p, o)] + [("turn", p + 1, 1, *key) for key in BEGIN], pushes)
            else:
                add(("final", p, o), 1, 2 * SMALL, macs, pushes)
    return jobs


def make_order(jobs):
    ready_at, missing, users = {}, {}, {}
    for name, (_, _, needs, _) in jobs.items():
        missing[name] = len(set(needs))
        ready_at[name] = 0.0
        for need in set(needs):
            users.setdefault(need, []).append(name)
    waiting, ready, free = [], [], {}
    rank = {name: n for n, name in enumerate(jobs)}

    def done(thing, when):
        for user in users.get(thing, ()):
            missing[user] -= 1
            ready_at[user] = max(ready_at[user], when)
            if missing[user] == 0:
                heapq.heappush(waiting, (ready_at[user], rank[user], user))

    for name in jobs:
        if missing[name] == 0:
            heapq.heappush(waiting, (0.0, rank[name], name))
    now, order, times = 0.0, [], {}
    while waiting or ready:
        if not ready and waiting[0][0] > now:
            now = waiting[0][0]
        while waiting and waiting[0][0] <= now:
            when, number, name = heapq.heappop(waiting)
            heapq.heappush(ready, (jobs[name][0], when, number, name))
        name = heapq.heappop(ready)[-1]
        _, cost, _, pushes = jobs[name]
        now += cost
        order.append(name)
        times[name] = now
        for (axis, steps), amount, piece in pushes:
            way = axis, steps > 0
            free[way] = max(free.get(way, 0.0), now) + amount * max(1, abs(steps)) * ROWS64
            done(piece, free[way] + HOP)
        done(name, now)
    return order, times


JOBS = make_jobs()
ORDER, TIMES = make_order(JOBS)
PIECES = [piece for name in JOBS for _, _, piece in JOBS[name][3]]
ROW = {name: n for n, name in enumerate(piece for piece in PIECES if piece[0] == "row")}
COL = {name: n for n, name in enumerate(piece for piece in PIECES if piece[0] == "col")}


def split(value):
    high = value.astype(bf16)
    return high, (value - high.astype(f32)).astype(bf16)


def kernel(pattern_in, density, out, wide_rows, half_rows, cols, col_hi, col_lo, acc, pattern,
           row_send, row_recv, col_send, col_recv, local_sem):
    size = density.shape[0]
    r, c = lax.axis_index("row"), lax.axis_index("col")
    z, core = r // 2, r % 2
    y, x = c // NX, c % NX

    def device(dx=0, dy=0, dz=0):
        return (((z + dz + NZ) % NZ) * 2 + core, ((y + dy + NY) % NY) * NX + (x + dx + NX) % NX)

    sibling = (z * 2 + 1 - core, c)

    def k_row(dx, dy):
        return ((y - dy + NY) % NY) * NX + (x - dx + NX) % NX

    def k_col(dz, other):
        return ((z - dz + NZ) % NZ) * 2 + (1 - core if other else core)

    def stream_of(p, h):
        before = [h_ for p_ in range(4) for h_, other in enumerate(STREAMS[p_])
                  if (p_, h_) < (p, h) and other[3] == STREAMS[p][h][3]]
        return (wide_rows if STREAMS[p][h][3] == size else half_rows).at[len(before)]

    step_rows = HALVES[0][1] // 2
    fetch = [
        pltpu.make_async_copy(density.at[pl.ds((2 * h + plan) * step_rows, step_rows)], stream_of(0, h).at[plan, 0, 0],
                              local_sem.at[2 * h + plan])
        for h in (0, 1) for plan in (0, 1)]
    fetch += [
        pltpu.make_async_copy(density, cols.at[0, r], local_sem.at[4]),
        pltpu.make_async_copy(pattern_in, pattern, local_sem.at[5]),
    ]
    for copy in fetch:
        copy.start()

    peers = [device(dx=1), device(dx=-1), device(dy=1), device(dy=-1), sibling]
    peers += [device(dz=step) for step in ((1, -1, 2, -2) if DIRECT else (1, -1))]
    barrier = pltpu.get_barrier_semaphore()
    for peer in peers:
        pl.semaphore_signal(barrier, inc=1, device_id=peer, device_id_type=MESH)
    pl.semaphore_wait(barrier, len(peers))
    mask = []

    def masked(value, low, lane):
        if not mask:
            fetch[-1].wait()
            mask.extend([pattern[a, b].astype(f32) for b in range(2)] for a in range(2))
        parts = [value[:, n:n + BLOCK] * mask[low // BLOCK][(lane + n) // BLOCK] for n in range(0, value.shape[1], BLOCK)]
        return jnp.concatenate(parts, axis=1)

    def slot_of(distance):
        return distance + distance // 2 - 2 * (distance // 3)

    def gathered(p, low, dx, dy):
        parts = []
        for h, stream in enumerate(STREAMS[p]):
            if stream[0] == low:
                ref = stream_of(p, h)
                parts.append(jnp.concatenate([ref[0, slot_of(dy), slot_of(dx)], ref[1, slot_of(dx), slot_of(dy)]], axis=0))
        return parts[0] if len(parts) == 1 else jnp.concatenate(parts, axis=1)

    def remote(src, dst, send, recv, target):
        return pltpu.make_async_remote_copy(
            src_ref=src, dst_ref=dst, send_sem=send, recv_sem=recv, device_id=target, device_id_type=MESH)

    def row_copy(piece, where):
        _, p, h, plan, a, b = piece
        ref = stream_of(p, h).at[plan]
        moved = a if b == 0 else b
        held = SLOTS.index(0 if abs(moved) == 1 else where[1]) if where else SLOTS.index(moved)
        if b == 0:
            src, dst = ref.at[0, held], ref.at[0, SLOTS.index(a)]
        else:
            first, count = sets_of(p, h)[int(a[1])]
            here = pl.ds(first, count) if count > 1 else first
            src, dst = ref.at[held, here], ref.at[SLOTS.index(b), here]
        if where and p == 0 and held == 0 and (b == 0 or a == "g0"):
            src = density.at[pl.ds((2 * h + plan) * step_rows, step_rows)]
        target = device(**{"d" + where[0]: where[1]}) if where else sibling
        return remote(src, dst, row_send.at[p], row_recv.at[ROW[piece]], target)

    def col_copy(piece, where):
        _, s, t, dz, part = piece
        low, count, lane, lanes = COLUMNS[t]
        if part in ("q0", "q1"):
            count //= 2
            low += count if part == "q1" else 0
        if not where:
            held, target = k_col(dz, part == "s"), sibling
        elif where[0] == "core":
            held, target = k_col(dz, False), sibling
        else:
            held, target = k_col(dz - where[1], False), device(dz=where[1])
        here = pl.ds(low, count), pl.ds(lane, lanes)
        ref = cols.at[s, held, *here]
        if where and s == 0 and dz in ((0,) if where[0] == "core" else (where[1],)):
            return remote(density.at[*here], ref, col_send.at[s], col_recv.at[COL[piece]], target)
        return remote(ref, ref, col_send.at[s], col_recv.at[COL[piece]], target)

    def copy_of(piece, where=None):
        return (row_copy if piece[0] == "row" else col_copy)(piece, where)

    waited, begun = set(), set()

    def run(name):
        _, _, needs, pushes = JOBS[name]
        for need in needs:
            if need[0] in ("row", "col") and need not in waited:
                waited.add(need)
                copy_of(need).wait_recv()
        kind = name[0]
        if kind == "split":
            _, s, t, dz, other = name
            k = k_col(dz, other)
            here = pl.ds(*COLUMNS[t][:2]), pl.ds(*COLUMNS[t][2:])
            high, low = split(cols[s, k, *here])
            col_hi[s, k, *here] = high
            col_lo[s, k, *here] = low
        elif kind == "mac":
            _, p, o = name[:3]
            low, count, lane, lanes = STREAMS[p + 1][o]
            here, wide = pl.ds(low, count), pl.ds(lane, lanes)
            keys = GROUPS[name[1:]]
            if isinstance(keys[0][1], bool):
                places = [k_col(*key) for key in keys]
                steps = [((x - k % NX + NX) % NX, (y - k // NX + NY) % NY) for k in places]
            else:
                places = [k_row(*key) for key in keys]
                steps = [(dx % NX, dy % NY) for dx, dy in keys]
            high_a, low_a = split(jnp.concatenate([gathered(p, low, *step) for step in steps], axis=1))
            high_b = jnp.concatenate([col_hi[p // 2, k, :, wide] for k in places], axis=0)
            low_b = jnp.concatenate([col_lo[p // 2, k, :, wide] for k in places], axis=0)
            both = jnp.dot(jnp.concatenate([high_a, low_a], axis=0), high_b, preferred_element_type=f32)
            term = both[:count] + both[count:] + jnp.dot(high_a, low_b, preferred_element_type=f32)
            if (p, o) in begun:
                acc[p, here, wide] += term
            else:
                begun.add((p, o))
                acc[p, here, wide] = term
        elif kind == "final":
            _, p, o = name
            low, count, lane, lanes = STREAMS[p + 1][o]
            here, wide = pl.ds(low, count), pl.ds(lane, lanes)
            value = masked(acc[p, here, wide], low, lane)
            if p % 2:
                value = 3.0 * gathered(p, low, 0, 0) - 2.0 * value
            if p == 2 * STEPS - 1:
                out[here, wide] = value
            else:
                ref = stream_of(p + 1, o)
                ref[0, 0, 0] = value[:count // 2]
                ref[1, 0, 0] = value[count // 2:]
                if p % 2:
                    cols[p // 2 + 1, r, here, wide] = value
        for where, _, piece in pushes:
            copy_of(piece, where).start()
        if kind == "start":
            for copy in fetch[:-1]:
                copy.wait()

    for name in ORDER:
        run(name)

    def sent(ref, sem):
        pltpu.make_async_copy(ref, ref, sem).wait()

    for p in range(2 * STEPS):
        sent(cols.at[0, pl.ds(0, 15)], row_send.at[p])
    for s in range(STEPS):
        sent(cols.at[s, pl.ds(0, 15)], col_send.at[s])


def local(density, pattern):
    size = density.shape[0]
    tiles = NX * NY
    return pl.pallas_call(
        kernel,
        out_shape=jax.ShapeDtypeStruct(density.shape, f32),
        in_specs=[pl.BlockSpec(memory_space=pltpu.HBM), pl.BlockSpec(memory_space=pltpu.HBM)],
        out_specs=pl.BlockSpec(memory_space=pltpu.VMEM),
        scratch_shapes=[
            pltpu.VMEM((3 * STEPS, 2, NY, NX, size // 4, size), f32),
            pltpu.VMEM((2 * STEPS, 2, NY, NX, size // 4, size // 2), f32),
            pltpu.VMEM((STEPS, tiles, size, size), f32),
            pltpu.VMEM((STEPS, tiles, size, size), bf16),
            pltpu.VMEM((STEPS, tiles, size, size), bf16),
            pltpu.VMEM((2 * STEPS, size, size), f32),
            pltpu.SMEM(pattern.shape, jnp.int32),
            pltpu.SemaphoreType.DMA((2 * STEPS,)),
            pltpu.SemaphoreType.DMA((len(ROW),)),
            pltpu.SemaphoreType.DMA((STEPS,)),
            pltpu.SemaphoreType.DMA((len(COL),)),
            pltpu.SemaphoreType.DMA((6,)),
        ],
        compiler_params=pltpu.CompilerParams(
            collective_id=0, has_side_effects=True, vmem_limit_bytes=53 * 1024 * 1024 + 512 * 1024),
    )(pattern, density)


def solution(mesh):
    placed = P("row", "col")
    return jax.shard_map(local, mesh=mesh, in_specs=(placed, placed), out_specs=placed, check_vma=False)
```

```python
import heapq

import jax
import jax.numpy as jnp
from jax import lax
from jax.experimental import pallas as pl
from jax.experimental.pallas import tpu as pltpu
from jax.sharding import PartitionSpec as P

BLOCK = 128
STEPS = 2
NX, NY, NZ = 4, 4, 8
MESH = pl.DeviceIdType.MESH
f32, bf16 = jnp.float32, jnp.bfloat16
OFFSETS = [(dx, dy) for dx in (0, 1, -1, 2) for dy in (0, 1, -1, 2)]
RING = (0, 1, -1, 2, -2, 3, -3, 4)

GROUPS = {}
BEGIN_ROWS = [(0, "g1"), (1, "g1")]
COL_SIZE = 1.0
BEGIN_COLS = {}
LATER_COLS = {}
DIRECT = set()
BEGIN = [(0, "g1"), (1, "g1")]

ROWS64, HOP, SMALL, DOT, DOT_TILE = 1.4, 2.2, 0.02, 0.1, 0.1
NEAR_FIRST = [
    [(0, 0), (1, 0), (-1, 0), (0, 1), (0, -1)],
    [(2, 0), (0, 2), (1, 1), (1, -1), (-1, 1), (-1, -1)],
    [(1, 2), (-1, 2), (2, 1), (2, -1)],
    [(2, 2)],
]
COL_GROUPS = [[0], [1, -1], [2, -2], [3, -3], [4]]


HALVES = [(0, 128, 0, 256), (128, 128, 0, 256)]
SQUARE = [(0, 128, 0, 128), (0, 128, 128, 128), (128, 128, 0, 256)]
STREAMS = [HALVES, SQUARE, HALVES, SQUARE, HALVES]
COLUMNS = [(0, 128, 0, 128), (128, 128, 0, 128), (0, 128, 128, 128), (128, 128, 128, 128)]
SLOTS = (0, 1, -1, 2)
SETS = [((0, 1), (1, 2), (3, 1)), ((0, 1), (1, 3))]
SET_CHOICE = [[0, 0], [0, 0, 0], [0, 0], [0, 0, 0]]
FAR = [(0, 1, 0), (0, 1)]


def sets_of(p, h):
    return SETS[SET_CHOICE[p][h]]


def far_sign(p, h, plan, group=None):
    turn = 0 if group is None else FAR[SET_CHOICE[p][h]][group]
    return 1 if (h + plan + turn) % 2 == 0 else -1


def group_of(p, h, a):
    slot = SLOTS.index(a)
    return next(n for n, (first, count) in enumerate(sets_of(p, h)) if first <= slot < first + count)


def row_tile(p, h, plan, a, b):
    if (a, b) == (0, 0):
        return []
    return [("row", p, h, plan, a if b == 0 else "g%d" % group_of(p, h, a), b)]


def col_tile(s, t, dz, other):
    if other:
        return [("col", s, t, dz, "s")]
    if dz == 0:
        return []
    return [("col", s, t, dz, part) for part in (("q0", "q1") if dz == 4 else ("h",))]


def make_jobs():
    jobs = {}

    def link(plan, axis, sign):
        return ("x" if (axis == 0) == (plan == 0) else "y", sign)

    def row_size(p, h):
        return STREAMS[p][h][1] * STREAMS[p][h][3] / (128 * 256)

    def own_row(p, h):
        pushes = []
        for axis in (0, 1):
            for plan in (0, 1):
                for sign in (1, -1):
                    a, b = (sign, 0) if axis == 0 else ("g0", sign)
                    pushes.append((link(plan, axis, sign), row_size(p, h), ("row", p, h, plan, a, b)))
        return pushes

    def own_col(s, ts):
        pushes = []
        for t in ts:
            pushes += [(("z", step), COL_SIZE, ("col", s, t, step, "h")) for step in ((1, -1, 2, -2) if (s, t) in DIRECT else (1, -1))]
        return pushes + [(("core", 0), 0.15, ("col", s, t, 0, "s")) for t in ts]

    def overlap(one, other):
        return all(one[i] < other[i] + other[i + 1] and other[i] < one[i] + one[i + 1] for i in (0, 2))

    def add(name, priority, cost, needs, pushes=()):
        jobs[name] = (priority, cost + SMALL * (len(pushes) + len(needs)), needs, list(pushes))

    add(("start",), 0, SMALL, [], own_row(0, 0) + own_col(0, [t for t in range(4) if t not in BEGIN_COLS]))
    add(("begin", 0, 1), 0, 0, [("turn", 0, 0, *key) for key in BEGIN_ROWS], own_row(0, 1))
    for t, (behind, dz) in BEGIN_COLS.items():
        add(("begin_col", t), 0, 0, [("ring", 0, behind, sign * dz) for sign in (1, -1)], own_col(0, (t,)))
    for t, (behind, dz) in LATER_COLS.items():
        begun = ("final", 1, COLUMNS[t][0] // 128)
        add(("later_col", t), 0, 0, [begun] + [("ring", 1, behind, sign * dz) for sign in (1, -1)], own_col(1, (t,)))
    for p in range(2 * STEPS):
        s = p // 2
        for h, stream in enumerate(STREAMS[p]):
            size = row_size(p, h)
            for plan in (0, 1):
                for sign in (1, -1):
                    pushes = []
                    if sign == far_sign(p, h, plan):
                        pushes = [(link(plan, 0, sign), size, ("row", p, h, plan, 2, 0))]
                        add(("turn", p, h, plan, sign), 0, 0, row_tile(p, h, plan, sign, 0), pushes)
                for g, (first, count) in enumerate(sets_of(p, h)):
                    if g:
                        needs = [piece for a in SLOTS[first:first + count] for piece in row_tile(p, h, plan, a, 0)]
                        add(("turn", p, h, plan, "g%d" % g), 0, 0, needs, [
                            (link(plan, 1, turn), size * count, ("row", p, h, plan, "g%d" % g, turn)) for turn in (1, -1)])
                    sign = far_sign(p, h, plan, g)
                    add(("pass", p, h, plan, "g%d" % g), 0, 0, [("row", p, h, plan, "g%d" % g, sign)],
                        [(link(plan, 1, sign), size * count, ("row", p, h, plan, "g%d" % g, 2))])
        if p % 2 == 0:
            for t, dz in ((t, dz) for dz in RING for t in range(4)):
                pushes = []
                if dz:
                    sign = 1 if dz > 0 else -1
                    if (s, t) in DIRECT:
                        if abs(dz) == 2:
                            pushes.append((("z", sign), COL_SIZE, ("col", s, t, dz + sign, "h")))
                            pushes.append((("z", 2 * sign), COL_SIZE / 2, ("col", s, t, 4, "q0" if sign == 1 else "q1")))
                    elif abs(dz) < 3:
                        pushes.append((("z", sign), COL_SIZE, ("col", s, t, dz + sign, "h")))
                    elif dz != 4:
                        pushes.append((("z", sign), COL_SIZE / 2, ("col", s, t, 4, "q0" if sign == 1 else "q1")))
                    pushes.append((("core", 0), 0.15, ("col", s, t, dz, "s")))
                    add(("ring", s, t, dz), 0, 0, col_tile(s, t, dz, False), pushes)
                before = [("ring", s, t, dz)] if dz else [("start",) if p == 0 else ("final", p - 1, t % 2)]
                add(("split", s, t, dz, False), 2, SMALL, before)
                add(("split", s, t, dz, True), 2, SMALL, col_tile(s, t, dz, True))
        for o, target in enumerate(STREAMS[p + 1]):
            rows_used = [h for h, stream in enumerate(STREAMS[p]) if overlap(stream, (target[0], target[1], 0, 256))]
            cols_used = [t for t, col in enumerate(COLUMNS) if overlap(col, (0, 256, target[2], target[3]))]
            pieces = {key: [piece for h in rows_used
                            for piece in row_tile(p, h, 0, *key) + row_tile(p, h, 1, *key[::-1])] for key in OFFSETS}
            starts = [("start",) if p == 0 else ("final", p - 1, h) for h in rows_used]
            if p % 2 == 0 and target[0] == 0:
                need = [piece for key in OFFSETS for piece in pieces[key]] + starts
                groups = [[(dz, other) for dz in group for other in (False, True)] for group in COL_GROUPS]
                needs = [need + [("split", s, t, *key) for t in cols_used for key in group] for group in groups]
            else:
                groups = NEAR_FIRST
                need = [("split", s, t, dz, other) for t in cols_used for dz in RING for other in (False, True)]
                needs = [[piece for key in group for piece in pieces[key]] + starts + (need if p % 2 == 0 else [])
                         for group in groups]
            for n, group in enumerate(groups):
                cost = DOT + DOT_TILE * len(group) * (0.6 if target[3] == 128 else 1)
                jobs[("mac", p, o, n)] = (4 + p, cost, needs[n], [])
                GROUPS[p, o, n] = group
            pushes = []
            if p < 2 * STEPS - 1:
                pushes = own_row(p + 1, o) + (own_col(s + 1, [t for t in (o, 2 + o) if t not in LATER_COLS]) if p % 2 else [])
            macs = [("mac", p, o, n) for n in range(len(groups))]
            if p % 2 == 0 and o == 2:
                add(("final", p, o), 1, 2 * SMALL, macs)
                add(("begin", p, o), 1, 0, [("final", p, o)] + [("turn", p + 1, 1, *key) for key in BEGIN], pushes)
            else:
                add(("final", p, o), 1, 2 * SMALL, macs, pushes)
    return jobs


def make_order(jobs):
    ready_at, missing, users = {}, {}, {}
    for name, (_, _, needs, _) in jobs.items():
        missing[name] = len(set(needs))
        ready_at[name] = 0.0
        for need in set(needs):
            users.setdefault(need, []).append(name)
    waiting, ready, free = [], [], {}
    rank = {name: n for n, name in enumerate(jobs)}

    def done(thing, when):
        for user in users.get(thing, ()):
            missing[user] -= 1
            ready_at[user] = max(ready_at[user], when)
            if missing[user] == 0:
                heapq.heappush(waiting, (ready_at[user], rank[user], user))

    for name in jobs:
        if missing[name] == 0:
            heapq.heappush(waiting, (0.0, rank[name], name))
    now, order, times = 0.0, [], {}
    while waiting or ready:
        if not ready and waiting[0][0] > now:
            now = waiting[0][0]
        while waiting and waiting[0][0] <= now:
            when, number, name = heapq.heappop(waiting)
            heapq.heappush(ready, (jobs[name][0], when, number, name))
        name = heapq.heappop(ready)[-1]
        _, cost, _, pushes = jobs[name]
        now += cost
        order.append(name)
        times[name] = now
        for (axis, steps), amount, piece in pushes:
            way = axis, steps > 0
            free[way] = max(free.get(way, 0.0), now) + amount * max(1, abs(steps)) * ROWS64
            done(piece, free[way] + HOP)
        done(name, now)
    return order, times


JOBS = make_jobs()
ORDER, TIMES = make_order(JOBS)
PIECES = [piece for name in JOBS for _, _, piece in JOBS[name][3]]
ROW = {name: n for n, name in enumerate(piece for piece in PIECES if piece[0] == "row")}
COL = {name: n for n, name in enumerate(piece for piece in PIECES if piece[0] == "col")}


def split(value):
    high = value.astype(bf16)
    return high, (value - high.astype(f32)).astype(bf16)


def kernel(pattern_in, density, out, wide_rows, half_rows, cols, col_hi, col_lo, acc, pattern,
           row_send, row_recv, col_send, col_recv, local_sem):
    size = density.shape[0]
    r, c = lax.axis_index("row"), lax.axis_index("col")
    z, core = r // 2, r % 2
    y, x = c // NX, c % NX

    def device(dx=0, dy=0, dz=0):
        return (((z + dz + NZ) % NZ) * 2 + core, ((y + dy + NY) % NY) * NX + (x + dx + NX) % NX)

    sibling = (z * 2 + 1 - core, c)

    mirror = 1 - 2 * core

    def k_row(dx, dy):
        return ((y - dy * mirror + NY) % NY) * NX + (x - dx * mirror + NX) % NX

    def k_col(dz, other):
        return ((z - dz + NZ) % NZ) * 2 + (1 - core if other else core)

    def stream_of(p, h):
        before = [h_ for p_ in range(4) for h_, other in enumerate(STREAMS[p_])
                  if (p_, h_) < (p, h) and other[3] == STREAMS[p][h][3]]
        return (wide_rows if STREAMS[p][h][3] == size else half_rows).at[len(before)]

    step_rows = HALVES[0][1] // 2
    fetch = [
        pltpu.make_async_copy(density.at[pl.ds((2 * h + plan) * step_rows, step_rows)], stream_of(0, h).at[plan, 0, 0],
                              local_sem.at[2 * h + plan])
        for h in (0, 1) for plan in (0, 1)]
    fetch += [
        pltpu.make_async_copy(density, cols.at[0, r], local_sem.at[4]),
        pltpu.make_async_copy(pattern_in, pattern, local_sem.at[5]),
    ]
    for copy in fetch:
        copy.start()

    peers = [device(dx=1), device(dx=-1), device(dy=1), device(dy=-1), sibling]
    peers += [device(dz=step) for step in ((1, -1, 2, -2) if DIRECT else (1, -1))]
    barrier = pltpu.get_barrier_semaphore()
    for peer in peers:
        pl.semaphore_signal(barrier, inc=1, device_id=peer, device_id_type=MESH)
    pl.semaphore_wait(barrier, len(peers))
    mask = []

    def masked(value, low, lane):
        if not mask:
            fetch[-1].wait()
            mask.extend([pattern[a, b].astype(f32) for b in range(2)] for a in range(2))
        parts = [value[:, n:n + BLOCK] * mask[low // BLOCK][(lane + n) // BLOCK] for n in range(0, value.shape[1], BLOCK)]
        return jnp.concatenate(parts, axis=1)

    def slot_of(distance):
        return distance + distance // 2 - 2 * (distance // 3)

    def gathered(p, low, dx, dy):
        parts = []
        for h, stream in enumerate(STREAMS[p]):
            if stream[0] == low:
                ref = stream_of(p, h)
                parts.append(jnp.concatenate([ref[0, slot_of(dy), slot_of(dx)], ref[1, slot_of(dx), slot_of(dy)]], axis=0))
        return parts[0] if len(parts) == 1 else jnp.concatenate(parts, axis=1)

    def remote(src, dst, send, recv, target):
        return pltpu.make_async_remote_copy(
            src_ref=src, dst_ref=dst, send_sem=send, recv_sem=recv, device_id=target, device_id_type=MESH)

    def row_copy(piece, where):
        _, p, h, plan, a, b = piece
        ref = stream_of(p, h).at[plan]
        moved = a if b == 0 else b
        held = SLOTS.index(0 if abs(moved) == 1 else where[1]) if where else SLOTS.index(moved)
        if b == 0:
            src, dst = ref.at[0, held], ref.at[0, SLOTS.index(a)]
        else:
            first, count = sets_of(p, h)[int(a[1])]
            here = pl.ds(first, count) if count > 1 else first
            src, dst = ref.at[held, here], ref.at[SLOTS.index(b), here]
        if where and p == 0 and held == 0 and (b == 0 or a == "g0"):
            src = density.at[pl.ds((2 * h + plan) * step_rows, step_rows)]
        target = device(**{"d" + where[0]: where[1] * mirror}) if where else sibling
        return remote(src, dst, row_send.at[p], row_recv.at[ROW[piece]], target)

    def col_copy(piece, where):
        _, s, t, dz, part = piece
        low, count, lane, lanes = COLUMNS[t]
        if part in ("q0", "q1"):
            count //= 2
            low += count if part == "q1" else 0
        if not where:
            held, target = k_col(dz, part == "s"), sibling
        elif where[0] == "core":
            held, target = k_col(dz, False), sibling
        else:
            held, target = k_col(dz - where[1], False), device(dz=where[1])
        here = pl.ds(low, count), pl.ds(lane, lanes)
        ref = cols.at[s, held, *here]
        if where and s == 0 and dz in ((0,) if where[0] == "core" else (where[1],)):
            return remote(density.at[*here], ref, col_send.at[s], col_recv.at[COL[piece]], target)
        return remote(ref, ref, col_send.at[s], col_recv.at[COL[piece]], target)

    def copy_of(piece, where=None):
        return (row_copy if piece[0] == "row" else col_copy)(piece, where)

    waited, begun = set(), set()

    def run(name):
        _, _, needs, pushes = JOBS[name]
        for need in needs:
            if need[0] in ("row", "col") and need not in waited:
                waited.add(need)
                copy_of(need).wait_recv()
        kind = name[0]
        if kind == "split":
            _, s, t, dz, other = name
            k = k_col(dz, other)
            here = pl.ds(*COLUMNS[t][:2]), pl.ds(*COLUMNS[t][2:])
            high, low = split(cols[s, k, *here])
            col_hi[s, k, *here] = high
            col_lo[s, k, *here] = low
        elif kind == "mac":
            _, p, o = name[:3]
            low, count, lane, lanes = STREAMS[p + 1][o]
            here, wide = pl.ds(low, count), pl.ds(lane, lanes)
            keys = GROUPS[name[1:]]
            if isinstance(keys[0][1], bool):
                places = [k_col(*key) for key in keys]
                steps = [(((x - k % NX) * mirror + NX) % NX, ((y - k // NX) * mirror + NY) % NY) for k in places]
            else:
                places = [k_row(*key) for key in keys]
                steps = [(dx % NX, dy % NY) for dx, dy in keys]
            high_a, low_a = split(jnp.concatenate([gathered(p, low, *step) for step in steps], axis=1))
            high_b = jnp.concatenate([col_hi[p // 2, k, :, wide] for k in places], axis=0)
            low_b = jnp.concatenate([col_lo[p // 2, k, :, wide] for k in places], axis=0)
            both = jnp.dot(jnp.concatenate([high_a, low_a], axis=0), high_b, preferred_element_type=f32)
            term = both[:count] + both[count:] + jnp.dot(high_a, low_b, preferred_element_type=f32)
            if (p, o) in begun:
                acc[p, here, wide] += term
            else:
                begun.add((p, o))
                acc[p, here, wide] = term
        elif kind == "final":
            _, p, o = name
            low, count, lane, lanes = STREAMS[p + 1][o]
            here, wide = pl.ds(low, count), pl.ds(lane, lanes)
            value = masked(acc[p, here, wide], low, lane)
            if p % 2:
                value = 3.0 * gathered(p, low, 0, 0) - 2.0 * value
            if p == 2 * STEPS - 1:
                out[here, wide] = value
            else:
                ref = stream_of(p + 1, o)
                ref[0, 0, 0] = value[:count // 2]
                ref[1, 0, 0] = value[count // 2:]
                if p % 2:
                    cols[p // 2 + 1, r, here, wide] = value
        for where, _, piece in pushes:
            copy_of(piece, where).start()
        if kind == "start":
            for copy in fetch[:-1]:
                copy.wait()

    for name in ORDER:
        run(name)

    def sent(ref, sem):
        pltpu.make_async_copy(ref, ref, sem).wait()

    for p in range(2 * STEPS):
        sent(cols.at[0, pl.ds(0, 15)], row_send.at[p])
    for s in range(STEPS):
        sent(cols.at[s, pl.ds(0, 15)], col_send.at[s])


def local(density, pattern):
    size = density.shape[0]
    tiles = NX * NY
    return pl.pallas_call(
        kernel,
        out_shape=jax.ShapeDtypeStruct(density.shape, f32),
        in_specs=[pl.BlockSpec(memory_space=pltpu.HBM), pl.BlockSpec(memory_space=pltpu.HBM)],
        out_specs=pl.BlockSpec(memory_space=pltpu.VMEM),
        scratch_shapes=[
            pltpu.VMEM((3 * STEPS, 2, NY, NX, size // 4, size), f32),
            pltpu.VMEM((2 * STEPS, 2, NY, NX, size // 4, size // 2), f32),
            pltpu.VMEM((STEPS, tiles, size, size), f32),
            pltpu.VMEM((STEPS, tiles, size, size), bf16),
            pltpu.VMEM((STEPS, tiles, size, size), bf16),
            pltpu.VMEM((2 * STEPS, size, size), f32),
            pltpu.SMEM(pattern.shape, jnp.int32),
            pltpu.SemaphoreType.DMA((2 * STEPS,)),
            pltpu.SemaphoreType.DMA((len(ROW),)),
            pltpu.SemaphoreType.DMA((STEPS,)),
            pltpu.SemaphoreType.DMA((len(COL),)),
            pltpu.SemaphoreType.DMA((6,)),
        ],
        compiler_params=pltpu.CompilerParams(
            collective_id=0, has_side_effects=True, vmem_limit_bytes=53 * 1024 * 1024 + 512 * 1024),
    )(pattern, density)


def solution(mesh):
    placed = P("row", "col")
    return jax.shard_map(local, mesh=mesh, in_specs=(placed, placed), out_specs=placed, check_vma=False)
```

```python
import heapq

import jax
import jax.numpy as jnp
from jax import lax
from jax.experimental import pallas as pl
from jax.experimental.pallas import tpu as pltpu
from jax.sharding import PartitionSpec as P

BLOCK = 128
STEPS = 2
NX, NY, NZ = 4, 4, 8
MESH = pl.DeviceIdType.MESH
f32, bf16 = jnp.float32, jnp.bfloat16
OFFSETS = [(dx, dy) for dx in (0, 1, -1, 2) for dy in (0, 1, -1, 2)]
RING = (0, 1, -1, 2, -2, 3, -3, 4)

GROUPS = {}
BEGIN_ROWS = [(0, "g1"), (1, "g1")]
COL_SIZE = 1.0
BEGIN_COLS = {}
LATER_COLS = {}
DIRECT = set()
BEGIN = [(0, "g1"), (1, "g1")]

ROWS64, HOP, SMALL, DOT, DOT_TILE = 1.4, 2.2, 0.02, 0.1, 0.1
NEAR_FIRST = [
    [(0, 0), (1, 0), (-1, 0)], [(0, 1), (0, -1)],
    [(2, 0), (0, 2)], [(1, 1), (1, -1), (-1, 1), (-1, -1)],
    [(1, 2), (-1, 2)], [(2, 1), (2, -1)],
    [(2, 2)],
]
COL_GROUPS = [[0], [1, -1], [2, -2], [3, -3], [4]]


HALVES = [(0, 128, 0, 256), (128, 128, 0, 256)]
SQUARE = [(0, 128, 0, 128), (0, 128, 128, 128), (128, 128, 0, 256)]
STREAMS = [HALVES, SQUARE, HALVES, SQUARE, HALVES]
COLUMNS = [(0, 128, 0, 128), (128, 128, 0, 128), (0, 128, 128, 128), (128, 128, 128, 128)]
SLOTS = (0, 1, -1, 2)
SETS = [((0, 1), (1, 1), (2, 1), (3, 1)), ((0, 1), (1, 3))]
SET_CHOICE = [[0, 0], [0, 0, 0], [0, 0], [0, 0, 0]]
FAR = [(0, 1, 0, 1), (0, 1)]


def sets_of(p, h):
    return SETS[SET_CHOICE[p][h]]


def far_sign(p, h, plan, group=None):
    turn = 0 if group is None else FAR[SET_CHOICE[p][h]][group]
    return 1 if (h + plan + turn) % 2 == 0 else -1


def group_of(p, h, a):
    slot = SLOTS.index(a)
    return next(n for n, (first, count) in enumerate(sets_of(p, h)) if first <= slot < first + count)


def row_tile(p, h, plan, a, b):
    if (a, b) == (0, 0):
        return []
    return [("row", p, h, plan, a if b == 0 else "g%d" % group_of(p, h, a), b)]


def col_tile(s, t, dz, other):
    if other:
        return [("col", s, t, dz, "s")]
    if dz == 0:
        return []
    return [("col", s, t, dz, part) for part in (("q0", "q1") if dz == 4 else ("h",))]


def make_jobs():
    jobs = {}

    def link(plan, axis, sign):
        return ("x" if (axis == 0) == (plan == 0) else "y", sign)

    def row_size(p, h):
        return STREAMS[p][h][1] * STREAMS[p][h][3] / (128 * 256)

    def own_row(p, h):
        pushes = []
        for axis in (0, 1):
            for plan in (0, 1):
                for sign in (1, -1):
                    a, b = (sign, 0) if axis == 0 else ("g0", sign)
                    pushes.append((link(plan, axis, sign), row_size(p, h), ("row", p, h, plan, a, b)))
        return pushes

    def own_col(s, ts):
        pushes = []
        for t in ts:
            pushes += [(("z", step), COL_SIZE, ("col", s, t, step, "h")) for step in ((1, -1, 2, -2) if (s, t) in DIRECT else (1, -1))]
        return pushes + [(("core", 0), 0.15, ("col", s, t, 0, "s")) for t in ts]

    def overlap(one, other):
        return all(one[i] < other[i] + other[i + 1] and other[i] < one[i] + one[i + 1] for i in (0, 2))

    def add(name, priority, cost, needs, pushes=()):
        jobs[name] = (priority, cost + SMALL * (len(pushes) + len(needs)), needs, list(pushes))

    add(("start",), 0, SMALL, [], own_row(0, 0) + own_col(0, [t for t in range(4) if t not in BEGIN_COLS]))
    add(("begin", 0, 1), 0, 0, [("turn", 0, 0, *key) for key in BEGIN_ROWS], own_row(0, 1))
    for t, (behind, dz) in BEGIN_COLS.items():
        add(("begin_col", t), 0, 0, [("ring", 0, behind, sign * dz) for sign in (1, -1)], own_col(0, (t,)))
    for t, (behind, dz) in LATER_COLS.items():
        begun = ("final", 1, COLUMNS[t][0] // 128)
        add(("later_col", t), 0, 0, [begun] + [("ring", 1, behind, sign * dz) for sign in (1, -1)], own_col(1, (t,)))
    for p in range(2 * STEPS):
        s = p // 2
        for h, stream in enumerate(STREAMS[p]):
            size = row_size(p, h)
            for plan in (0, 1):
                for sign in (1, -1):
                    pushes = []
                    if sign == far_sign(p, h, plan):
                        pushes = [(link(plan, 0, sign), size, ("row", p, h, plan, 2, 0))]
                        add(("turn", p, h, plan, sign), 0, 0, row_tile(p, h, plan, sign, 0), pushes)
                for g, (first, count) in enumerate(sets_of(p, h)):
                    if g:
                        needs = [piece for a in SLOTS[first:first + count] for piece in row_tile(p, h, plan, a, 0)]
                        add(("turn", p, h, plan, "g%d" % g), 0, 0, needs, [
                            (link(plan, 1, turn), size * count, ("row", p, h, plan, "g%d" % g, turn)) for turn in (1, -1)])
                    sign = far_sign(p, h, plan, g)
                    add(("pass", p, h, plan, "g%d" % g), 0, 0, [("row", p, h, plan, "g%d" % g, sign)],
                        [(link(plan, 1, sign), size * count, ("row", p, h, plan, "g%d" % g, 2))])
        if p % 2 == 0:
            for t, dz in ((t, dz) for dz in RING for t in range(4)):
                pushes = []
                if dz:
                    sign = 1 if dz > 0 else -1
                    if (s, t) in DIRECT:
                        if abs(dz) == 2:
                            pushes.append((("z", sign), COL_SIZE, ("col", s, t, dz + sign, "h")))
                            pushes.append((("z", 2 * sign), COL_SIZE / 2, ("col", s, t, 4, "q0" if sign == 1 else "q1")))
                    elif abs(dz) < 3:
                        pushes.append((("z", sign), COL_SIZE, ("col", s, t, dz + sign, "h")))
                    elif dz != 4:
                        pushes.append((("z", sign), COL_SIZE / 2, ("col", s, t, 4, "q0" if sign == 1 else "q1")))
                    pushes.append((("core", 0), 0.15, ("col", s, t, dz, "s")))
                    add(("ring", s, t, dz), 0, 0, col_tile(s, t, dz, False), pushes)
                before = [("ring", s, t, dz)] if dz else [("start",) if p == 0 else ("final", p - 1, t % 2)]
                add(("split", s, t, dz, False), 2, SMALL, before)
                add(("split", s, t, dz, True), 2, SMALL, col_tile(s, t, dz, True))
        for o, target in enumerate(STREAMS[p + 1]):
            rows_used = [h for h, stream in enumerate(STREAMS[p]) if overlap(stream, (target[0], target[1], 0, 256))]
            cols_used = [t for t, col in enumerate(COLUMNS) if overlap(col, (0, 256, target[2], target[3]))]
            pieces = {key: [piece for h in rows_used
                            for piece in row_tile(p, h, 0, *key) + row_tile(p, h, 1, *key[::-1])] for key in OFFSETS}
            starts = [("start",) if p == 0 else ("final", p - 1, h) for h in rows_used]
            if p % 2 == 0 and target[0] == 0:
                need = [piece for key in OFFSETS for piece in pieces[key]] + starts
                groups = [[(dz, other) for dz in group for other in (False, True)] for group in COL_GROUPS]
                needs = [need + [("split", s, t, *key) for t in cols_used for key in group] for group in groups]
            else:
                groups = NEAR_FIRST
                need = [("split", s, t, dz, other) for t in cols_used for dz in RING for other in (False, True)]
                needs = [[piece for key in group for piece in pieces[key]] + starts + (need if p % 2 == 0 else [])
                         for group in groups]
            for n, group in enumerate(groups):
                cost = DOT + DOT_TILE * len(group) * (0.6 if target[3] == 128 else 1)
                jobs[("mac", p, o, n)] = (4 + p, cost, needs[n], [])
                GROUPS[p, o, n] = group
            pushes = []
            if p < 2 * STEPS - 1:
                pushes = own_row(p + 1, o) + (own_col(s + 1, [t for t in (o, 2 + o) if t not in LATER_COLS]) if p % 2 else [])
            macs = [("mac", p, o, n) for n in range(len(groups))]
            if p % 2 == 0 and o == 2:
                add(("final", p, o), 1, 2 * SMALL, macs)
                add(("begin", p, o), 1, 0, [("final", p, o)] + [("turn", p + 1, 1, *key) for key in BEGIN], pushes)
            else:
                add(("final", p, o), 1, 2 * SMALL, macs, pushes)
    return jobs


def make_order(jobs):
    ready_at, missing, users = {}, {}, {}
    for name, (_, _, needs, _) in jobs.items():
        missing[name] = len(set(needs))
        ready_at[name] = 0.0
        for need in set(needs):
            users.setdefault(need, []).append(name)
    waiting, ready, free = [], [], {}
    rank = {name: n for n, name in enumerate(jobs)}

    def done(thing, when):
        for user in users.get(thing, ()):
            missing[user] -= 1
            ready_at[user] = max(ready_at[user], when)
            if missing[user] == 0:
                heapq.heappush(waiting, (ready_at[user], rank[user], user))

    for name in jobs:
        if missing[name] == 0:
            heapq.heappush(waiting, (0.0, rank[name], name))
    now, order, times = 0.0, [], {}
    while waiting or ready:
        if not ready and waiting[0][0] > now:
            now = waiting[0][0]
        while waiting and waiting[0][0] <= now:
            when, number, name = heapq.heappop(waiting)
            heapq.heappush(ready, (jobs[name][0], when, number, name))
        name = heapq.heappop(ready)[-1]
        _, cost, _, pushes = jobs[name]
        now += cost
        order.append(name)
        times[name] = now
        for (axis, steps), amount, piece in pushes:
            way = axis, steps > 0
            free[way] = max(free.get(way, 0.0), now) + amount * max(1, abs(steps)) * ROWS64
            done(piece, free[way] + HOP)
        done(name, now)
    return order, times


JOBS = make_jobs()
ORDER, TIMES = make_order(JOBS)
PIECES = [piece for name in JOBS for _, _, piece in JOBS[name][3]]
ROW = {name: n for n, name in enumerate(piece for piece in PIECES if piece[0] == "row")}
COL = {name: n for n, name in enumerate(piece for piece in PIECES if piece[0] == "col")}


def split(value):
    high = value.astype(bf16)
    return high, (value - high.astype(f32)).astype(bf16)


def kernel(pattern_in, density, out, wide_rows, half_rows, cols, col_hi, col_lo, acc, pattern,
           row_send, row_recv, col_send, col_recv, local_sem):
    size = density.shape[0]
    r, c = lax.axis_index("row"), lax.axis_index("col")
    z, core = r // 2, r % 2
    y, x = c // NX, c % NX

    def device(dx=0, dy=0, dz=0):
        return (((z + dz + NZ) % NZ) * 2 + core, ((y + dy + NY) % NY) * NX + (x + dx + NX) % NX)

    sibling = (z * 2 + 1 - core, c)

    mirror = 1 - 2 * core

    def k_row(dx, dy):
        return ((y - dy * mirror + NY) % NY) * NX + (x - dx * mirror + NX) % NX

    def k_col(dz, other):
        return ((z - dz + NZ) % NZ) * 2 + (1 - core if other else core)

    def stream_of(p, h):
        before = [h_ for p_ in range(4) for h_, other in enumerate(STREAMS[p_])
                  if (p_, h_) < (p, h) and other[3] == STREAMS[p][h][3]]
        return (wide_rows if STREAMS[p][h][3] == size else half_rows).at[len(before)]

    step_rows = HALVES[0][1] // 2
    fetch = [
        pltpu.make_async_copy(density.at[pl.ds((2 * h + plan) * step_rows, step_rows)], stream_of(0, h).at[plan, 0, 0],
                              local_sem.at[2 * h + plan])
        for h in (0, 1) for plan in (0, 1)]
    fetch += [
        pltpu.make_async_copy(density, cols.at[0, r], local_sem.at[4]),
        pltpu.make_async_copy(pattern_in, pattern, local_sem.at[5]),
    ]
    for copy in fetch:
        copy.start()

    peers = [device(dx=1), device(dx=-1), device(dy=1), device(dy=-1), sibling]
    peers += [device(dz=step) for step in ((1, -1, 2, -2) if DIRECT else (1, -1))]
    barrier = pltpu.get_barrier_semaphore()
    for peer in peers:
        pl.semaphore_signal(barrier, inc=1, device_id=peer, device_id_type=MESH)
    pl.semaphore_wait(barrier, len(peers))
    mask = []

    def masked(value, low, lane):
        if not mask:
            fetch[-1].wait()
            mask.extend([pattern[a, b].astype(f32) for b in range(2)] for a in range(2))
        parts = [value[:, n:n + BLOCK] * mask[low // BLOCK][(lane + n) // BLOCK] for n in range(0, value.shape[1], BLOCK)]
        return jnp.concatenate(parts, axis=1)

    def slot_of(distance):
        return distance + distance // 2 - 2 * (distance // 3)

    def gathered(p, low, dx, dy):
        parts = []
        for h, stream in enumerate(STREAMS[p]):
            if stream[0] == low:
                ref = stream_of(p, h)
                parts.append(jnp.concatenate([ref[0, slot_of(dy), slot_of(dx)], ref[1, slot_of(dx), slot_of(dy)]], axis=0))
        return parts[0] if len(parts) == 1 else jnp.concatenate(parts, axis=1)

    def remote(src, dst, send, recv, target):
        return pltpu.make_async_remote_copy(
            src_ref=src, dst_ref=dst, send_sem=send, recv_sem=recv, device_id=target, device_id_type=MESH)

    def row_copy(piece, where):
        _, p, h, plan, a, b = piece
        ref = stream_of(p, h).at[plan]
        moved = a if b == 0 else b
        held = SLOTS.index(0 if abs(moved) == 1 else where[1]) if where else SLOTS.index(moved)
        if b == 0:
            src, dst = ref.at[0, held], ref.at[0, SLOTS.index(a)]
        else:
            first, count = sets_of(p, h)[int(a[1])]
            here = pl.ds(first, count) if count > 1 else first
            src, dst = ref.at[held, here], ref.at[SLOTS.index(b), here]
        if where and p == 0 and held == 0 and (b == 0 or a == "g0"):
            src = density.at[pl.ds((2 * h + plan) * step_rows, step_rows)]
        target = device(**{"d" + where[0]: where[1] * mirror}) if where else sibling
        return remote(src, dst, row_send.at[p], row_recv.at[ROW[piece]], target)

    def col_copy(piece, where):
        _, s, t, dz, part = piece
        low, count, lane, lanes = COLUMNS[t]
        if part in ("q0", "q1"):
            count //= 2
            low += count if part == "q1" else 0
        if not where:
            held, target = k_col(dz, part == "s"), sibling
        elif where[0] == "core":
            held, target = k_col(dz, False), sibling
        else:
            held, target = k_col(dz - where[1], False), device(dz=where[1])
        here = pl.ds(low, count), pl.ds(lane, lanes)
        ref = cols.at[s, held, *here]
        if where and s == 0 and dz in ((0,) if where[0] == "core" else (where[1],)):
            return remote(density.at[*here], ref, col_send.at[s], col_recv.at[COL[piece]], target)
        return remote(ref, ref, col_send.at[s], col_recv.at[COL[piece]], target)

    def copy_of(piece, where=None):
        return (row_copy if piece[0] == "row" else col_copy)(piece, where)

    waited, begun = set(), set()

    def run(name):
        _, _, needs, pushes = JOBS[name]
        for need in needs:
            if need[0] in ("row", "col") and need not in waited:
                waited.add(need)
                copy_of(need).wait_recv()
        kind = name[0]
        if kind == "split":
            _, s, t, dz, other = name
            k = k_col(dz, other)
            here = pl.ds(*COLUMNS[t][:2]), pl.ds(*COLUMNS[t][2:])
            high, low = split(cols[s, k, *here])
            col_hi[s, k, *here] = high
            col_lo[s, k, *here] = low
        elif kind == "mac":
            _, p, o = name[:3]
            low, count, lane, lanes = STREAMS[p + 1][o]
            here, wide = pl.ds(low, count), pl.ds(lane, lanes)
            keys = GROUPS[name[1:]]
            if isinstance(keys[0][1], bool):
                places = [k_col(*key) for key in keys]
                steps = [(((x - k % NX) * mirror + NX) % NX, ((y - k // NX) * mirror + NY) % NY) for k in places]
            else:
                places = [k_row(*key) for key in keys]
                steps = [(dx % NX, dy % NY) for dx, dy in keys]
            high_a, low_a = split(jnp.concatenate([gathered(p, low, *step) for step in steps], axis=1))
            high_b = jnp.concatenate([col_hi[p // 2, k, :, wide] for k in places], axis=0)
            low_b = jnp.concatenate([col_lo[p // 2, k, :, wide] for k in places], axis=0)
            both = jnp.dot(jnp.concatenate([high_a, low_a], axis=0), high_b, preferred_element_type=f32)
            term = both[:count] + both[count:] + jnp.dot(high_a, low_b, preferred_element_type=f32)
            if (p, o) in begun:
                acc[p, here, wide] += term
            else:
                begun.add((p, o))
                acc[p, here, wide] = term
        elif kind == "final":
            _, p, o = name
            low, count, lane, lanes = STREAMS[p + 1][o]
            here, wide = pl.ds(low, count), pl.ds(lane, lanes)
            value = masked(acc[p, here, wide], low, lane)
            if p % 2:
                value = 3.0 * gathered(p, low, 0, 0) - 2.0 * value
            if p == 2 * STEPS - 1:
                out[here, wide] = value
            else:
                ref = stream_of(p + 1, o)
                ref[0, 0, 0] = value[:count // 2]
                ref[1, 0, 0] = value[count // 2:]
                if p % 2:
                    cols[p // 2 + 1, r, here, wide] = value
        for where, _, piece in pushes:
            copy_of(piece, where).start()
        if kind == "start":
            for copy in fetch[:-1]:
                copy.wait()

    for name in ORDER:
        run(name)

    def sent(ref, sem):
        pltpu.make_async_copy(ref, ref, sem).wait()

    for p in range(2 * STEPS):
        sent(cols.at[0, pl.ds(0, 15)], row_send.at[p])
    for s in range(STEPS):
        sent(cols.at[s, pl.ds(0, 15)], col_send.at[s])


def local(density, pattern):
    size = density.shape[0]
    tiles = NX * NY
    return pl.pallas_call(
        kernel,
        out_shape=jax.ShapeDtypeStruct(density.shape, f32),
        in_specs=[pl.BlockSpec(memory_space=pltpu.HBM), pl.BlockSpec(memory_space=pltpu.HBM)],
        out_specs=pl.BlockSpec(memory_space=pltpu.VMEM),
        scratch_shapes=[
            pltpu.VMEM((3 * STEPS, 2, NY, NX, size // 4, size), f32),
            pltpu.VMEM((2 * STEPS, 2, NY, NX, size // 4, size // 2), f32),
            pltpu.VMEM((STEPS, tiles, size, size), f32),
            pltpu.VMEM((STEPS, tiles, size, size), bf16),
            pltpu.VMEM((STEPS, tiles, size, size), bf16),
            pltpu.VMEM((2 * STEPS, size, size), f32),
            pltpu.SMEM(pattern.shape, jnp.int32),
            pltpu.SemaphoreType.DMA((2 * STEPS,)),
            pltpu.SemaphoreType.DMA((len(ROW),)),
            pltpu.SemaphoreType.DMA((STEPS,)),
            pltpu.SemaphoreType.DMA((len(COL),)),
            pltpu.SemaphoreType.DMA((6,)),
        ],
        compiler_params=pltpu.CompilerParams(
            collective_id=0, has_side_effects=True, vmem_limit_bytes=53 * 1024 * 1024 + 512 * 1024),
    )(pattern, density)


def solution(mesh):
    placed = P("row", "col")
    return jax.shard_map(local, mesh=mesh, in_specs=(placed, placed), out_specs=placed, check_vma=False)
```

```python
import heapq

import jax
import jax.numpy as jnp
from jax import lax
from jax.experimental import pallas as pl
from jax.experimental.pallas import tpu as pltpu
from jax.sharding import PartitionSpec as P

BLOCK = 128
STEPS = 2
NX, NY, NZ = 4, 4, 8
MESH = pl.DeviceIdType.MESH
f32, bf16 = jnp.float32, jnp.bfloat16
OFFSETS = [(dx, dy) for dx in (0, 1, -1, 2) for dy in (0, 1, -1, 2)]
RING = (0, 1, -1, 2, -2, 3, -3, 4)

GROUPS = {}
AFTER_RING = []
BEGIN_ROWS = [(0, "g2"), (1, "g2")]
COL_SIZE = 1.0
BEGIN_COLS = {2: (1, 1), 3: (1, 2)}
LATER_COLS = {}
DIRECT = set()
BEGIN = [(0, "g1"), (1, "g1")]

ROWS64, HOP, SMALL, DOT, DOT_TILE = 1.4, 2.2, 0.02, 0.1, 0.1
NEAR_FIRST = [
    [(0, 0), (1, 0), (-1, 0), (0, 1), (0, -1)],
    [(2, 0), (0, 2), (1, 1), (1, -1), (-1, 1), (-1, -1)],
    [(1, 2), (-1, 2), (2, 1), (2, -1)],
    [(2, 2)],
]
COL_GROUPS = [[0], [1, -1], [2, -2], [3, -3], [4]]


HALVES = [(0, 128, 0, 256), (128, 128, 0, 256)]
SQUARE = [(0, 128, 0, 128), (0, 128, 128, 128), (128, 128, 0, 256)]
STREAMS = [HALVES, SQUARE, HALVES, SQUARE, HALVES]
COLUMNS = [(0, 128, 0, 128), (128, 128, 0, 128), (0, 128, 128, 128), (128, 128, 128, 128)]
SLOTS = (0, 1, -1, 2)
SETS = [((0, 1), (1, 2), (3, 1)), ((0, 1), (1, 3))]
SET_CHOICE = [[0, 0], [0, 0, 0], [0, 0], [0, 0, 0]]
FAR = [(0, 1, 0), (0, 1)]


def sets_of(p, h):
    return SETS[SET_CHOICE[p][h]]


def far_sign(p, h, plan, group=None):
    turn = 0 if group is None else FAR[SET_CHOICE[p][h]][group]
    return 1 if (h + plan + turn) % 2 == 0 else -1


def group_of(p, h, a):
    slot = SLOTS.index(a)
    return next(n for n, (first, count) in enumerate(sets_of(p, h)) if first <= slot < first + count)


def row_tile(p, h, plan, a, b):
    if (a, b) == (0, 0):
        return []
    return [("row", p, h, plan, a if b == 0 else "g%d" % group_of(p, h, a), b)]


def col_tile(s, t, dz, other):
    if other:
        return [("col", s, t, dz, "s")]
    if dz == 0:
        return []
    return [("col", s, t, dz, part) for part in (("q0", "q1") if dz == 4 else ("h",))]


def make_jobs():
    jobs = {}

    def link(plan, axis, sign):
        return ("x" if (axis == 0) == (plan == 0) else "y", sign)

    def row_size(p, h):
        return STREAMS[p][h][1] * STREAMS[p][h][3] / (128 * 256)

    def own_row(p, h):
        pushes = []
        for axis in (0, 1):
            for plan in (0, 1):
                for sign in (1, -1):
                    a, b = (sign, 0) if axis == 0 else ("g0", sign)
                    pushes.append((link(plan, axis, sign), row_size(p, h), ("row", p, h, plan, a, b)))
        return pushes

    def own_col(s, ts):
        pushes = []
        for t in ts:
            pushes += [(("z", step), COL_SIZE, ("col", s, t, step, "h")) for step in ((1, -1, 2, -2) if (s, t) in DIRECT else (1, -1))]
        return pushes + [(("core", 0), 0.15, ("col", s, t, 0, "s")) for t in ts]

    def overlap(one, other):
        return all(one[i] < other[i] + other[i + 1] and other[i] < one[i] + one[i + 1] for i in (0, 2))

    def add(name, priority, cost, needs, pushes=()):
        jobs[name] = (priority, cost + SMALL * (len(pushes) + len(needs)), needs, list(pushes))

    add(("start",), 0, SMALL, [], own_row(0, 0) + own_col(0, [t for t in range(4) if t not in BEGIN_COLS]))
    add(("begin", 0, 1), 0, 0, [("turn", 0, 0, *key) for key in BEGIN_ROWS] + [("ring", 0, t, dz) for t, dz in AFTER_RING], own_row(0, 1))
    for t, (behind, dz) in BEGIN_COLS.items():
        add(("begin_col", t), 0, 0, [("ring", 0, behind, sign * dz) for sign in (1, -1)], own_col(0, (t,)))
    for t, (behind, dz) in LATER_COLS.items():
        begun = ("final", 1, COLUMNS[t][0] // 128)
        add(("later_col", t), 0, 0, [begun] + [("ring", 1, behind, sign * dz) for sign in (1, -1)], own_col(1, (t,)))
    for p in range(2 * STEPS):
        s = p // 2
        for h, stream in enumerate(STREAMS[p]):
            size = row_size(p, h)
            for plan in (0, 1):
                for sign in (1, -1):
                    pushes = []
                    if sign == far_sign(p, h, plan):
                        pushes = [(link(plan, 0, sign), size, ("row", p, h, plan, 2, 0))]
                        add(("turn", p, h, plan, sign), 0, 0, row_tile(p, h, plan, sign, 0), pushes)
                for g, (first, count) in enumerate(sets_of(p, h)):
                    if g:
                        needs = [piece for a in SLOTS[first:first + count] for piece in row_tile(p, h, plan, a, 0)]
                        add(("turn", p, h, plan, "g%d" % g), 0, 0, needs, [
                            (link(plan, 1, turn), size * count, ("row", p, h, plan, "g%d" % g, turn)) for turn in (1, -1)])
                    sign = far_sign(p, h, plan, g)
                    add(("pass", p, h, plan, "g%d" % g), 0, 0, [("row", p, h, plan, "g%d" % g, sign)],
                        [(link(plan, 1, sign), size * count, ("row", p, h, plan, "g%d" % g, 2))])
        if p % 2 == 0:
            for t, dz in ((t, dz) for dz in RING for t in range(4)):
                pushes = []
                if dz:
                    sign = 1 if dz > 0 else -1
                    if (s, t) in DIRECT:
                        if abs(dz) == 2:
                            pushes.append((("z", sign), COL_SIZE, ("col", s, t, dz + sign, "h")))
                            pushes.append((("z", 2 * sign), COL_SIZE / 2, ("col", s, t, 4, "q0" if sign == 1 else "q1")))
                    elif abs(dz) < 3:
                        pushes.append((("z", sign), COL_SIZE, ("col", s, t, dz + sign, "h")))
                    elif dz != 4:
                        pushes.append((("z", sign), COL_SIZE / 2, ("col", s, t, 4, "q0" if sign == 1 else "q1")))
                    pushes.append((("core", 0), 0.15, ("col", s, t, dz, "s")))
                    add(("ring", s, t, dz), 0, 0, col_tile(s, t, dz, False), pushes)
                before = [("ring", s, t, dz)] if dz else [("start",) if p == 0 else ("final", p - 1, t % 2)]
                add(("split", s, t, dz, False), 2, SMALL, before)
                add(("split", s, t, dz, True), 2, SMALL, col_tile(s, t, dz, True))
        for o, target in enumerate(STREAMS[p + 1]):
            rows_used = [h for h, stream in enumerate(STREAMS[p]) if overlap(stream, (target[0], target[1], 0, 256))]
            cols_used = [t for t, col in enumerate(COLUMNS) if overlap(col, (0, 256, target[2], target[3]))]
            pieces = {key: [piece for h in rows_used
                            for piece in row_tile(p, h, 0, *key) + row_tile(p, h, 1, *key[::-1])] for key in OFFSETS}
            starts = [("start",) if p == 0 else ("final", p - 1, h) for h in rows_used]
            if p % 2 == 0 and target[0] == 0:
                need = [piece for key in OFFSETS for piece in pieces[key]] + starts
                groups = [[(dz, other) for dz in group for other in (False, True)] for group in COL_GROUPS]
                needs = [need + [("split", s, t, *key) for t in cols_used for key in group] for group in groups]
            else:
                groups = NEAR_FIRST
                need = [("split", s, t, dz, other) for t in cols_used for dz in RING for other in (False, True)]
                needs = [[piece for key in group for piece in pieces[key]] + starts + (need if p % 2 == 0 else [])
                         for group in groups]
            for n, group in enumerate(groups):
                cost = DOT + DOT_TILE * len(group) * (0.6 if target[3] == 128 else 1)
                jobs[("mac", p, o, n)] = (4 + p, cost, needs[n], [])
                GROUPS[p, o, n] = group
            pushes = []
            if p < 2 * STEPS - 1:
                pushes = own_row(p + 1, o) + (own_col(s + 1, [t for t in (o, 2 + o) if t not in LATER_COLS]) if p % 2 else [])
            macs = [("mac", p, o, n) for n in range(len(groups))]
            if p % 2 == 0 and o == 2:
                add(("final", p, o), 1, 2 * SMALL, macs)
                add(("begin", p, o), 1, 0, [("final", p, o)] + [("turn", p + 1, 1, *key) for key in BEGIN], pushes)
            else:
                add(("final", p, o), 1, 2 * SMALL, macs, pushes)
    return jobs


def make_order(jobs):
    ready_at, missing, users = {}, {}, {}
    for name, (_, _, needs, _) in jobs.items():
        missing[name] = len(set(needs))
        ready_at[name] = 0.0
        for need in set(needs):
            users.setdefault(need, []).append(name)
    waiting, ready, free = [], [], {}
    rank = {name: n for n, name in enumerate(jobs)}

    def done(thing, when):
        for user in users.get(thing, ()):
            missing[user] -= 1
            ready_at[user] = max(ready_at[user], when)
            if missing[user] == 0:
                heapq.heappush(waiting, (ready_at[user], rank[user], user))

    for name in jobs:
        if missing[name] == 0:
            heapq.heappush(waiting, (0.0, rank[name], name))
    now, order, times = 0.0, [], {}
    while waiting or ready:
        if not ready and waiting[0][0] > now:
            now = waiting[0][0]
        while waiting and waiting[0][0] <= now:
            when, number, name = heapq.heappop(waiting)
            heapq.heappush(ready, (jobs[name][0], when, number, name))
        name = heapq.heappop(ready)[-1]
        _, cost, _, pushes = jobs[name]
        now += cost
        order.append(name)
        times[name] = now
        for (axis, steps), amount, piece in pushes:
            way = axis, steps > 0
            free[way] = max(free.get(way, 0.0), now) + amount * max(1, abs(steps)) * ROWS64
            done(piece, free[way] + HOP)
        done(name, now)
    return order, times


JOBS = make_jobs()
ORDER, TIMES = make_order(JOBS)
PIECES = [piece for name in JOBS for _, _, piece in JOBS[name][3]]
ROW = {name: n for n, name in enumerate(piece for piece in PIECES if piece[0] == "row")}
COL = {name: n for n, name in enumerate(piece for piece in PIECES if piece[0] == "col")}


def split(value):
    high = value.astype(bf16)
    return high, (value - high.astype(f32)).astype(bf16)


def kernel(pattern_in, density, out, wide_rows, half_rows, cols, col_hi, col_lo, acc, pattern,
           row_send, row_recv, col_send, col_recv, local_sem):
    size = density.shape[0]
    r, c = lax.axis_index("row"), lax.axis_index("col")
    z, core = r // 2, r % 2
    y, x = c // NX, c % NX

    def device(dx=0, dy=0, dz=0):
        return (((z + dz + NZ) % NZ) * 2 + core, ((y + dy + NY) % NY) * NX + (x + dx + NX) % NX)

    sibling = (z * 2 + 1 - core, c)

    mirror = 1 - 2 * core

    def k_row(dx, dy):
        return ((y - dy * mirror + NY) % NY) * NX + (x - dx * mirror + NX) % NX

    def k_col(dz, other):
        return ((z - dz + NZ) % NZ) * 2 + (1 - core if other else core)

    def stream_of(p, h):
        before = [h_ for p_ in range(4) for h_, other in enumerate(STREAMS[p_])
                  if (p_, h_) < (p, h) and other[3] == STREAMS[p][h][3]]
        return (wide_rows if STREAMS[p][h][3] == size else half_rows).at[len(before)]

    step_rows = HALVES[0][1] // 2
    fetch = [
        pltpu.make_async_copy(density.at[pl.ds((2 * h + plan) * step_rows, step_rows)], stream_of(0, h).at[plan, 0, 0],
                              local_sem.at[2 * h + plan])
        for h in (0, 1) for plan in (0, 1)]
    fetch += [
        pltpu.make_async_copy(density, cols.at[0, r], local_sem.at[4]),
        pltpu.make_async_copy(pattern_in, pattern, local_sem.at[5]),
    ]
    for copy in fetch:
        copy.start()

    peers = [device(dx=1), device(dx=-1), device(dy=1), device(dy=-1), sibling]
    peers += [device(dz=step) for step in ((1, -1, 2, -2) if DIRECT else (1, -1))]
    barrier = pltpu.get_barrier_semaphore()
    for peer in peers:
        pl.semaphore_signal(barrier, inc=1, device_id=peer, device_id_type=MESH)
    pl.semaphore_wait(barrier, len(peers))
    mask = []

    def masked(value, low, lane):
        if not mask:
            fetch[-1].wait()
            mask.extend([pattern[a, b].astype(f32) for b in range(2)] for a in range(2))
        parts = [value[:, n:n + BLOCK] * mask[low // BLOCK][(lane + n) // BLOCK] for n in range(0, value.shape[1], BLOCK)]
        return jnp.concatenate(parts, axis=1)

    def slot_of(distance):
        return distance + distance // 2 - 2 * (distance // 3)

    def gathered(p, low, dx, dy):
        parts = []
        for h, stream in enumerate(STREAMS[p]):
            if stream[0] == low:
                ref = stream_of(p, h)
                parts.append(jnp.concatenate([ref[0, slot_of(dy), slot_of(dx)], ref[1, slot_of(dx), slot_of(dy)]], axis=0))
        return parts[0] if len(parts) == 1 else jnp.concatenate(parts, axis=1)

    def remote(src, dst, send, recv, target):
        return pltpu.make_async_remote_copy(
            src_ref=src, dst_ref=dst, send_sem=send, recv_sem=recv, device_id=target, device_id_type=MESH)

    def row_copy(piece, where):
        _, p, h, plan, a, b = piece
        ref = stream_of(p, h).at[plan]
        moved = a if b == 0 else b
        held = SLOTS.index(0 if abs(moved) == 1 else where[1]) if where else SLOTS.index(moved)
        if b == 0:
            src, dst = ref.at[0, held], ref.at[0, SLOTS.index(a)]
        else:
            first, count = sets_of(p, h)[int(a[1])]
            here = pl.ds(first, count) if count > 1 else first
            src, dst = ref.at[held, here], ref.at[SLOTS.index(b), here]
        if where and p == 0 and held == 0 and (b == 0 or a == "g0"):
            src = density.at[pl.ds((2 * h + plan) * step_rows, step_rows)]
        target = device(**{"d" + where[0]: where[1] * mirror}) if where else sibling
        return remote(src, dst, row_send.at[p], row_recv.at[ROW[piece]], target)

    def col_copy(piece, where):
        _, s, t, dz, part = piece
        low, count, lane, lanes = COLUMNS[t]
        if part in ("q0", "q1"):
            count //= 2
            low += count if part == "q1" else 0
        if not where:
            held, target = k_col(dz, part == "s"), sibling
        elif where[0] == "core":
            held, target = k_col(dz, False), sibling
        else:
            held, target = k_col(dz - where[1], False), device(dz=where[1])
        here = pl.ds(low, count), pl.ds(lane, lanes)
        ref = cols.at[s, held, *here]
        if where and s == 0 and dz in ((0,) if where[0] == "core" else (where[1],)):
            return remote(density.at[*here], ref, col_send.at[s], col_recv.at[COL[piece]], target)
        return remote(ref, ref, col_send.at[s], col_recv.at[COL[piece]], target)

    def copy_of(piece, where=None):
        return (row_copy if piece[0] == "row" else col_copy)(piece, where)

    waited, begun = set(), set()

    def run(name):
        _, _, needs, pushes = JOBS[name]
        for need in needs:
            if need[0] in ("row", "col") and need not in waited:
                waited.add(need)
                copy_of(need).wait_recv()
        kind = name[0]
        if kind == "split":
            _, s, t, dz, other = name
            k = k_col(dz, other)
            here = pl.ds(*COLUMNS[t][:2]), pl.ds(*COLUMNS[t][2:])
            high, low = split(cols[s, k, *here])
            col_hi[s, k, *here] = high
            col_lo[s, k, *here] = low
        elif kind == "mac":
            _, p, o = name[:3]
            low, count, lane, lanes = STREAMS[p + 1][o]
            here, wide = pl.ds(low, count), pl.ds(lane, lanes)
            keys = GROUPS[name[1:]]
            if isinstance(keys[0][1], bool):
                places = [k_col(*key) for key in keys]
                steps = [(((x - k % NX) * mirror + NX) % NX, ((y - k // NX) * mirror + NY) % NY) for k in places]
            else:
                places = [k_row(*key) for key in keys]
                steps = [(dx % NX, dy % NY) for dx, dy in keys]
            high_a, low_a = split(jnp.concatenate([gathered(p, low, *step) for step in steps], axis=1))
            high_b = jnp.concatenate([col_hi[p // 2, k, :, wide] for k in places], axis=0)
            low_b = jnp.concatenate([col_lo[p // 2, k, :, wide] for k in places], axis=0)
            both = jnp.dot(jnp.concatenate([high_a, low_a], axis=0), high_b, preferred_element_type=f32)
            term = both[:count] + both[count:] + jnp.dot(high_a, low_b, preferred_element_type=f32)
            if (p, o) in begun:
                acc[p, here, wide] += term
            else:
                begun.add((p, o))
                acc[p, here, wide] = term
        elif kind == "final":
            _, p, o = name
            low, count, lane, lanes = STREAMS[p + 1][o]
            here, wide = pl.ds(low, count), pl.ds(lane, lanes)
            value = masked(acc[p, here, wide], low, lane)
            if p % 2:
                value = 3.0 * gathered(p, low, 0, 0) - 2.0 * value
            if p == 2 * STEPS - 1:
                out[here, wide] = value
            else:
                ref = stream_of(p + 1, o)
                ref[0, 0, 0] = value[:count // 2]
                ref[1, 0, 0] = value[count // 2:]
                if p % 2:
                    cols[p // 2 + 1, r, here, wide] = value
        for where, _, piece in pushes:
            copy_of(piece, where).start()
        if kind == "start":
            for copy in fetch[:-1]:
                copy.wait()

    for name in ORDER:
        run(name)

    def sent(ref, sem):
        pltpu.make_async_copy(ref, ref, sem).wait()

    for p in range(2 * STEPS):
        sent(cols.at[0, pl.ds(0, 15)], row_send.at[p])
    for s in range(STEPS):
        sent(cols.at[s, pl.ds(0, 15)], col_send.at[s])


def local(density, pattern):
    size = density.shape[0]
    tiles = NX * NY
    return pl.pallas_call(
        kernel,
        out_shape=jax.ShapeDtypeStruct(density.shape, f32),
        in_specs=[pl.BlockSpec(memory_space=pltpu.HBM), pl.BlockSpec(memory_space=pltpu.HBM)],
        out_specs=pl.BlockSpec(memory_space=pltpu.VMEM),
        scratch_shapes=[
            pltpu.VMEM((3 * STEPS, 2, NY, NX, size // 4, size), f32),
            pltpu.VMEM((2 * STEPS, 2, NY, NX, size // 4, size // 2), f32),
            pltpu.VMEM((STEPS, tiles, size, size), f32),
            pltpu.VMEM((STEPS, tiles, size, size), bf16),
            pltpu.VMEM((STEPS, tiles, size, size), bf16),
            pltpu.VMEM((2 * STEPS, size, size), f32),
            pltpu.SMEM(pattern.shape, jnp.int32),
            pltpu.SemaphoreType.DMA((2 * STEPS,)),
            pltpu.SemaphoreType.DMA((len(ROW),)),
            pltpu.SemaphoreType.DMA((STEPS,)),
            pltpu.SemaphoreType.DMA((len(COL),)),
            pltpu.SemaphoreType.DMA((6,)),
        ],
        compiler_params=pltpu.CompilerParams(
            collective_id=0, has_side_effects=True, vmem_limit_bytes=53 * 1024 * 1024 + 512 * 1024),
    )(pattern, density)


def solution(mesh):
    placed = P("row", "col")
    return jax.shard_map(local, mesh=mesh, in_specs=(placed, placed), out_specs=placed, check_vma=False)
```

```python
import heapq

import jax
import jax.numpy as jnp
from jax import lax
from jax.experimental import pallas as pl
from jax.experimental.pallas import tpu as pltpu
from jax.sharding import PartitionSpec as P

BLOCK = 128
STEPS = 2
NX, NY, NZ = 4, 4, 8
MESH = pl.DeviceIdType.MESH
f32, bf16 = jnp.float32, jnp.bfloat16
OFFSETS = [(dx, dy) for dx in (0, 1, -1, 2) for dy in (0, 1, -1, 2)]
RING = (0, 1, -1, 2, -2, 3, -3, 4)

GROUPS = {}
BEGIN_ROWS = [(0, "g1"), (1, "g1")]
BEGIN_COLS = {}
LATER_COLS = {}
DIRECT = set()
BEGIN = [(0, "g1"), (1, "g1")]

ROWS64, HOP, SMALL, DOT, DOT_TILE = 1.4, 2.2, 0.02, 0.1, 0.1
NEAR_FIRST = [
    [(0, 0), (1, 0), (-1, 0), (0, 1), (0, -1)],
    [(2, 0), (0, 2), (1, 1), (1, -1), (-1, 1), (-1, -1)],
    [(1, 2), (-1, 2), (2, 1), (2, -1)],
    [(2, 2)],
]
COL_GROUPS = [[0], [1, -1], [2, -2], [3, -3], [4]]


HALVES = [(0, 128, 0, 256), (128, 128, 0, 256)]
SQUARE = [(0, 128, 0, 128), (0, 128, 128, 128), (128, 128, 0, 256)]
STREAMS = [HALVES, SQUARE, HALVES, SQUARE, HALVES]
COLUMNS = [(0, 128, 0, 128), (128, 64, 0, 128), (192, 64, 0, 128), (0, 128, 128, 128), (128, 64, 128, 128), (192, 64, 128, 128)]
SLOTS = (0, 1, -1, 2)
SETS = [((0, 1), (1, 2), (3, 1)), ((0, 1), (1, 3))]
SET_CHOICE = [[0, 0], [0, 0, 0], [0, 0], [0, 0, 0]]
FAR = [(0, 1, 0), (0, 1)]


def sets_of(p, h):
    return SETS[SET_CHOICE[p][h]]


def far_sign(p, h, plan, group=None):
    turn = 0 if group is None else FAR[SET_CHOICE[p][h]][group]
    return 1 if (h + plan + turn) % 2 == 0 else -1


def group_of(p, h, a):
    slot = SLOTS.index(a)
    return next(n for n, (first, count) in enumerate(sets_of(p, h)) if first <= slot < first + count)


def row_tile(p, h, plan, a, b):
    if (a, b) == (0, 0):
        return []
    return [("row", p, h, plan, a if b == 0 else "g%d" % group_of(p, h, a), b)]


def col_tile(s, t, dz, other):
    if other:
        return [("col", s, t, dz, "s")]
    if dz == 0:
        return []
    return [("col", s, t, dz, part) for part in (("q0", "q1") if dz == 4 else ("h",))]


def make_jobs():
    jobs = {}

    def link(plan, axis, sign):
        return ("x" if (axis == 0) == (plan == 0) else "y", sign)

    def row_size(p, h):
        return STREAMS[p][h][1] * STREAMS[p][h][3] / (128 * 256)

    def own_row(p, h):
        pushes = []
        for axis in (0, 1):
            for plan in (0, 1):
                for sign in (1, -1):
                    a, b = (sign, 0) if axis == 0 else ("g0", sign)
                    pushes.append((link(plan, axis, sign), row_size(p, h), ("row", p, h, plan, a, b)))
        return pushes

    def col_size(t):
        return COLUMNS[t][1] * COLUMNS[t][3] / (64 * 256)

    def own_col(s, ts):
        pushes = []
        for t in ts:
            pushes += [(("z", step), col_size(t), ("col", s, t, step, "h")) for step in ((1, -1, 2, -2) if (s, t) in DIRECT else (1, -1))]
        return pushes + [(("core", 0), 0.15, ("col", s, t, 0, "s")) for t in ts]

    def overlap(one, other):
        return all(one[i] < other[i] + other[i + 1] and other[i] < one[i] + one[i + 1] for i in (0, 2))

    def add(name, priority, cost, needs, pushes=()):
        jobs[name] = (priority, cost + SMALL * (len(pushes) + len(needs)), needs, list(pushes))

    add(("start",), 0, SMALL, [], own_row(0, 0) + own_col(0, [t for t in range(len(COLUMNS)) if t not in BEGIN_COLS]))
    add(("begin", 0, 1), 0, 0, [("turn", 0, 0, *key) for key in BEGIN_ROWS], own_row(0, 1))
    for t, (behind, dz) in BEGIN_COLS.items():
        add(("begin_col", t), 0, 0, [("ring", 0, behind, sign * dz) for sign in (1, -1)], own_col(0, (t,)))
    for t, (behind, dz) in LATER_COLS.items():
        begun = ("final", 1, COLUMNS[t][0] // 128)
        add(("later_col", t), 0, 0, [begun] + [("ring", 1, behind, sign * dz) for sign in (1, -1)], own_col(1, (t,)))
    for p in range(2 * STEPS):
        s = p // 2
        for h, stream in enumerate(STREAMS[p]):
            size = row_size(p, h)
            for plan in (0, 1):
                for sign in (1, -1):
                    pushes = []
                    if sign == far_sign(p, h, plan):
                        pushes = [(link(plan, 0, sign), size, ("row", p, h, plan, 2, 0))]
                        add(("turn", p, h, plan, sign), 0, 0, row_tile(p, h, plan, sign, 0), pushes)
                for g, (first, count) in enumerate(sets_of(p, h)):
                    if g:
                        needs = [piece for a in SLOTS[first:first + count] for piece in row_tile(p, h, plan, a, 0)]
                        add(("turn", p, h, plan, "g%d" % g), 0, 0, needs, [
                            (link(plan, 1, turn), size * count, ("row", p, h, plan, "g%d" % g, turn)) for turn in (1, -1)])
                    sign = far_sign(p, h, plan, g)
                    add(("pass", p, h, plan, "g%d" % g), 0, 0, [("row", p, h, plan, "g%d" % g, sign)],
                        [(link(plan, 1, sign), size * count, ("row", p, h, plan, "g%d" % g, 2))])
        if p % 2 == 0:
            for t, dz in ((t, dz) for dz in RING for t in range(len(COLUMNS))):
                pushes = []
                if dz:
                    sign = 1 if dz > 0 else -1
                    if (s, t) in DIRECT:
                        if abs(dz) == 2:
                            pushes.append((("z", sign), col_size(t), ("col", s, t, dz + sign, "h")))
                            pushes.append((("z", 2 * sign), col_size(t) / 2, ("col", s, t, 4, "q0" if sign == 1 else "q1")))
                    elif abs(dz) < 3:
                        pushes.append((("z", sign), col_size(t), ("col", s, t, dz + sign, "h")))
                    elif dz != 4:
                        pushes.append((("z", sign), col_size(t) / 2, ("col", s, t, 4, "q0" if sign == 1 else "q1")))
                    pushes.append((("core", 0), 0.15, ("col", s, t, dz, "s")))
                    add(("ring", s, t, dz), 0, 0, col_tile(s, t, dz, False), pushes)
                before = [("ring", s, t, dz)] if dz else [("start",) if p == 0 else ("final", p - 1, COLUMNS[t][0] // 128)]
                add(("split", s, t, dz, False), 2, SMALL, before)
                add(("split", s, t, dz, True), 2, SMALL, col_tile(s, t, dz, True))
        for o, target in enumerate(STREAMS[p + 1]):
            rows_used = [h for h, stream in enumerate(STREAMS[p]) if overlap(stream, (target[0], target[1], 0, 256))]
            cols_used = [t for t, col in enumerate(COLUMNS) if overlap(col, (0, 256, target[2], target[3]))]
            pieces = {key: [piece for h in rows_used
                            for piece in row_tile(p, h, 0, *key) + row_tile(p, h, 1, *key[::-1])] for key in OFFSETS}
            starts = [("start",) if p == 0 else ("final", p - 1, h) for h in rows_used]
            if p % 2 == 0 and target[0] == 0:
                need = [piece for key in OFFSETS for piece in pieces[key]] + starts
                groups = [[(dz, other) for dz in group for other in (False, True)] for group in COL_GROUPS]
                needs = [need + [("split", s, t, *key) for t in cols_used for key in group] for group in groups]
            else:
                groups = NEAR_FIRST
                need = [("split", s, t, dz, other) for t in cols_used for dz in RING for other in (False, True)]
                needs = [[piece for key in group for piece in pieces[key]] + starts + (need if p % 2 == 0 else [])
                         for group in groups]
            for n, group in enumerate(groups):
                cost = DOT + DOT_TILE * len(group) * (0.6 if target[3] == 128 else 1)
                jobs[("mac", p, o, n)] = (4 + p, cost, needs[n], [])
                GROUPS[p, o, n] = group
            pushes = []
            if p < 2 * STEPS - 1:
                pushes = own_row(p + 1, o) + (own_col(s + 1, [t for t, col in enumerate(COLUMNS) if col[0] // 128 == o and t not in LATER_COLS]) if p % 2 else [])
            macs = [("mac", p, o, n) for n in range(len(groups))]
            if p % 2 == 0 and o == 2:
                add(("final", p, o), 1, 2 * SMALL, macs)
                add(("begin", p, o), 1, 0, [("final", p, o)] + [("turn", p + 1, 1, *key) for key in BEGIN], pushes)
            else:
                add(("final", p, o), 1, 2 * SMALL, macs, pushes)
    return jobs


def make_order(jobs):
    ready_at, missing, users = {}, {}, {}
    for name, (_, _, needs, _) in jobs.items():
        missing[name] = len(set(needs))
        ready_at[name] = 0.0
        for need in set(needs):
            users.setdefault(need, []).append(name)
    waiting, ready, free = [], [], {}
    rank = {name: n for n, name in enumerate(jobs)}

    def done(thing, when):
        for user in users.get(thing, ()):
            missing[user] -= 1
            ready_at[user] = max(ready_at[user], when)
            if missing[user] == 0:
                heapq.heappush(waiting, (ready_at[user], rank[user], user))

    for name in jobs:
        if missing[name] == 0:
            heapq.heappush(waiting, (0.0, rank[name], name))
    now, order, times = 0.0, [], {}
    while waiting or ready:
        if not ready and waiting[0][0] > now:
            now = waiting[0][0]
        while waiting and waiting[0][0] <= now:
            when, number, name = heapq.heappop(waiting)
            heapq.heappush(ready, (jobs[name][0], when, number, name))
        name = heapq.heappop(ready)[-1]
        _, cost, _, pushes = jobs[name]
        now += cost
        order.append(name)
        times[name] = now
        for (axis, steps), amount, piece in pushes:
            way = axis, steps > 0
            free[way] = max(free.get(way, 0.0), now) + amount * max(1, abs(steps)) * ROWS64
            done(piece, free[way] + HOP)
        done(name, now)
    return order, times


JOBS = make_jobs()
ORDER, TIMES = make_order(JOBS)
PIECES = [piece for name in JOBS for _, _, piece in JOBS[name][3]]
ROW = {name: n for n, name in enumerate(piece for piece in PIECES if piece[0] == "row")}
COL = {name: n for n, name in enumerate(piece for piece in PIECES if piece[0] == "col")}


def split(value):
    high = value.astype(bf16)
    return high, (value - high.astype(f32)).astype(bf16)


def kernel(pattern_in, density, out, wide_rows, half_rows, cols, col_hi, col_lo, acc, pattern,
           row_send, row_recv, col_send, col_recv, local_sem):
    size = density.shape[0]
    r, c = lax.axis_index("row"), lax.axis_index("col")
    z, core = r // 2, r % 2
    y, x = c // NX, c % NX

    def device(dx=0, dy=0, dz=0):
        return (((z + dz + NZ) % NZ) * 2 + core, ((y + dy + NY) % NY) * NX + (x + dx + NX) % NX)

    sibling = (z * 2 + 1 - core, c)

    mirror = 1 - 2 * core

    def k_row(dx, dy):
        return ((y - dy * mirror + NY) % NY) * NX + (x - dx * mirror + NX) % NX

    def k_col(dz, other):
        return ((z - dz + NZ) % NZ) * 2 + (1 - core if other else core)

    def stream_of(p, h):
        before = [h_ for p_ in range(4) for h_, other in enumerate(STREAMS[p_])
                  if (p_, h_) < (p, h) and other[3] == STREAMS[p][h][3]]
        return (wide_rows if STREAMS[p][h][3] == size else half_rows).at[len(before)]

    step_rows = HALVES[0][1] // 2
    fetch = [
        pltpu.make_async_copy(density.at[pl.ds((2 * h + plan) * step_rows, step_rows)], stream_of(0, h).at[plan, 0, 0],
                              local_sem.at[2 * h + plan])
        for h in (0, 1) for plan in (0, 1)]
    fetch += [
        pltpu.make_async_copy(density, cols.at[0, r], local_sem.at[4]),
        pltpu.make_async_copy(pattern_in, pattern, local_sem.at[5]),
    ]
    for copy in fetch:
        copy.start()

    peers = [device(dx=1), device(dx=-1), device(dy=1), device(dy=-1), sibling]
    peers += [device(dz=step) for step in ((1, -1, 2, -2) if DIRECT else (1, -1))]
    barrier = pltpu.get_barrier_semaphore()
    for peer in peers:
        pl.semaphore_signal(barrier, inc=1, device_id=peer, device_id_type=MESH)
    pl.semaphore_wait(barrier, len(peers))
    mask = []

    def masked(value, low, lane):
        if not mask:
            fetch[-1].wait()
            mask.extend([pattern[a, b].astype(f32) for b in range(2)] for a in range(2))
        parts = [value[:, n:n + BLOCK] * mask[low // BLOCK][(lane + n) // BLOCK] for n in range(0, value.shape[1], BLOCK)]
        return jnp.concatenate(parts, axis=1)

    def slot_of(distance):
        return distance + distance // 2 - 2 * (distance // 3)

    def gathered(p, low, dx, dy):
        parts = []
        for h, stream in enumerate(STREAMS[p]):
            if stream[0] == low:
                ref = stream_of(p, h)
                parts.append(jnp.concatenate([ref[0, slot_of(dy), slot_of(dx)], ref[1, slot_of(dx), slot_of(dy)]], axis=0))
        return parts[0] if len(parts) == 1 else jnp.concatenate(parts, axis=1)

    def remote(src, dst, send, recv, target):
        return pltpu.make_async_remote_copy(
            src_ref=src, dst_ref=dst, send_sem=send, recv_sem=recv, device_id=target, device_id_type=MESH)

    def row_copy(piece, where):
        _, p, h, plan, a, b = piece
        ref = stream_of(p, h).at[plan]
        moved = a if b == 0 else b
        held = SLOTS.index(0 if abs(moved) == 1 else where[1]) if where else SLOTS.index(moved)
        if b == 0:
            src, dst = ref.at[0, held], ref.at[0, SLOTS.index(a)]
        else:
            first, count = sets_of(p, h)[int(a[1])]
            here = pl.ds(first, count) if count > 1 else first
            src, dst = ref.at[held, here], ref.at[SLOTS.index(b), here]
        if where and p == 0 and held == 0 and (b == 0 or a == "g0"):
            src = density.at[pl.ds((2 * h + plan) * step_rows, step_rows)]
        target = device(**{"d" + where[0]: where[1] * mirror}) if where else sibling
        return remote(src, dst, row_send.at[p], row_recv.at[ROW[piece]], target)

    def col_copy(piece, where):
        _, s, t, dz, part = piece
        low, count, lane, lanes = COLUMNS[t]
        if part in ("q0", "q1"):
            count //= 2
            low += count if part == "q1" else 0
        if not where:
            held, target = k_col(dz, part == "s"), sibling
        elif where[0] == "core":
            held, target = k_col(dz, False), sibling
        else:
            held, target = k_col(dz - where[1], False), device(dz=where[1])
        here = pl.ds(low, count), pl.ds(lane, lanes)
        ref = cols.at[s, held, *here]
        if where and s == 0 and dz in ((0,) if where[0] == "core" else (where[1],)):
            return remote(density.at[*here], ref, col_send.at[s], col_recv.at[COL[piece]], target)
        return remote(ref, ref, col_send.at[s], col_recv.at[COL[piece]], target)

    def copy_of(piece, where=None):
        return (row_copy if piece[0] == "row" else col_copy)(piece, where)

    waited, begun = set(), set()

    def run(name):
        _, _, needs, pushes = JOBS[name]
        for need in needs:
            if need[0] in ("row", "col") and need not in waited:
                waited.add(need)
                copy_of(need).wait_recv()
        kind = name[0]
        if kind == "split":
            _, s, t, dz, other = name
            k = k_col(dz, other)
            here = pl.ds(*COLUMNS[t][:2]), pl.ds(*COLUMNS[t][2:])
            high, low = split(cols[s, k, *here])
            col_hi[s, k, *here] = high
            col_lo[s, k, *here] = low
        elif kind == "mac":
            _, p, o = name[:3]
            low, count, lane, lanes = STREAMS[p + 1][o]
            here, wide = pl.ds(low, count), pl.ds(lane, lanes)
            keys = GROUPS[name[1:]]
            if isinstance(keys[0][1], bool):
                places = [k_col(*key) for key in keys]
                steps = [(((x - k % NX) * mirror + NX) % NX, ((y - k // NX) * mirror + NY) % NY) for k in places]
            else:
                places = [k_row(*key) for key in keys]
                steps = [(dx % NX, dy % NY) for dx, dy in keys]
            high_a, low_a = split(jnp.concatenate([gathered(p, low, *step) for step in steps], axis=1))
            high_b = jnp.concatenate([col_hi[p // 2, k, :, wide] for k in places], axis=0)
            low_b = jnp.concatenate([col_lo[p // 2, k, :, wide] for k in places], axis=0)
            both = jnp.dot(jnp.concatenate([high_a, low_a], axis=0), high_b, preferred_element_type=f32)
            term = both[:count] + both[count:] + jnp.dot(high_a, low_b, preferred_element_type=f32)
            if (p, o) in begun:
                acc[p, here, wide] += term
            else:
                begun.add((p, o))
                acc[p, here, wide] = term
        elif kind == "final":
            _, p, o = name
            low, count, lane, lanes = STREAMS[p + 1][o]
            here, wide = pl.ds(low, count), pl.ds(lane, lanes)
            value = masked(acc[p, here, wide], low, lane)
            if p % 2:
                value = 3.0 * gathered(p, low, 0, 0) - 2.0 * value
            if p == 2 * STEPS - 1:
                out[here, wide] = value
            else:
                ref = stream_of(p + 1, o)
                ref[0, 0, 0] = value[:count // 2]
                ref[1, 0, 0] = value[count // 2:]
                if p % 2:
                    cols[p // 2 + 1, r, here, wide] = value
        for where, _, piece in pushes:
            copy_of(piece, where).start()
        if kind == "start":
            for copy in fetch[:-1]:
                copy.wait()

    for name in ORDER:
        run(name)

    def sent(ref, sem):
        pltpu.make_async_copy(ref, ref, sem).wait()

    for p in range(2 * STEPS):
        sent(cols.at[0, pl.ds(0, 15)], row_send.at[p])
    for s in range(STEPS):
        sent(cols.at[s, pl.ds(0, 15)], col_send.at[s])


def local(density, pattern):
    size = density.shape[0]
    tiles = NX * NY
    return pl.pallas_call(
        kernel,
        out_shape=jax.ShapeDtypeStruct(density.shape, f32),
        in_specs=[pl.BlockSpec(memory_space=pltpu.HBM), pl.BlockSpec(memory_space=pltpu.HBM)],
        out_specs=pl.BlockSpec(memory_space=pltpu.VMEM),
        scratch_shapes=[
            pltpu.VMEM((3 * STEPS, 2, NY, NX, size // 4, size), f32),
            pltpu.VMEM((2 * STEPS, 2, NY, NX, size // 4, size // 2), f32),
            pltpu.VMEM((STEPS, tiles, size, size), f32),
            pltpu.VMEM((STEPS, tiles, size, size), bf16),
            pltpu.VMEM((STEPS, tiles, size, size), bf16),
            pltpu.VMEM((2 * STEPS, size, size), f32),
            pltpu.SMEM(pattern.shape, jnp.int32),
            pltpu.SemaphoreType.DMA((2 * STEPS,)),
            pltpu.SemaphoreType.DMA((len(ROW),)),
            pltpu.SemaphoreType.DMA((STEPS,)),
            pltpu.SemaphoreType.DMA((len(COL),)),
            pltpu.SemaphoreType.DMA((6,)),
        ],
        compiler_params=pltpu.CompilerParams(
            collective_id=0, has_side_effects=True, vmem_limit_bytes=53 * 1024 * 1024 + 512 * 1024),
    )(pattern, density)


def solution(mesh):
    placed = P("row", "col")
    return jax.shard_map(local, mesh=mesh, in_specs=(placed, placed), out_specs=placed, check_vma=False)
```

```python
import heapq

import jax
import jax.numpy as jnp
from jax import lax
from jax.experimental import pallas as pl
from jax.experimental.pallas import tpu as pltpu
from jax.sharding import PartitionSpec as P

BLOCK = 128
STEPS = 2
NX, NY, NZ = 4, 4, 8
MESH = pl.DeviceIdType.MESH
f32, bf16 = jnp.float32, jnp.bfloat16
OFFSETS = [(dx, dy) for dx in (0, 1, -1, 2) for dy in (0, 1, -1, 2)]
RING = (0, 1, -1, 2, -2, 3, -3, 4)

GROUPS = {}
BEGIN_ROWS = [(0, "g1"), (1, "g1")]
BEGIN_COLS = {}
LATER_COLS = {}
DIRECT = set()
BEGIN = [(0, "g1"), (1, "g1")]

ROWS64, HOP, SMALL, DOT, DOT_TILE = 1.4, 2.2, 0.02, 0.1, 0.1
NEAR_FIRST = [
    [(0, 0), (1, 0), (-1, 0), (0, 1), (0, -1)],
    [(2, 0), (0, 2), (1, 1), (1, -1), (-1, 1), (-1, -1)],
    [(1, 2), (-1, 2), (2, 1), (2, -1)],
    [(2, 2)],
]
COL_GROUPS = [[0], [1, -1], [2, -2], [3, -3], [4]]


HALVES = [(0, 128, 0, 256), (128, 128, 0, 256)]
SQUARE = [(0, 128, 0, 128), (0, 128, 128, 128), (128, 128, 0, 256)]
STREAMS = [HALVES, SQUARE, HALVES, SQUARE, HALVES]
COLUMNS = [(0, 128, 0, 256), (128, 128, 0, 128), (128, 128, 128, 128)]
SLOTS = (0, 1, -1, 2)
SETS = [((0, 1), (1, 2), (3, 1)), ((0, 1), (1, 3))]
SET_CHOICE = [[0, 0], [0, 0, 0], [0, 0], [0, 0, 0]]
FAR = [(0, 1, 0), (0, 1)]


def sets_of(p, h):
    return SETS[SET_CHOICE[p][h]]


def far_sign(p, h, plan, group=None):
    turn = 0 if group is None else FAR[SET_CHOICE[p][h]][group]
    return 1 if (h + plan + turn) % 2 == 0 else -1


def group_of(p, h, a):
    slot = SLOTS.index(a)
    return next(n for n, (first, count) in enumerate(sets_of(p, h)) if first <= slot < first + count)


def row_tile(p, h, plan, a, b):
    if (a, b) == (0, 0):
        return []
    return [("row", p, h, plan, a if b == 0 else "g%d" % group_of(p, h, a), b)]


def col_tile(s, t, dz, other):
    if other:
        return [("col", s, t, dz, "s")]
    if dz == 0:
        return []
    return [("col", s, t, dz, part) for part in (("q0", "q1") if dz == 4 else ("h",))]


def make_jobs():
    jobs = {}

    def link(plan, axis, sign):
        return ("x" if (axis == 0) == (plan == 0) else "y", sign)

    def row_size(p, h):
        return STREAMS[p][h][1] * STREAMS[p][h][3] / (128 * 256)

    def own_row(p, h):
        pushes = []
        for axis in (0, 1):
            for plan in (0, 1):
                for sign in (1, -1):
                    a, b = (sign, 0) if axis == 0 else ("g0", sign)
                    pushes.append((link(plan, axis, sign), row_size(p, h), ("row", p, h, plan, a, b)))
        return pushes

    def col_size(t):
        return COLUMNS[t][1] * COLUMNS[t][3] / (64 * 256)

    def own_col(s, ts):
        pushes = []
        for t in ts:
            pushes += [(("z", step), col_size(t), ("col", s, t, step, "h")) for step in ((1, -1, 2, -2) if (s, t) in DIRECT else (1, -1))]
        return pushes + [(("core", 0), 0.15, ("col", s, t, 0, "s")) for t in ts]

    def overlap(one, other):
        return all(one[i] < other[i] + other[i + 1] and other[i] < one[i] + one[i + 1] for i in (0, 2))

    def add(name, priority, cost, needs, pushes=()):
        jobs[name] = (priority, cost + SMALL * (len(pushes) + len(needs)), needs, list(pushes))

    add(("start",), 0, SMALL, [], own_row(0, 0) + own_col(0, [t for t in range(len(COLUMNS)) if t not in BEGIN_COLS]))
    add(("begin", 0, 1), 0, 0, [("turn", 0, 0, *key) for key in BEGIN_ROWS], own_row(0, 1))
    for t, (behind, dz) in BEGIN_COLS.items():
        add(("begin_col", t), 0, 0, [("ring", 0, behind, sign * dz) for sign in (1, -1)], own_col(0, (t,)))
    for t, (behind, dz) in LATER_COLS.items():
        begun = ("final", 1, COLUMNS[t][0] // 128)
        add(("later_col", t), 0, 0, [begun] + [("ring", 1, behind, sign * dz) for sign in (1, -1)], own_col(1, (t,)))
    for p in range(2 * STEPS):
        s = p // 2
        for h, stream in enumerate(STREAMS[p]):
            size = row_size(p, h)
            for plan in (0, 1):
                for sign in (1, -1):
                    pushes = []
                    if sign == far_sign(p, h, plan):
                        pushes = [(link(plan, 0, sign), size, ("row", p, h, plan, 2, 0))]
                        add(("turn", p, h, plan, sign), 0, 0, row_tile(p, h, plan, sign, 0), pushes)
                for g, (first, count) in enumerate(sets_of(p, h)):
                    if g:
                        needs = [piece for a in SLOTS[first:first + count] for piece in row_tile(p, h, plan, a, 0)]
                        add(("turn", p, h, plan, "g%d" % g), 0, 0, needs, [
                            (link(plan, 1, turn), size * count, ("row", p, h, plan, "g%d" % g, turn)) for turn in (1, -1)])
                    sign = far_sign(p, h, plan, g)
                    add(("pass", p, h, plan, "g%d" % g), 0, 0, [("row", p, h, plan, "g%d" % g, sign)],
                        [(link(plan, 1, sign), size * count, ("row", p, h, plan, "g%d" % g, 2))])
        if p % 2 == 0:
            for t, dz in ((t, dz) for dz in RING for t in range(len(COLUMNS))):
                pushes = []
                if dz:
                    sign = 1 if dz > 0 else -1
                    if (s, t) in DIRECT:
                        if abs(dz) == 2:
                            pushes.append((("z", sign), col_size(t), ("col", s, t, dz + sign, "h")))
                            pushes.append((("z", 2 * sign), col_size(t) / 2, ("col", s, t, 4, "q0" if sign == 1 else "q1")))
                    elif abs(dz) < 3:
                        pushes.append((("z", sign), col_size(t), ("col", s, t, dz + sign, "h")))
                    elif dz != 4:
                        pushes.append((("z", sign), col_size(t) / 2, ("col", s, t, 4, "q0" if sign == 1 else "q1")))
                    pushes.append((("core", 0), 0.15, ("col", s, t, dz, "s")))
                    add(("ring", s, t, dz), 0, 0, col_tile(s, t, dz, False), pushes)
                before = [("ring", s, t, dz)] if dz else [("start",) if p == 0 else ("final", p - 1, COLUMNS[t][0] // 128)]
                add(("split", s, t, dz, False), 2, SMALL, before)
                add(("split", s, t, dz, True), 2, SMALL, col_tile(s, t, dz, True))
        for o, target in enumerate(STREAMS[p + 1]):
            rows_used = [h for h, stream in enumerate(STREAMS[p]) if overlap(stream, (target[0], target[1], 0, 256))]
            cols_used = [t for t, col in enumerate(COLUMNS) if overlap(col, (0, 256, target[2], target[3]))]
            pieces = {key: [piece for h in rows_used
                            for piece in row_tile(p, h, 0, *key) + row_tile(p, h, 1, *key[::-1])] for key in OFFSETS}
            starts = [("start",) if p == 0 else ("final", p - 1, h) for h in rows_used]
            if p % 2 == 0 and target[0] == 0:
                need = [piece for key in OFFSETS for piece in pieces[key]] + starts
                groups = [[(dz, other) for dz in group for other in (False, True)] for group in COL_GROUPS]
                needs = [need + [("split", s, t, *key) for t in cols_used for key in group] for group in groups]
            else:
                groups = NEAR_FIRST
                need = [("split", s, t, dz, other) for t in cols_used for dz in RING for other in (False, True)]
                needs = [[piece for key in group for piece in pieces[key]] + starts + (need if p % 2 == 0 else [])
                         for group in groups]
            for n, group in enumerate(groups):
                cost = DOT + DOT_TILE * len(group) * (0.6 if target[3] == 128 else 1)
                jobs[("mac", p, o, n)] = (4 + p, cost, needs[n], [])
                GROUPS[p, o, n] = group
            pushes = []
            if p < 2 * STEPS - 1:
                pushes = own_row(p + 1, o) + (own_col(s + 1, [t for t, col in enumerate(COLUMNS) if col[0] // 128 == o and t not in LATER_COLS]) if p % 2 else [])
            macs = [("mac", p, o, n) for n in range(len(groups))]
            if p % 2 == 0 and o == 2:
                add(("final", p, o), 1, 2 * SMALL, macs)
                add(("begin", p, o), 1, 0, [("final", p, o)] + [("turn", p + 1, 1, *key) for key in BEGIN], pushes)
            else:
                add(("final", p, o), 1, 2 * SMALL, macs, pushes)
    return jobs


def make_order(jobs):
    ready_at, missing, users = {}, {}, {}
    for name, (_, _, needs, _) in jobs.items():
        missing[name] = len(set(needs))
        ready_at[name] = 0.0
        for need in set(needs):
            users.setdefault(need, []).append(name)
    waiting, ready, free = [], [], {}
    rank = {name: n for n, name in enumerate(jobs)}

    def done(thing, when):
        for user in users.get(thing, ()):
            missing[user] -= 1
            ready_at[user] = max(ready_at[user], when)
            if missing[user] == 0:
                heapq.heappush(waiting, (ready_at[user], rank[user], user))

    for name in jobs:
        if missing[name] == 0:
            heapq.heappush(waiting, (0.0, rank[name], name))
    now, order, times = 0.0, [], {}
    while waiting or ready:
        if not ready and waiting[0][0] > now:
            now = waiting[0][0]
        while waiting and waiting[0][0] <= now:
            when, number, name = heapq.heappop(waiting)
            heapq.heappush(ready, (jobs[name][0], when, number, name))
        name = heapq.heappop(ready)[-1]
        _, cost, _, pushes = jobs[name]
        now += cost
        order.append(name)
        times[name] = now
        for (axis, steps), amount, piece in pushes:
            way = axis, steps > 0
            free[way] = max(free.get(way, 0.0), now) + amount * max(1, abs(steps)) * ROWS64
            done(piece, free[way] + HOP)
        done(name, now)
    return order, times


JOBS = make_jobs()
ORDER, TIMES = make_order(JOBS)
PIECES = [piece for name in JOBS for _, _, piece in JOBS[name][3]]
ROW = {name: n for n, name in enumerate(piece for piece in PIECES if piece[0] == "row")}
COL = {name: n for n, name in enumerate(piece for piece in PIECES if piece[0] == "col")}


def split(value):
    high = value.astype(bf16)
    return high, (value - high.astype(f32)).astype(bf16)


def kernel(pattern_in, density, out, wide_rows, half_rows, cols, col_hi, col_lo, acc, pattern,
           row_send, row_recv, col_send, col_recv, local_sem):
    size = density.shape[0]
    r, c = lax.axis_index("row"), lax.axis_index("col")
    z, core = r // 2, r % 2
    y, x = c // NX, c % NX

    def device(dx=0, dy=0, dz=0):
        return (((z + dz + NZ) % NZ) * 2 + core, ((y + dy + NY) % NY) * NX + (x + dx + NX) % NX)

    sibling = (z * 2 + 1 - core, c)

    mirror = 1 - 2 * core

    def k_row(dx, dy):
        return ((y - dy * mirror + NY) % NY) * NX + (x - dx * mirror + NX) % NX

    def k_col(dz, other):
        return ((z - dz + NZ) % NZ) * 2 + (1 - core if other else core)

    def stream_of(p, h):
        before = [h_ for p_ in range(4) for h_, other in enumerate(STREAMS[p_])
                  if (p_, h_) < (p, h) and other[3] == STREAMS[p][h][3]]
        return (wide_rows if STREAMS[p][h][3] == size else half_rows).at[len(before)]

    step_rows = HALVES[0][1] // 2
    fetch = [
        pltpu.make_async_copy(density.at[pl.ds((2 * h + plan) * step_rows, step_rows)], stream_of(0, h).at[plan, 0, 0],
                              local_sem.at[2 * h + plan])
        for h in (0, 1) for plan in (0, 1)]
    fetch += [
        pltpu.make_async_copy(density, cols.at[0, r], local_sem.at[4]),
        pltpu.make_async_copy(pattern_in, pattern, local_sem.at[5]),
    ]
    for copy in fetch:
        copy.start()

    peers = [device(dx=1), device(dx=-1), device(dy=1), device(dy=-1), sibling]
    peers += [device(dz=step) for step in ((1, -1, 2, -2) if DIRECT else (1, -1))]
    barrier = pltpu.get_barrier_semaphore()
    for peer in peers:
        pl.semaphore_signal(barrier, inc=1, device_id=peer, device_id_type=MESH)
    pl.semaphore_wait(barrier, len(peers))
    mask = []

    def masked(value, low, lane):
        if not mask:
            fetch[-1].wait()
            mask.extend([pattern[a, b].astype(f32) for b in range(2)] for a in range(2))
        parts = [value[:, n:n + BLOCK] * mask[low // BLOCK][(lane + n) // BLOCK] for n in range(0, value.shape[1], BLOCK)]
        return jnp.concatenate(parts, axis=1)

    def slot_of(distance):
        return distance + distance // 2 - 2 * (distance // 3)

    def gathered(p, low, dx, dy):
        parts = []
        for h, stream in enumerate(STREAMS[p]):
            if stream[0] == low:
                ref = stream_of(p, h)
                parts.append(jnp.concatenate([ref[0, slot_of(dy), slot_of(dx)], ref[1, slot_of(dx), slot_of(dy)]], axis=0))
        return parts[0] if len(parts) == 1 else jnp.concatenate(parts, axis=1)

    def remote(src, dst, send, recv, target):
        return pltpu.make_async_remote_copy(
            src_ref=src, dst_ref=dst, send_sem=send, recv_sem=recv, device_id=target, device_id_type=MESH)

    def row_copy(piece, where):
        _, p, h, plan, a, b = piece
        ref = stream_of(p, h).at[plan]
        moved = a if b == 0 else b
        held = SLOTS.index(0 if abs(moved) == 1 else where[1]) if where else SLOTS.index(moved)
        if b == 0:
            src, dst = ref.at[0, held], ref.at[0, SLOTS.index(a)]
        else:
            first, count = sets_of(p, h)[int(a[1])]
            here = pl.ds(first, count) if count > 1 else first
            src, dst = ref.at[held, here], ref.at[SLOTS.index(b), here]
        if where and p == 0 and held == 0 and (b == 0 or a == "g0"):
            src = density.at[pl.ds((2 * h + plan) * step_rows, step_rows)]
        target = device(**{"d" + where[0]: where[1] * mirror}) if where else sibling
        return remote(src, dst, row_send.at[p], row_recv.at[ROW[piece]], target)

    def col_copy(piece, where):
        _, s, t, dz, part = piece
        low, count, lane, lanes = COLUMNS[t]
        if part in ("q0", "q1"):
            count //= 2
            low += count if part == "q1" else 0
        if not where:
            held, target = k_col(dz, part == "s"), sibling
        elif where[0] == "core":
            held, target = k_col(dz, False), sibling
        else:
            held, target = k_col(dz - where[1], False), device(dz=where[1])
        here = pl.ds(low, count), pl.ds(lane, lanes)
        ref = cols.at[s, held, *here]
        if where and s == 0 and dz in ((0,) if where[0] == "core" else (where[1],)):
            return remote(density.at[*here], ref, col_send.at[s], col_recv.at[COL[piece]], target)
        return remote(ref, ref, col_send.at[s], col_recv.at[COL[piece]], target)

    def copy_of(piece, where=None):
        return (row_copy if piece[0] == "row" else col_copy)(piece, where)

    waited, begun = set(), set()

    def run(name):
        _, _, needs, pushes = JOBS[name]
        for need in needs:
            if need[0] in ("row", "col") and need not in waited:
                waited.add(need)
                copy_of(need).wait_recv()
        kind = name[0]
        if kind == "split":
            _, s, t, dz, other = name
            k = k_col(dz, other)
            here = pl.ds(*COLUMNS[t][:2]), pl.ds(*COLUMNS[t][2:])
            high, low = split(cols[s, k, *here])
            col_hi[s, k, *here] = high
            col_lo[s, k, *here] = low
        elif kind == "mac":
            _, p, o = name[:3]
            low, count, lane, lanes = STREAMS[p + 1][o]
            here, wide = pl.ds(low, count), pl.ds(lane, lanes)
            keys = GROUPS[name[1:]]
            if isinstance(keys[0][1], bool):
                places = [k_col(*key) for key in keys]
                steps = [(((x - k % NX) * mirror + NX) % NX, ((y - k // NX) * mirror + NY) % NY) for k in places]
            else:
                places = [k_row(*key) for key in keys]
                steps = [(dx % NX, dy % NY) for dx, dy in keys]
            high_a, low_a = split(jnp.concatenate([gathered(p, low, *step) for step in steps], axis=1))
            high_b = jnp.concatenate([col_hi[p // 2, k, :, wide] for k in places], axis=0)
            low_b = jnp.concatenate([col_lo[p // 2, k, :, wide] for k in places], axis=0)
            both = jnp.dot(jnp.concatenate([high_a, low_a], axis=0), high_b, preferred_element_type=f32)
            term = both[:count] + both[count:] + jnp.dot(high_a, low_b, preferred_element_type=f32)
            if (p, o) in begun:
                acc[p, here, wide] += term
            else:
                begun.add((p, o))
                acc[p, here, wide] = term
        elif kind == "final":
            _, p, o = name
            low, count, lane, lanes = STREAMS[p + 1][o]
            here, wide = pl.ds(low, count), pl.ds(lane, lanes)
            value = masked(acc[p, here, wide], low, lane)
            if p % 2:
                value = 3.0 * gathered(p, low, 0, 0) - 2.0 * value
            if p == 2 * STEPS - 1:
                out[here, wide] = value
            else:
                ref = stream_of(p + 1, o)
                ref[0, 0, 0] = value[:count // 2]
                ref[1, 0, 0] = value[count // 2:]
                if p % 2:
                    cols[p // 2 + 1, r, here, wide] = value
        for where, _, piece in pushes:
            copy_of(piece, where).start()
        if kind == "start":
            for copy in fetch[:-1]:
                copy.wait()

    for name in ORDER:
        run(name)

    def sent(ref, sem):
        pltpu.make_async_copy(ref, ref, sem).wait()

    for p in range(2 * STEPS):
        sent(cols.at[0, pl.ds(0, 15)], row_send.at[p])
    for s in range(STEPS):
        sent(cols.at[s, pl.ds(0, 15)], col_send.at[s])


def local(density, pattern):
    size = density.shape[0]
    tiles = NX * NY
    return pl.pallas_call(
        kernel,
        out_shape=jax.ShapeDtypeStruct(density.shape, f32),
        in_specs=[pl.BlockSpec(memory_space=pltpu.HBM), pl.BlockSpec(memory_space=pltpu.HBM)],
        out_specs=pl.BlockSpec(memory_space=pltpu.VMEM),
        scratch_shapes=[
            pltpu.VMEM((3 * STEPS, 2, NY, NX, size // 4, size), f32),
            pltpu.VMEM((2 * STEPS, 2, NY, NX, size // 4, size // 2), f32),
            pltpu.VMEM((STEPS, tiles, size, size), f32),
            pltpu.VMEM((STEPS, tiles, size, size), bf16),
            pltpu.VMEM((STEPS, tiles, size, size), bf16),
            pltpu.VMEM((2 * STEPS, size, size), f32),
            pltpu.SMEM(pattern.shape, jnp.int32),
            pltpu.SemaphoreType.DMA((2 * STEPS,)),
            pltpu.SemaphoreType.DMA((len(ROW),)),
            pltpu.SemaphoreType.DMA((STEPS,)),
            pltpu.SemaphoreType.DMA((len(COL),)),
            pltpu.SemaphoreType.DMA((6,)),
        ],
        compiler_params=pltpu.CompilerParams(
            collective_id=0, has_side_effects=True, vmem_limit_bytes=53 * 1024 * 1024 + 512 * 1024),
    )(pattern, density)


def solution(mesh):
    placed = P("row", "col")
    return jax.shard_map(local, mesh=mesh, in_specs=(placed, placed), out_specs=placed, check_vma=False)
```
